32 devices in a mesh: dp: 4 (over x, core), fsdp: 8 (over z, y).
Axes of the slice: x: 2, y: 2, z: 4, core: 2. Of those that a mesh axis runs over, the one named last changes fastest.
Arguments:
- hidden_in: bfloat16 [8, 2048, 960], P('dp', 'fsdp'), may hold values from -6 to 6
- segment: int32 [8, 2048], P('dp', 'fsdp'), may hold values from 0 to 8, as said below
- position: int32 [8, 2048], P('dp', 'fsdp'), may hold values from 0 to 1215, as said below
- selected: int32 [8, 2048], P('dp', 'fsdp'), may hold values from 0 to 1, as said below
- gain_attn: bfloat16 [960], replicated, may hold values from 0.5 to 1.5
- gain_ffn: bfloat16 [960], replicated, may hold values from 0.5 to 1.5
- router: bfloat16 [960], replicated, may hold values from -0.1875 to 0.1875
- w_query: bfloat16 [960, 960], P('dp', 'fsdp'), may hold values from -0.1875 to 0.1875
- key_weight: bfloat16 [960, 320], P('dp', 'fsdp'), may hold values from -0.1875 to 0.1875
- value_weight: bfloat16 [960, 320], P('dp', 'fsdp'), may hold values from -0.1875 to 0.1875
- w_output: bfloat16 [960, 960], P('fsdp', 'dp'), may hold values from -1.5 to 1.5
- w_gate: bfloat16 [960, 2560], P('dp', 'fsdp'), may hold values from -0.1875 to 0.1875
- w_up: bfloat16 [960, 2560], P('dp', 'fsdp'), may hold values from -0.1875 to 0.1875
- w_down: bfloat16 [2560, 960], P('fsdp', 'dp'), may hold values from -0.125 to 0.125
- cotangent: bfloat16 [8, 2048, 960], P('dp', 'fsdp'), may hold values from -6 to 6
Outputs:
- hidden_out: bfloat16 [8, 2048, 960], P('dp', 'fsdp')
- grad_in: float32 [8, 2048, 960], P('dp', 'fsdp')
- grad_gain_attn: float32 [960], replicated
- grad_gain_ffn: float32 [960], replicated
- grad_router: float32 [960], replicated
- grad_w_query: float32 [960, 960], P('dp', 'fsdp')
- grad_w_key: float32 [960, 320], P('dp', 'fsdp')
- grad_w_value: float32 [960, 320], P('dp', 'fsdp')
- grad_w_output: float32 [960, 960], P('fsdp', 'dp')
- grad_w_gate: float32 [960, 2560], P('dp', 'fsdp')
- grad_w_up: float32 [960, 2560], P('dp', 'fsdp')
- grad_w_down: float32 [2560, 960], P('fsdp', 'dp')
The draws below stay inside these ranges and needn't reach their ends.
Inputs may be any that keep to these rules, and one draw needn't show every extreme that they name: Every group begins with 1024 tokens of segment 0; continuations 1 to 8 follow in order, each 64 to 192 tokens long; in every group one or more continuations, which ones drawn from the seed, are exactly 192 tokens long. `position`: A prompt token carries its index in the group; a continuation token carries 1024 plus its index in its continuation. `selected`: exactly 1024 tokens of every group are 1.
All inputs are finite; a program needn't handle non-finite values.
Results may differ from the reference program's by a relative error of at most 0.023.
Values may be sent and summed in bfloat16 or wider, within the bound.
No kernel may reach another device: no remote copies, remote signals or barrier semaphores. Data moves between devices by JAX's collectives and lax.ppermute only.
A program may use at most 192 MiB of HBM per device.

```python
import jax
import jax.numpy as jnp
from jax import lax

MODEL_DIM = 960
QUERY_HEAD_COUNT = 15
KEY_VALUE_HEADS = 5
HEAD_DIM = 64
FF = 2560
GT = 2048
PROMPT = 1024
CONT = 8
GROUPS = 8


def layout(key):
    pair_count = CONT // 2
    mean_length = (GT - PROMPT) // CONT
    swing = jax.random.randint(jax.random.fold_in(key, 11), (GROUPS, pair_count), 0, mean_length // 2 + 1)
    swing = jnp.where(jnp.arange(pair_count)[None, :] == 0, mean_length // 2, swing)
    flipped = jax.random.randint(jax.random.fold_in(key, 12), (GROUPS, pair_count), 0, 2)
    first_length = mean_length + swing * (1 - 2 * flipped)
    second_length = 2 * mean_length - first_length
    lengths = jnp.stack([first_length, second_length], axis=2).reshape(GROUPS, CONT)
    ends = jnp.cumsum(lengths, axis=1)
    offset = jnp.arange(GT, dtype=jnp.int32) - PROMPT
    passed = offset[None, :, None] >= ends[:, None, :]
    number = jnp.sum(passed.astype(jnp.int32), axis=2)
    begin = jnp.sum(jnp.where(passed, lengths[:, None, :], 0), axis=2)
    in_prompt = offset[None, :] < 0
    segment = jnp.where(in_prompt, 0, number + 1).astype(jnp.int32)
    position = jnp.where(in_prompt, offset[None, :] + PROMPT, PROMPT + offset[None, :] - begin).astype(jnp.int32)
    return (segment, position)


def draw_segment(key, part):
    return layout(key)[0]


def draw_position(key, part):
    return layout(key)[1]


def draw_selected(key, part):
    lift = jax.random.randint(jax.random.fold_in(key, 21), (GROUPS, 16), 0, 4)
    lift_full = jnp.repeat(lift, GT // 16, axis=1)
    base = jax.random.randint(jax.random.fold_in(key, 22), (GROUPS, GT), 0, 4096)
    distinct = (base + 2048 * lift_full) * GT + jnp.arange(GT, dtype=jnp.int32)[None, :]
    top_values = lax.top_k(distinct, GT // 2)[0]
    threshold = top_values[:, GT // 2 - 1]
    return (distinct >= threshold[:, None]).astype(jnp.int32)


def steps_of(own_key, shape, cuts, low, top_value):
    def one(axis_at, parts):
        heights = jax.random.uniform(jax.random.fold_in(jax.random.fold_in(own_key, 6), axis_at), (parts,), jnp.float32, low / len(cuts), top_value / len(cuts))
        return jnp.repeat(jnp.exp(heights), shape[axis_at] // parts).reshape((-1,) + (1,) * (len(shape) - axis_at - 1))

    loudness = one(*cuts[0])
    for cut in cuts[1:]:
        loudness = loudness * one(*cut)
    return loudness


def normal_values(stream_key, shape, scale, most, cuts=(), kind=jnp.bfloat16):
    array = scale * jax.random.normal(stream_key, shape, jnp.float32)
    if cuts:
        array = array * steps_of(stream_key, shape, cuts, -0.22, 0.18)
    return jnp.clip(array, -most, most).astype(kind)


def setup_inputs(seed: int = 0) -> dict:
    seeds = jax.random.split(jax.random.key(seed), 16)
    return {
        "hidden_in": normal_values(seeds[0], (GROUPS, GT, MODEL_DIM), 1.0, 6.0, ((0, 4), (1, 8))),
        "segment": draw_segment(jax.random.fold_in(seeds[15], 71), 0),
        "position": draw_position(jax.random.fold_in(seeds[15], 71), 0),
        "selected": draw_selected(jax.random.fold_in(seeds[15], 71), 0),
        "gain_attn": jnp.clip(1.0 + 0.1 * jax.random.normal(seeds[4], (MODEL_DIM,), jnp.float32), 0.5, 1.5).astype(jnp.bfloat16),
        "gain_ffn": jnp.clip(1.0 + 0.1 * jax.random.normal(seeds[5], (MODEL_DIM,), jnp.float32), 0.5, 1.5).astype(jnp.bfloat16),
        "router": normal_values(seeds[6], (MODEL_DIM,), MODEL_DIM ** -0.5, 0.1875),
        "w_query": normal_values(seeds[7], (MODEL_DIM, QUERY_HEAD_COUNT * HEAD_DIM), MODEL_DIM ** -0.5, 0.1875, ((0, 4), (1, 8))),
        "key_weight": normal_values(seeds[8], (MODEL_DIM, KEY_VALUE_HEADS * HEAD_DIM), MODEL_DIM ** -0.5, 0.1875, ((0, 4), (1, 8))),
        "value_weight": normal_values(seeds[9], (MODEL_DIM, KEY_VALUE_HEADS * HEAD_DIM), MODEL_DIM ** -0.5, 0.1875, ((0, 4), (1, 8))),
        "w_output": normal_values(seeds[10], (QUERY_HEAD_COUNT * HEAD_DIM, MODEL_DIM), (max(QUERY_HEAD_COUNT * HEAD_DIM // 64, 1)) ** -0.5, 1.5, ((0, 8), (1, 4))),
        "w_gate": normal_values(seeds[11], (MODEL_DIM, FF), MODEL_DIM ** -0.5, 0.1875, ((0, 4), (1, 8))),
        "w_up": normal_values(seeds[12], (MODEL_DIM, FF), MODEL_DIM ** -0.5, 0.1875, ((0, 4), (1, 8))),
        "w_down": normal_values(seeds[13], (FF, MODEL_DIM), FF ** -0.5, 0.125, ((0, 8), (1, 4))),
        "cotangent": normal_values(seeds[14], (GROUPS, GT, MODEL_DIM), 1.0, 6.0, ((0, 4), (1, 8))),
    }


EPSILON = 1e-05
THETA = 10000.0
MINUS_LARGE = -1e+30
TOP_PRECISION = lax.Precision.HIGHEST

@jax.custom_vjp
def lower_cast(v):
    return lax.optimization_barrier(v.astype(jnp.bfloat16)).astype(jnp.float32)

@jax.custom_vjp
def lower_cast_reverse(v):
    return v

def low_keep(v):
    return (lower_cast(v), None)

def low_pass(kept, grad):
    return (grad,)

def back_keep(v):
    return (v, None)

def back_low(kept, grad):
    return (lower_cast(grad),)
lower_cast.defvjp(low_keep, low_pass)
lower_cast_reverse.defvjp(back_keep, back_low)

def inverse_rms(value_matrix):
    return lax.rsqrt(lax.optimization_barrier(jnp.mean(value_matrix * value_matrix, axis=-1, keepdims=True)) + EPSILON)

def apply_rotary(value_matrix, cosine_table, sine_table):
    half_width = value_matrix.shape[-1] // 2
    first_half = value_matrix[..., :half_width]
    second_half = value_matrix[..., half_width:]
    return jnp.concatenate([first_half * cosine_table - second_half * sine_table, second_half * cosine_table + first_half * sine_table], axis=-1)

def group_forward(inputs, segment, position, selected, gain_attn, gain_ffn, router, w_query, key_weight, value_weight, w_output, w_gate, w_up, w_down):
    token_ids = inputs.shape[0]
    first_normed = lower_cast(inputs * inverse_rms(inputs) * gain_attn)
    frequency = THETA ** (-(jnp.arange(HEAD_DIM // 2).astype(jnp.float32) * 2.0) / HEAD_DIM)
    angles = position.astype(jnp.float32)[:, None] * frequency[None, :]
    cosine_table = jnp.cos(angles)[:, None, :]
    sine_table = jnp.sin(angles)[:, None, :]
    query_matrix = lower_cast_reverse(jnp.dot(first_normed, w_query, precision=TOP_PRECISION)).reshape(token_ids, QUERY_HEAD_COUNT, HEAD_DIM)
    key_rotary = lower_cast_reverse(jnp.dot(first_normed, key_weight, precision=TOP_PRECISION)).reshape(token_ids, KEY_VALUE_HEADS, HEAD_DIM)
    value_matrix = lower_cast(lower_cast_reverse(jnp.dot(first_normed, value_weight, precision=TOP_PRECISION))).reshape(token_ids, KEY_VALUE_HEADS, HEAD_DIM)
    query_matrix = lower_cast(apply_rotary(query_matrix, cosine_table, sine_table)).reshape(token_ids, KEY_VALUE_HEADS, QUERY_HEAD_COUNT // KEY_VALUE_HEADS, HEAD_DIM)
    key_rotary = lower_cast(apply_rotary(key_rotary, cosine_table, sine_table))
    scores = lower_cast_reverse(jnp.einsum('qkgd,ckd->kgqc', query_matrix, key_rotary, precision=TOP_PRECISION) * HEAD_DIM ** (-0.5))
    row_index = jnp.arange(token_ids)
    key_tags = jnp.where(selected == 1, segment, -1)
    allowed = (key_tags[None, :] == 0) | (key_tags[None, :] == segment[:, None])
    visible = (row_index[None, :] <= row_index[:, None]) & allowed | (row_index[None, :] == row_index[:, None])
    scores = jnp.where(visible, scores, MINUS_LARGE)
    row_peak = lax.optimization_barrier(jnp.max(scores, axis=-1, keepdims=True))
    weights = jnp.exp(scores - row_peak)
    probability = lower_cast(weights / lax.optimization_barrier(jnp.sum(weights, axis=-1, keepdims=True)))
    mixed_heads = jnp.einsum('kgqc,ckd->qkgd', probability, value_matrix, precision=TOP_PRECISION).reshape(token_ids, QUERY_HEAD_COUNT * HEAD_DIM)
    mixed_heads = lower_cast(lower_cast_reverse(mixed_heads))
    attn_out = lower_cast_reverse(jnp.dot(mixed_heads, w_output, precision=TOP_PRECISION))
    middle = inputs + attn_out
    normed_two = lower_cast(middle * inverse_rms(middle) * gain_ffn)
    gate_proj = lower_cast_reverse(jnp.dot(normed_two, w_gate, precision=TOP_PRECISION))
    up_proj = lower_cast_reverse(jnp.dot(normed_two, w_up, precision=TOP_PRECISION))
    hidden = lower_cast(jax.nn.silu(gate_proj) * up_proj)
    ffn_out = lower_cast_reverse(jnp.dot(hidden, w_down, precision=TOP_PRECISION))
    mix_weight = selected.astype(jnp.float32) * jax.nn.sigmoid(jnp.dot(inputs, router, precision=TOP_PRECISION))
    return inputs + mix_weight[:, None] * (attn_out + ffn_out)

def reference(hidden_in, segment, position, selected, gain_attn, gain_ffn, router, w_query, key_weight, value_weight, w_output, w_gate, w_up, w_down, cotangent):
    floats = tuple((member.astype(jnp.float32) for member in (hidden_in, gain_attn, gain_ffn, router, w_query, key_weight, value_weight, w_output, w_gate, w_up, w_down)))

    def forward(inputs, gain_one, gain_two, router_vec, query_w, key_w, value_w, output_w, gate_w, up_w, down_w):

        def one_group(pieces):
            return group_forward(pieces[0], pieces[1], pieces[2], pieces[3], gain_one, gain_two, router_vec, query_w, key_w, value_w, output_w, gate_w, up_w, down_w)
        return lax.map(jax.checkpoint(one_group), (inputs, segment, position, selected))
    output, pullback = jax.vjp(forward, *floats)
    gradients = pullback(cotangent.astype(jnp.float32))
    return (output.astype(jnp.bfloat16), gradients[0], gradients[1], gradients[2], gradients[3], gradients[4], gradients[5], gradients[6], gradients[7], gradients[8], gradients[9], gradients[10])
```

```python
import functools
import math

import jax
import jax.numpy as jnp
import numpy as np
from jax import lax
from jax.experimental import pallas as pl
from jax.experimental.pallas import tpu as pltpu
from jax.sharding import PartitionSpec as P

QUERY_HEADS = 15
KV_HEADS = 5
SHARE = QUERY_HEADS // KV_HEADS
HEAD_DIM = 64
TILE = 128
PROMPT = 1024
LONGEST = 192
EPSILON = 1e-05
THETA = 10000.0
MINUS_LARGE = -1e30
AXES = ("dp", "fsdp")
F32 = jnp.float32
BF16 = jnp.bfloat16
VMEM_BYTES = 60 * 1024 * 1024

NT = (((1,), (1,)), ((), ()))
NN = (((1,), (0,)), ((), ()))
TN = (((0,), (0,)), ((), ()))


def dot(a, b, dims=NN):
    return lax.dot_general(a, b, dims, preferred_element_type=F32)


def params(steps=0):
    return pltpu.CompilerParams(
        vmem_limit_bytes=VMEM_BYTES,
        dimension_semantics=("arbitrary",) * steps if steps else None,
    )


def cost(flops, moved, exps=0):
    return pl.CostEstimate(flops=int(flops), bytes_accessed=int(moved), transcendentals=int(exps))


def whole(shape):
    zeros = (0,) * len(shape)
    return pl.BlockSpec(shape, lambda *_: zeros)


def norm_kernel(hid_ref, cot_ref, gain_ref, router_ref, sel_ref, xn_ref, s1_ref, fg_ref, mix_ref, slope_ref):
    parts, _, width = hid_ref.shape
    square = 0.0
    logit = 0.0
    for d in range(parts):
        x = hid_ref[d].astype(F32)
        square = square + jnp.sum(x * x, axis=-1, keepdims=True)
        logit = logit + jnp.sum(x * router_ref[d], axis=-1, keepdims=True)
    scale = lax.rsqrt(square / (parts * width) + EPSILON)
    chance = 1.0 / (1.0 + jnp.exp(-logit))
    mix = sel_ref[...] * chance
    s1_ref[...] = scale
    mix_ref[...] = mix
    slope_ref[...] = mix * (1.0 - chance)
    for d in range(parts):
        x = hid_ref[d].astype(F32)
        xn_ref[d] = (x * scale * gain_ref[d]).astype(BF16)
        fg_ref[d] = (cot_ref[d].astype(F32) * mix).astype(BF16)


def first_norm(hid4, cot4, gain, router, chosen):
    parts, tokens, width = hid4.shape
    rows = 128
    block = pl.BlockSpec((parts, rows, width), lambda i: (0, i, 0))
    column = pl.BlockSpec((rows, 1), lambda i: (i, 0))
    vector = whole((parts, 1, width))
    return pl.pallas_call(
        norm_kernel,
        grid=(tokens // rows,),
        in_specs=[block, block, vector, vector, column],
        out_specs=[block, column, block, column, column],
        out_shape=[
            jax.ShapeDtypeStruct(hid4.shape, BF16),
            jax.ShapeDtypeStruct((tokens, 1), F32),
            jax.ShapeDtypeStruct(hid4.shape, BF16),
            jax.ShapeDtypeStruct((tokens, 1), F32),
            jax.ShapeDtypeStruct((tokens, 1), F32),
        ],
        compiler_params=params(1),
        cost_estimate=cost(tokens * 960 * 10, tokens * 960 * 8),
        name="first_norm",
    )(hid4, cot4, gain, router, chosen)


def kv_kernel(xn_ref, w_ref, cos_ref, sin1_ref, sin2_ref, tag_ref, out_ref):
    rows = xn_ref.shape[1]
    total = 0.0
    for d in range(xn_ref.shape[0]):
        total = total + dot(xn_ref[d], w_ref[d], NT)
    for h in range(KV_HEADS):
        u = total[:, h * TILE : (h + 1) * TILE]
        turned = (
            u * cos_ref[...]
            + pltpu.roll(u, TILE - HEAD_DIM // 2, 1) * sin1_ref[...]
            + pltpu.roll(u, HEAD_DIM // 2, 1) * sin2_ref[...]
        )
        out_ref[0, :rows, h * TILE : (h + 1) * TILE] = turned.astype(BF16)
        out_ref[0, rows:, h * TILE : (h + 1) * TILE] = tag_ref[0]


def kv_project(xn4, wkv, tables, tags, groups):
    parts, tokens, width = xn4.shape
    rows = tokens // groups
    table = pl.BlockSpec((rows, TILE), lambda g: (g, 0))
    return pl.pallas_call(
        kv_kernel,
        grid=(groups,),
        in_specs=[
            pl.BlockSpec((parts, rows, width), lambda g: (0, g, 0)),
            whole(wkv.shape),
            table,
            table,
            table,
            pl.BlockSpec((1, 16, TILE), lambda g: (g, 0, 0)),
        ],
        out_specs=pl.BlockSpec((1, rows + 16, KV_HEADS * TILE), lambda g: (g, 0, 0)),
        out_shape=jax.ShapeDtypeStruct((groups, rows + 16, KV_HEADS * TILE), BF16),
        compiler_params=params(1),
        cost_estimate=cost(2 * tokens * 960 * 640, 3 * tokens * 960 * 2),
        name="kv_project",
    )(xn4, wkv, *tables, tags)


def q_kernel(xn_ref, w_ref, cos_ref, sin_ref, out_ref):
    for h in range(QUERY_HEADS):
        u = 0.0
        for d in range(xn_ref.shape[0]):
            u = u + dot(xn_ref[d], w_ref[d, h * TILE : (h + 1) * TILE], NT)
        turned = u * cos_ref[...] + pltpu.roll(u, HEAD_DIM, 1) * sin_ref[...]
        out_ref[:, h * TILE : (h + 1) * TILE] = turned.astype(BF16)


def q_project(xn4, wq_pad, cos_q, sin_q, groups):
    parts, tokens, width = xn4.shape
    rows = tokens // groups
    table = pl.BlockSpec((rows, TILE), lambda g: (g, 0))
    return pl.pallas_call(
        q_kernel,
        grid=(groups,),
        in_specs=[
            pl.BlockSpec((parts, rows, width), lambda g: (0, g, 0)),
            whole(wq_pad.shape),
            table,
            table,
        ],
        out_specs=pl.BlockSpec((rows, QUERY_HEADS * TILE), lambda g: (g, 0)),
        out_shape=jax.ShapeDtypeStruct((tokens, QUERY_HEADS * TILE), BF16),
        compiler_params=params(1),
        cost_estimate=cost(2 * tokens * 960 * 1920, 6 * tokens * 960 * 2),
        name="q_project",
    )(xn4, wq_pad, cos_q, sin_q)


def slot_needed(slot_ref, s, rows):
    own = slot_ref[0]
    block = slot_ref[s]
    prompt_blocks = PROMPT // rows
    reach = -(-(LONGEST - 1) // rows)
    near = (block < prompt_blocks) | (block >= own - reach)
    return (block >= 0) & (block <= own) & near


def fill_bias(slot_ref, seg_ref, kv_refs, bias_ref):
    rows = bias_ref.shape[1]
    for s, kv_ref in enumerate(kv_refs):

        @pl.when(slot_needed(slot_ref, s, rows))
        def _(s=s, kv_ref=kv_ref):
            for i in range(rows // TILE):
                tag_row = kv_ref[0, rows : rows + 16, 0:TILE].astype(F32)[i : i + 1]
                tag = jnp.broadcast_to(tag_row, (TILE, TILE)).T
                for j in range(rows // TILE):
                    seg = seg_ref[0, :, j * TILE : (j + 1) * TILE]
                    allowed = (tag == 0.0) | (tag == seg)
                    if s == 0:
                        key_row = i * TILE + lax.broadcasted_iota(jnp.int32, (TILE, TILE), 0)
                        query_row = j * TILE + lax.broadcasted_iota(jnp.int32, (TILE, TILE), 1)
                        allowed = (allowed & (key_row <= query_row)) | (key_row == query_row)
                    bias_ref[s, i * TILE : (i + 1) * TILE, j * TILE : (j + 1) * TILE] = jnp.where(
                        allowed, 0.0, MINUS_LARGE
                    )


def stack_heads(ref):
    return jnp.concatenate([ref[:, j * TILE : (j + 1) * TILE] for j in range(SHARE)], axis=0)


def forward_kernel(slot_ref, q_ref, seg_ref, *refs):
    slots = len(refs) - 6
    kv_refs = refs[:slots]
    o_ref, lse_ref, bias_ref, peak_ref, total_ref, acc_ref = refs[slots:]
    rows = q_ref.shape[0]

    @pl.when(pl.program_id(1) == 0)
    def _():
        fill_bias(slot_ref, seg_ref, kv_refs, bias_ref)

    q = stack_heads(q_ref)

    def scores(s):
        kv = kv_refs[s][0, :rows, :]
        bias = bias_ref[s]
        return kv, dot(kv, q, NT) + jnp.concatenate([bias] * SHARE, axis=1)

    kv, score = scores(0)
    peak = jnp.max(score, axis=0, keepdims=True)
    weights = jnp.exp(score - peak)
    peak_ref[...] = peak
    total_ref[...] = jnp.sum(weights, axis=0, keepdims=True)
    acc_ref[...] = dot(kv, weights.astype(BF16), TN)

    for s in range(1, slots):

        @pl.when(slot_needed(slot_ref, s, rows))
        def _(s=s):
            kv, score = scores(s)
            old = peak_ref[...]
            peak = jnp.maximum(old, jnp.max(score, axis=0, keepdims=True))
            fade = jnp.exp(old - peak)
            weights = jnp.exp(score - peak)
            peak_ref[...] = peak
            total_ref[...] = total_ref[...] * fade + jnp.sum(weights, axis=0, keepdims=True)
            acc_ref[...] = acc_ref[...] * fade + dot(kv, weights.astype(BF16), TN)

    total = total_ref[...]
    lse_ref[0, 0] = peak_ref[...] + jnp.log(total)
    mixed = (acc_ref[...] / total).T
    lane = lax.broadcasted_iota(jnp.int32, mixed.shape, 1)
    mixed = jnp.where(lane >= HEAD_DIM, mixed, 0.0).astype(BF16)
    for j in range(SHARE):
        o_ref[:, j * TILE : (j + 1) * TILE] = mixed[j * rows : (j + 1) * rows]


def attention_specs(groups, rows, slots):
    heads = pl.BlockSpec((rows, SHARE * TILE), lambda g, h, _: (g, h))
    seg = pl.BlockSpec((1, 1, rows), lambda g, h, _: (g, 0, 0))
    kv = pl.BlockSpec((1, rows + 16, TILE), lambda g, h, _: (g, 0, h))
    lse = pl.BlockSpec((1, 1, 1, SHARE * rows), lambda g, h, _: (g, h, 0, 0))
    return heads, seg, kv, lse


def attention_forward(slot_ids, q, seg, kvs):
    groups = kvs[0].shape[0]
    tokens = q.shape[0]
    rows = tokens // groups
    slots = len(kvs)
    heads, seg_spec, kv_spec, lse_spec = attention_specs(groups, rows, slots)
    wide = SHARE * rows
    return pl.pallas_call(
        forward_kernel,
        grid_spec=pltpu.PrefetchScalarGridSpec(
            num_scalar_prefetch=1,
            grid=(groups, KV_HEADS),
            in_specs=[heads, seg_spec] + [kv_spec] * slots,
            out_specs=[heads, lse_spec],
            scratch_shapes=[
                pltpu.VMEM((slots, rows, rows), F32),
                pltpu.VMEM((1, wide), F32),
                pltpu.VMEM((1, wide), F32),
                pltpu.VMEM((TILE, wide), F32),
            ],
        ),
        out_shape=[
            jax.ShapeDtypeStruct(q.shape, BF16),
            jax.ShapeDtypeStruct((groups, KV_HEADS, 1, wide), F32),
        ],
        compiler_params=params(2),
        cost_estimate=cost(2 * 15 * tokens * 1536 * 256, 8 * tokens * 960 * 2, 15 * tokens * 1536),
        name="attention_forward",
    )(slot_ids, q, seg, *kvs)


def backward_kernel(slot_ref, q_ref, do_ref, o_ref, lse_ref, seg_ref, cos_ref, sin1_ref, sin2_ref, *refs):
    slots = (len(refs) - 3) // 2
    kv_refs = refs[:slots]
    dq_ref = refs[slots]
    dkv_refs = refs[slots + 1 : 2 * slots + 1]
    bias_ref, acc_ref = refs[2 * slots + 1 :]
    rows = q_ref.shape[0]

    @pl.when(pl.program_id(1) == 0)
    def _():
        fill_bias(slot_ref, seg_ref, kv_refs, bias_ref)

    q = stack_heads(q_ref)
    do = stack_heads(do_ref)
    o = stack_heads(o_ref)
    delta = jnp.sum((do.astype(F32) * o.astype(F32)).T, axis=0, keepdims=True)
    lse = lse_ref[0, 0]

    for s in range(slots):

        def work(s=s):
            kv = kv_refs[s][0, :rows, :]
            bias = bias_ref[s]
            score = dot(kv, q, NT) + jnp.concatenate([bias] * SHARE, axis=1)
            prob = jnp.exp(score - lse)
            slope = (prob * (dot(kv, do, NT) - delta)).astype(BF16)
            dkv_refs[s][0] = (dot(slope, q) + dot(prob.astype(BF16), do)).astype(BF16)
            return dot(kv, slope, TN)

        if s == 0:
            acc_ref[...] = work()
        else:
            needed = slot_needed(slot_ref, s, rows)

            @pl.when(needed)
            def _(s=s, work=work):
                acc_ref[...] += work()

            @pl.when(jnp.logical_not(needed))
            def _(s=s):
                dkv_refs[s][0] = jnp.zeros((rows, TILE), BF16)

    u = acc_ref[...].T
    for j in range(SHARE):
        part = u[j * rows : (j + 1) * rows]
        back = (
            part * cos_ref[...]
            - pltpu.roll(part, TILE - HEAD_DIM // 2, 1) * sin1_ref[...]
            - pltpu.roll(part, HEAD_DIM // 2, 1) * sin2_ref[...]
        )
        dq_ref[:, j * TILE : (j + 1) * TILE] = back.astype(BF16)


def attention_backward(slot_ids, q, do, o, lse, seg, tables, kvs):
    groups = kvs[0].shape[0]
    tokens = q.shape[0]
    rows = tokens // groups
    slots = len(kvs)
    heads, seg_spec, kv_spec, lse_spec = attention_specs(groups, rows, slots)
    table = pl.BlockSpec((rows, TILE), lambda g, h, _: (g, 0))
    grad = pl.BlockSpec((1, rows, TILE), lambda g, h, _: (g, 0, h))
    wide = SHARE * rows
    out = pl.pallas_call(
        backward_kernel,
        grid_spec=pltpu.PrefetchScalarGridSpec(
            num_scalar_prefetch=1,
            grid=(groups, KV_HEADS),
            in_specs=[heads, heads, heads, lse_spec, seg_spec, table, table, table] + [kv_spec] * slots,
            out_specs=[heads] + [grad] * slots,
            scratch_shapes=[
                pltpu.VMEM((slots, rows, rows), F32),
                pltpu.VMEM((TILE, wide), F32),
            ],
        ),
        out_shape=[jax.ShapeDtypeStruct(q.shape, BF16)]
        + [jax.ShapeDtypeStruct((groups, rows, KV_HEADS * TILE), BF16)] * slots,
        compiler_params=params(2),
        cost_estimate=cost(5 * 15 * tokens * 1536 * 256, 16 * tokens * 960 * 2, 15 * tokens * 1536),
        name="attention_backward",
    )(slot_ids, q, do, o, lse, seg, *tables, *kvs)
    return out[0], out[1:]


def out_kernel(o_ref, w_ref, hid_ref, gain_ref, mid_ref, x2_ref, s2_ref):
    parts, _, width = hid_ref.shape
    o = o_ref[...]
    square = 0.0
    for d in range(parts):
        middle = hid_ref[d].astype(F32) + dot(o, w_ref[d])
        mid_ref[d] = middle
        square = square + jnp.sum(middle * middle, axis=-1, keepdims=True)
    scale = lax.rsqrt(square / (parts * width) + EPSILON)
    s2_ref[...] = scale
    for d in range(parts):
        x2_ref[d] = (mid_ref[d] * scale * gain_ref[d]).astype(BF16)


def out_project(o, wo_pad, hid4, gain):
    parts, tokens, width = hid4.shape
    rows = 128
    block = pl.BlockSpec((parts, rows, width), lambda i: (0, i, 0))
    column = pl.BlockSpec((rows, 1), lambda i: (i, 0))
    return pl.pallas_call(
        out_kernel,
        grid=(tokens // rows,),
        in_specs=[
            pl.BlockSpec((rows, o.shape[1]), lambda i: (i, 0)),
            whole(wo_pad.shape),
            block,
            whole((parts, 1, width)),
        ],
        out_specs=[block, block, column],
        out_shape=[
            jax.ShapeDtypeStruct(hid4.shape, F32),
            jax.ShapeDtypeStruct(hid4.shape, BF16),
            jax.ShapeDtypeStruct((tokens, 1), F32),
        ],
        compiler_params=params(1),
        cost_estimate=cost(2 * tokens * 960 * 1920, 8 * tokens * 960 * 2),
        name="out_project",
    )(o, wo_pad, hid4, gain)


def ffn_kernel(meta_ref, x_ref, fg_ref, w_ref, out_ref, xg_ref, keep_ref, send_ref):
    parts = x_ref.shape[0]
    rows = w_ref.shape[2] // 3
    my_part = meta_ref[0]
    odd = meta_ref[1]

    def weight(d, which):
        pair = [w_ref[d, pl.ds(odd ^ i, 1), which * rows : (which + 1) * rows, :] for i in range(2)]
        return jnp.concatenate([p.reshape(rows, p.shape[-1]) for p in pair], axis=0)

    gate = 0.0
    up = 0.0
    hidden_grad = 0.0
    for d in range(parts):
        gate = gate + dot(x_ref[d], weight(d, 0), NT)
        up = up + dot(x_ref[d], weight(d, 1), NT)
        hidden_grad = hidden_grad + dot(fg_ref[d], weight(d, 2), NT)
    chance = 1.0 / (1.0 + jnp.exp(-gate))
    silu = gate * chance
    hidden = (silu * up).astype(BF16)
    up_grad = (hidden_grad * silu).astype(BF16)
    gate_grad = (hidden_grad * up * chance * (1.0 + gate * (1.0 - chance))).astype(BF16)

    first = pl.program_id(0) == 0
    for d in range(parts):
        out = dot(hidden, weight(d, 2))
        back = dot(gate_grad, weight(d, 0)) + dot(up_grad, weight(d, 1))

        @pl.when(first)
        def _(d=d, out=out, back=back):
            out_ref[d] = out
            xg_ref[d] = back

        @pl.when(jnp.logical_not(first))
        def _(d=d, out=out, back=back):
            out_ref[d] += out
            xg_ref[d] += back

    turned = (gate_grad.T, up_grad.T, hidden.T)
    for e in range(parts):
        place = pl.ds(my_part ^ e, 1)
        x = x_ref[place].reshape(x_ref.shape[1:])
        fg = fg_ref[place].reshape(x_ref.shape[1:])
        target = send_ref if e % 2 else keep_ref
        for which in range(3):
            grad = dot(turned[which], fg if which == 2 else x).astype(BF16)
            for i in range(2):
                target[e // 2, i, which * rows : (which + 1) * rows, :] = grad[i * rows : (i + 1) * rows]


def ffn(my_part, my_shard, half, x4, fg4, weights):
    parts, tokens, width = x4.shape
    shards, rows3 = weights.shape[1:3]
    steps = shards // 4
    pair = (my_shard ^ (half * (shards // 2))) // 2
    meta = jnp.stack([my_part, my_shard % 2, pair]).astype(jnp.int32)
    grads = pl.BlockSpec((parts // 2, 2, rows3, width), lambda j, m: (0, j, 0, 0))
    inputs = 2 * tokens * 960 * 2
    return pl.pallas_call(
        ffn_kernel,
        grid_spec=pltpu.PrefetchScalarGridSpec(
            num_scalar_prefetch=1,
            grid=(steps,),
            in_specs=[
                whole(x4.shape),
                whole(x4.shape),
                pl.BlockSpec((parts, 2, rows3, width), lambda j, m: (0, m[2] ^ j, 0, 0)),
            ],
            out_specs=[whole(x4.shape), whole(x4.shape), grads, grads],
        ),
        out_shape=[
            jax.ShapeDtypeStruct(x4.shape, F32),
            jax.ShapeDtypeStruct(x4.shape, F32),
            jax.ShapeDtypeStruct((parts // 2, shards // 2, rows3, width), BF16),
            jax.ShapeDtypeStruct((parts // 2, shards // 2, rows3, width), BF16),
        ],
        compiler_params=params(1),
        cost_estimate=cost(6 * tokens * 960 * rows3 * shards // 2, inputs * 4 + 4 * 960 * rows3 * shards // 2),
        name="ffn",
    )(meta, x4, fg4, weights)


def middle_kernel(
    mid_ref, hid_ref, cot_ref, out_a_ref, out_b_ref, xg_a_ref, xg_b_ref, mix_ref, slope_ref, s2_ref, gain_ref, router_ref,
    hidden_ref, part_ref, ag_ref, router_grad_ref, gain_grad_ref,
):
    parts, rows, width = mid_ref.shape
    mix = mix_ref[...]
    scale = s2_ref[...]
    inner = 0.0
    mean = 0.0
    for d in range(parts):
        middle = mid_ref[d]
        inputs = hid_ref[d].astype(F32)
        branch = (middle - inputs) + (out_a_ref[d] + out_b_ref[d])
        upstream = cot_ref[d].astype(F32)
        inner = inner + jnp.sum(upstream * branch, axis=-1, keepdims=True)
        hidden_ref[d] = (inputs + mix * branch).astype(BF16)
        mean = mean + jnp.sum((xg_a_ref[d] + xg_b_ref[d]) * gain_ref[d] * middle, axis=-1, keepdims=True)
    logit_grad = slope_ref[...] * inner
    mean = mean / (parts * width) * (scale * scale * scale)
    first = pl.program_id(0) == 0
    for d in range(parts):
        middle = mid_ref[d]
        inputs = hid_ref[d].astype(F32)
        upstream = cot_ref[d].astype(F32)
        grad = xg_a_ref[d] + xg_b_ref[d]
        middle_grad = scale * (grad * gain_ref[d]) - middle * mean
        ag_ref[d] = (upstream * mix + middle_grad).astype(BF16)
        part_ref[d] = upstream + logit_grad * router_ref[d] + middle_grad
        router_grad = jnp.sum(logit_grad * inputs, axis=0, keepdims=True)
        gain_grad = jnp.sum(grad * middle * scale, axis=0, keepdims=True)

        @pl.when(first)
        def _(d=d, router_grad=router_grad, gain_grad=gain_grad):
            router_grad_ref[d] = router_grad
            gain_grad_ref[d] = gain_grad

        @pl.when(jnp.logical_not(first))
        def _(d=d, router_grad=router_grad, gain_grad=gain_grad):
            router_grad_ref[d] += router_grad
            gain_grad_ref[d] += gain_grad


def middle_step(mid4, hid4, cot4, outs, grads, mix, slope, s2, gain, router):
    parts, tokens, width = mid4.shape
    rows = 128
    block = pl.BlockSpec((parts, rows, width), lambda i: (0, i, 0))
    column = pl.BlockSpec((rows, 1), lambda i: (i, 0))
    vector = whole((parts, 1, width))
    return pl.pallas_call(
        middle_kernel,
        grid=(tokens // rows,),
        in_specs=[block] * 7 + [column] * 3 + [vector] * 2,
        out_specs=[block, block, block, vector, vector],
        out_shape=[
            jax.ShapeDtypeStruct(mid4.shape, BF16),
            jax.ShapeDtypeStruct(mid4.shape, F32),
            jax.ShapeDtypeStruct(mid4.shape, BF16),
            jax.ShapeDtypeStruct((parts, 1, width), F32),
            jax.ShapeDtypeStruct((parts, 1, width), F32),
        ],
        compiler_params=params(1),
        cost_estimate=cost(tokens * 960 * 30, tokens * 960 * 36),
        name="middle_step",
    )(mid4, hid4, cot4, *outs, *grads, mix, slope, s2, gain, router)


def compact(tile_major, upper):
    count = tile_major.shape[0] // TILE
    start = HEAD_DIM if upper else 0
    return jnp.concatenate(
        [tile_major[h * TILE + start : h * TILE + start + HEAD_DIM] for h in range(count)], axis=0
    )


def out_back_kernel(meta_ref, ag_ref, w_ref, o_ref, do_ref, keep_ref, send_ref):
    parts = ag_ref.shape[0]
    for h in range(QUERY_HEADS):
        total = 0.0
        for d in range(parts):
            total = total + dot(ag_ref[d], w_ref[d, h * TILE : (h + 1) * TILE], NT)
        do_ref[:, h * TILE : (h + 1) * TILE] = total.astype(BF16)
    mixed = compact(o_ref[...].T, True)
    for e in range(parts):
        ag = ag_ref[pl.ds(meta_ref[0] ^ e, 1)].reshape(ag_ref.shape[1:])
        target = send_ref if e % 2 else keep_ref
        target[e // 2] = dot(mixed, ag).astype(BF16)


def out_back(my_part, ag4, wo_pad, o):
    parts, tokens, width = ag4.shape
    grad = jax.ShapeDtypeStruct((parts // 2, QUERY_HEADS * HEAD_DIM, width), BF16)
    return pl.pallas_call(
        out_back_kernel,
        grid_spec=pltpu.PrefetchScalarGridSpec(
            num_scalar_prefetch=1,
            grid=(1,),
            in_specs=[whole(ag4.shape), whole(wo_pad.shape), whole(o.shape)],
            out_specs=[whole(o.shape), whole(grad.shape), whole(grad.shape)],
        ),
        out_shape=[jax.ShapeDtypeStruct(o.shape, BF16), grad, grad],
        compiler_params=params(1),
        cost_estimate=cost(2 * tokens * 960 * 2880, 12 * tokens * 960 * 2),
        name="out_back",
    )(my_part.reshape(1), ag4, wo_pad, o)


def q_back_kernel(meta_ref, dq_ref, xn_ref, keep_ref, send_ref):
    turned = compact(dq_ref[...].T, False)
    for e in range(xn_ref.shape[0]):
        x = xn_ref[pl.ds(meta_ref[0] ^ e, 1)].reshape(xn_ref.shape[1:])
        target = send_ref if e % 2 else keep_ref
        target[e // 2] = dot(turned, x).astype(BF16)


def q_back(my_part, dq, xn4):
    parts, tokens, width = xn4.shape
    grad = jax.ShapeDtypeStruct((parts // 2, QUERY_HEADS * HEAD_DIM, width), BF16)
    return pl.pallas_call(
        q_back_kernel,
        grid_spec=pltpu.PrefetchScalarGridSpec(
            num_scalar_prefetch=1,
            grid=(1,),
            in_specs=[whole(dq.shape), whole(xn4.shape)],
            out_specs=[whole(grad.shape), whole(grad.shape)],
        ),
        out_shape=[grad, grad],
        compiler_params=params(1),
        cost_estimate=cost(2 * tokens * 960 * 960, 6 * tokens * 960 * 2),
        name="q_back",
    )(my_part.reshape(1), dq, xn4)


def kv_back_kernel(meta_ref, dkv_ref, cos_ref, sin1_ref, sin2_ref, xn_ref, back_ref, keep_ref, send_ref):
    for h in range(KV_HEADS):
        u = dkv_ref[:, h * TILE : (h + 1) * TILE].astype(F32)
        back = (
            u * cos_ref[...]
            - pltpu.roll(u, TILE - HEAD_DIM // 2, 1) * sin1_ref[...]
            - pltpu.roll(u, HEAD_DIM // 2, 1) * sin2_ref[...]
        )
        back_ref[:, h * TILE : (h + 1) * TILE] = back.astype(BF16)
    turned = back_ref[...].T
    for e in range(xn_ref.shape[0]):
        x = xn_ref[pl.ds(meta_ref[0] ^ e, 1)].reshape(xn_ref.shape[1:])
        target = send_ref if e % 2 else keep_ref
        target[e // 2] = dot(turned, x).astype(BF16)


def kv_back(my_part, dkv, tables, xn4):
    parts, tokens, width = xn4.shape
    grad = jax.ShapeDtypeStruct((parts // 2, KV_HEADS * TILE, width), BF16)
    table = whole((tokens, TILE))
    return pl.pallas_call(
        kv_back_kernel,
        grid_spec=pltpu.PrefetchScalarGridSpec(
            num_scalar_prefetch=1,
            grid=(1,),
            in_specs=[whole(dkv.shape), table, table, table, whole(xn4.shape)],
            out_specs=[whole((tokens, KV_HEADS * TILE)), whole(grad.shape), whole(grad.shape)],
        ),
        out_shape=[jax.ShapeDtypeStruct((tokens, KV_HEADS * TILE), BF16), grad, grad],
        compiler_params=params(1),
        cost_estimate=cost(2 * tokens * 960 * 640, 6 * tokens * 960 * 2),
        name="kv_back",
    )(my_part.reshape(1), dkv, *tables, xn4)


def final_kernel(dq_ref, kvb_ref, wq_ref, wkv_ref, hid_ref, part_ref, s1_ref, gain_ref, out_ref, gain_grad_ref):
    parts, rows, width = hid_ref.shape
    scale = s1_ref[...]
    dq = dq_ref[...]
    kvb = kvb_ref[...]
    mean = 0.0
    first = pl.program_id(0) == 0
    for d in range(parts):
        grad = dot(dq, wq_ref[d]) + dot(kvb, wkv_ref[d])
        inputs = hid_ref[d].astype(F32)
        gain_grad = jnp.sum(grad * inputs * scale, axis=0, keepdims=True)
        scaled = grad * gain_ref[d]
        out_ref[d] = scaled
        mean = mean + jnp.sum(scaled * inputs, axis=-1, keepdims=True)

        @pl.when(first)
        def _(d=d, gain_grad=gain_grad):
            gain_grad_ref[d] = gain_grad

        @pl.when(jnp.logical_not(first))
        def _(d=d, gain_grad=gain_grad):
            gain_grad_ref[d] += gain_grad

    mean = mean / (parts * width) * (scale * scale * scale)
    for d in range(parts):
        out_ref[d] = part_ref[d] + scale * out_ref[d] - hid_ref[d].astype(F32) * mean


def final_step(dq, kvb, wq_pad, wkv, hid4, part4, s1, gain):
    parts, tokens, width = hid4.shape
    rows = 128
    block = pl.BlockSpec((parts, rows, width), lambda i: (0, i, 0))
    column = pl.BlockSpec((rows, 1), lambda i: (i, 0))
    vector = whole((parts, 1, width))
    return pl.pallas_call(
        final_kernel,
        grid=(tokens // rows,),
        in_specs=[
            pl.BlockSpec((rows, dq.shape[1]), lambda i: (i, 0)),
            pl.BlockSpec((rows, kvb.shape[1]), lambda i: (i, 0)),
            whole(wq_pad.shape),
            whole(wkv.shape),
            block,
            block,
            column,
            vector,
        ],
        out_specs=[block, vector],
        out_shape=[
            jax.ShapeDtypeStruct(hid4.shape, F32),
            jax.ShapeDtypeStruct((parts, 1, width), F32),
        ],
        compiler_params=params(1),
        cost_estimate=cost(2 * tokens * 960 * 2560, 10 * tokens * 960 * 2),
        name="final_step",
    )(dq, kvb, wq_pad, wkv, hid4, part4, s1, gain)


class Net:
    def __init__(self, parts, shards):
        self.parts, self.shards = parts, shards
        self.size = parts * shards
        self.index = lax.axis_index("dp") * shards + lax.axis_index("fsdp")
        self.shard_bits = shards.bit_length() - 1
        self.part_bits = parts.bit_length() - 1

    def swap(self, array, bit):
        flip = 1 << bit
        return lax.ppermute(array, AXES, [(i, i ^ flip) for i in range(self.size)])

    def on(self, bit):
        return (self.index >> bit) & 1 == 1

    def gather(self, array):
        order = list(range(self.shard_bits - 1, -1, -1))
        order += list(range(self.size.bit_length() - 2, self.shard_bits - 1, -1))
        for bit in order:
            other = self.swap(array, bit)
            here = self.on(bit)
            array = jnp.stack([jnp.where(here, other, array), jnp.where(here, array, other)])
        bits = len(order)
        place = {bit: bits - 1 - i for i, bit in enumerate(order)}
        high_first = [place[bit] for bit in range(bits - 1, -1, -1)]
        array = jnp.transpose(array, high_first + list(range(bits, array.ndim)))
        return array.reshape((self.parts, self.shards) + array.shape[bits:])

    def add(self, mine, other, dtype=BF16):
        return (mine.astype(F32) + other.astype(F32)).astype(dtype)

    def scatter_parts(self, keep, send):
        other = self.swap(send, self.shard_bits)
        for bit in range(self.size.bit_length() - 2, self.shard_bits, -1):
            half = keep.shape[0] // 2
            send = self.add(keep[half:], other[half:])
            keep = self.add(keep[:half], other[:half])
            other = self.swap(send, bit)
        return keep[0], other[0]

    def scatter_bit(self, keep, other, bit, axis, relative):
        if relative:
            away, near = 1, 0
            pick = lambda a, i: lax.index_in_dim(a, i, axis, keepdims=False)
        else:
            near = (self.index >> bit) & 1
            away = 1 - near
            pick = lambda a, i: lax.dynamic_index_in_dim(a, i, axis, keepdims=False)
        send = self.add(pick(keep, away), pick(other, away))
        return self.add(pick(keep, near), pick(other, near)), self.swap(send, bit)

    def scatter_shards(self, keep, other, relative, bits):
        shape = keep.shape[1:]
        keep = keep.reshape((2,) * bits + shape)
        other = other.reshape((2,) * bits + shape)
        for bit in range(bits):
            keep, other = self.scatter_bit(keep, other, bit, bits - 1 - bit, relative)
        return keep, other

    def scatter(self, keep, send, rows):
        keep, other = self.scatter_parts(keep, send)
        shape = (self.shards, rows) + keep.shape[1:]
        keep, other = self.scatter_shards(keep.reshape(shape), other.reshape(shape), False, self.shard_bits)
        return self.add(keep, other, F32)

    def scatter_halves(self, keep_half, send_half):
        bits = self.shard_bits - 1
        far = self.scatter_shards(*self.scatter_parts(*send_half), True, bits)
        near = self.scatter_shards(*self.scatter_parts(*keep_half), True, bits)
        arrived = self.swap(self.add(*far), bits)
        return self.add(self.add(*near, F32), arrived, F32)


def send_down(array, moves, shards, parts):
    pairs = [(d * shards + a, d * shards + b) for d in range(parts) for a, b in moves]
    return lax.ppermute(array, AXES, pairs)


class EightShards:
    a_moves = [(2 * z, 2 * z + 1) for z in range(4)] + [(7, 6)]
    b_moves = [(2, 3), (3, 2), (4, 5), (5, 4), (6, 7), (7, 6)]
    c_moves = [(4, 5), (5, 4), (6, 7), (7, 6)]

    def __init__(self, parts):
        self.parts = parts
        self.shard = lax.axis_index("fsdp")
        self.z, self.y = self.shard // 2, self.shard % 2

    def move(self, array, moves):
        return send_down(array, moves, 8, self.parts)

    def up(self, array, lowest):
        return self.move(array, [(2 * z + y, 2 * z + y + 2) for z in range(lowest, 3) for y in range(2)])

    def down(self, array, lowest):
        return self.move(array, [(2 * z + y + 2, 2 * z + y) for z in range(lowest, 3) for y in range(2)])

    def slot_ids(self):
        shard, z, y = self.shard, self.z, self.y
        none = jnp.int32(-1)
        return jnp.stack(
            [
                shard,
                jnp.where(y == 1, shard - 1, jnp.where(z == 3, 5, none)),
                jnp.where(z >= 1, shard - 2, none),
                jnp.where(z == 3, 3 - y, jnp.where(z >= 1, 2 * (z - 1) + 1 - y, none)),
                jnp.where(z >= 2, shard - 4, none),
                jnp.where(z >= 2, 1 - y, none),
                jnp.where(z == 3, y, none),
            ]
        ).astype(jnp.int32)

    def spread(self, own):
        up1 = self.up(own, 0)
        up2 = self.up(up1, 1)
        top = self.z == 3
        a = self.move(jnp.where(top & (self.y == 1), up1, own), self.a_moves)
        b = self.move(jnp.where(top, up2, up1), self.b_moves)
        up3 = self.up(up2, 2)
        c = self.move(jnp.where(top, up3, up2), self.c_moves)
        return [own, a, up1, b, up2, c, up3]

    def collect(self, grads):
        own, a, up1, b, up2, c, up3 = grads
        back = lambda moves: [(t, s) for s, t in moves]
        top = self.z == 3
        from_c = self.move(c, back(self.c_moves)).astype(F32)
        from_b = self.move(b, back(self.b_moves)).astype(F32)
        from_a = self.move(a, back(self.a_moves)).astype(F32)
        first = self.down((up3.astype(F32) + from_c).astype(BF16), 2).astype(F32)
        level2 = up2.astype(F32) + jnp.where(top, from_b, from_c + first)
        second = self.down(level2.astype(BF16), 1).astype(F32)
        level1 = up1.astype(F32) + jnp.where(top, jnp.where(self.y == 1, from_a, 0.0), from_b + second)
        third = self.down(level1.astype(BF16), 0).astype(F32)
        keep_a = jnp.where(top & (self.y == 1), 0.0, from_a)
        return (own.astype(F32) + keep_a + third).astype(BF16)


class AnyShards:
    def __init__(self, shards):
        self.shards = shards
        self.shard = lax.axis_index("fsdp")

    def slot_ids(self):
        return (self.shard - jnp.arange(self.shards)).astype(jnp.int32)

    def spread(self, own):
        every = lax.all_gather(own, "fsdp", axis=0, tiled=False)
        place = lambda s: (self.shard - s) % self.shards
        return [own] + [
            lax.dynamic_index_in_dim(every, place(s), 0, keepdims=False) for s in range(1, self.shards)
        ]

    def collect(self, grads):
        every = jnp.stack(grads)
        place = lambda j: (self.shard - j) % self.shards
        order = [lax.dynamic_index_in_dim(every, place(j), 0, keepdims=False) for j in range(self.shards)]
        return lax.psum_scatter(jnp.stack(order), "fsdp", scatter_dimension=0, tiled=False)


def shards(
    hidden_in, segment, position, selected, gain_attn, gain_ffn, router,
    w_query, key_weight, value_weight, w_output, w_gate, w_up, w_down, cotangent,
):
    groups, rows, model = hidden_in.shape
    tokens = groups * rows
    parts, shard_count = lax.axis_size("dp"), lax.axis_size("fsdp")
    width = model // parts
    net = Net(parts, shard_count)
    my_part, my_shard = lax.axis_index("dp"), lax.axis_index("fsdp")
    ring = EightShards(parts) if shard_count == 8 else AnyShards(shard_count)

    small = jnp.concatenate([key_weight.T, value_weight.T], axis=0)
    medium = jnp.concatenate([w_query.T, w_output], axis=0)
    large = jnp.concatenate([w_gate.T, w_up.T, w_down], axis=0)
    kv_all = net.gather(small)
    qo_all = net.gather(medium)
    ffn_all = lax.all_gather(large, AXES, axis=0, tiled=False).reshape((parts, shard_count) + large.shape)

    def heads_of(array, count):
        return array.reshape(parts, count, HEAD_DIM, width)

    kv_rows = small.shape[0] // 2
    q_rows = medium.shape[0] // 2
    keys = heads_of(kv_all[:, :, :kv_rows], KV_HEADS)
    values = heads_of(kv_all[:, :, kv_rows:], KV_HEADS)
    wkv = jnp.concatenate([keys, values], axis=2).reshape(parts, KV_HEADS * TILE, width)
    queries = heads_of(qo_all[:, :, :q_rows], QUERY_HEADS)
    outputs = heads_of(qo_all[:, :, q_rows:], QUERY_HEADS)
    half = HEAD_DIM // 2
    wq_pad = jnp.concatenate([queries, queries[:, :, half:], queries[:, :, :half]], axis=2)
    wq_pad = wq_pad.reshape(parts, QUERY_HEADS * TILE, width)
    wo_pad = jnp.concatenate([jnp.zeros_like(outputs), outputs], axis=2)
    wo_pad = wo_pad.reshape(parts, QUERY_HEADS * TILE, width)

    def split(array):
        return jnp.transpose(array.reshape(tokens, parts, width), (1, 0, 2))

    def join(array):
        return jnp.transpose(array, (1, 0, 2)).reshape(groups, rows, model)

    hid4, cot4 = split(hidden_in), split(cotangent)
    vector = lambda v: v.astype(F32).reshape(parts, 1, width)
    gain_one, gain_two, route = vector(gain_attn), vector(gain_ffn), vector(router)
    chosen = selected.reshape(tokens, 1).astype(F32)

    frequency = THETA ** (-(jnp.arange(half).astype(F32) * 2.0) / HEAD_DIM)
    angles = position.reshape(tokens).astype(F32)[:, None] * frequency[None, :]
    cos, sin = jnp.cos(angles), jnp.sin(angles)
    zero, one = jnp.zeros_like(cos), jnp.ones_like(cos)
    table = lambda *four: jnp.concatenate(four, axis=1)
    kv_tables = (table(cos, cos, one, one), table(-sin, zero, zero, zero), table(zero, sin, zero, zero))
    shrink = HEAD_DIM**-0.5
    q_tables = tuple(
        shrink * t
        for t in (table(cos, cos, zero, zero), table(-sin, zero, zero, zero), table(zero, sin, zero, zero))
    )
    seg_rows = segment.astype(F32).reshape(groups, 1, rows)
    tags = jnp.where(selected == 1, segment, -1).astype(BF16).reshape(groups, rows // TILE, TILE)
    tags = jnp.pad(tags, ((0, 0), (0, 16 - rows // TILE), (0, 0)))

    xn4, s1, fg4, mix, slope = first_norm(hid4, cot4, gain_one, route, chosen)
    own_kv = kv_project(xn4, wkv, kv_tables, tags, groups)
    kvs = ring.spread(own_kv)
    q = q_project(xn4, wq_pad, q_tables[0], q_tables[1] + q_tables[2], groups)
    slot_ids = ring.slot_ids()
    o, lse = attention_forward(slot_ids, q, seg_rows, kvs)
    mid4, x24, s2 = out_project(o, wo_pad, hid4, gain_two)
    out_a, xg_a, keep_a, send_a = ffn(my_part, my_shard, 1, x24, fg4, ffn_all)
    out_b, xg_b, keep_b, send_b = ffn(my_part, my_shard, 0, x24, fg4, ffn_all)
    hidden4, part4, ag4, router_sum, gain_two_sum = middle_step(
        mid4, hid4, cot4, (out_a, out_b), (xg_a, xg_b), mix, slope, s2, gain_two, route
    )
    do, keep_o, send_o = out_back(my_part, ag4, wo_pad, o)
    dq, dkvs = attention_backward(slot_ids, q, do, o, lse, seg_rows, q_tables, kvs)
    keep_q, send_q = q_back(my_part, dq, xn4)
    dkv = ring.collect(dkvs).reshape(tokens, KV_HEADS * TILE)
    kvb, keep_kv, send_kv = kv_back(my_part, dkv, kv_tables, xn4)
    grad_in4, gain_one_sum = final_step(dq, kvb, wq_pad, wkv, hid4, part4, s1, gain_one)

    sums = lax.psum(jnp.stack([gain_one_sum, gain_two_sum, router_sum]), AXES).reshape(3, model)

    ffn_grad = net.scatter_halves((keep_b, send_b), (keep_a, send_a))
    o_grad = net.scatter(keep_o, send_o, q_rows)
    q_grad = net.scatter(keep_q, send_q, q_rows)

    def by_shard(array):
        tiles = array.reshape(array.shape[0], KV_HEADS, 2, HEAD_DIM, width)
        both = jnp.transpose(tiles, (0, 2, 1, 3, 4)).reshape(-1, 2, shard_count, kv_rows, width)
        return jnp.transpose(both, (0, 2, 1, 3, 4)).reshape(-1, 2 * shard_count * kv_rows, width)

    kv_grad = net.scatter(by_shard(keep_kv), by_shard(send_kv), 2 * kv_rows)
    third = ffn_grad.shape[0] // 3
    return (
        join(hidden4),
        join(grad_in4),
        sums[0],
        sums[1],
        sums[2],
        q_grad.T,
        kv_grad[:kv_rows].T,
        kv_grad[kv_rows:].T,
        o_grad,
        ffn_grad[:third].T,
        ffn_grad[third : 2 * third].T,
        ffn_grad[2 * third :],
    )


def solution(mesh):
    tokens = P("dp", "fsdp")
    inner_first = P("fsdp", "dp")
    return jax.shard_map(
        shards,
        mesh=mesh,
        in_specs=(P("dp", "fsdp", None),) + (tokens,) * 3 + (P(),) * 3
        + (tokens,) * 3 + (inner_first,) + (tokens,) * 2 + (inner_first, P("dp", "fsdp", None)),
        out_specs=(P("dp", "fsdp", None),) * 2 + (P(),) * 3
        + (tokens,) * 3 + (inner_first,) + (tokens,) * 2 + (inner_first,),
        check_vma=False,
    )
```

```python
import functools

import jax
import jax.numpy as jnp
from jax import lax
from jax.experimental import pallas as pl
from jax.experimental.pallas import tpu as pltpu
from jax.sharding import PartitionSpec as P

QUERY_HEADS = 15
KV_HEADS = 5
SHARE = QUERY_HEADS // KV_HEADS
HEAD_DIM = 64
TILE = 128
PROMPT = 1024
LONGEST = 192
EPSILON = 1e-05
THETA = 10000.0
MINUS_LARGE = -1e30
AXES = ("dp", "fsdp")
F32 = jnp.float32
BF16 = jnp.bfloat16
VMEM_BYTES = 60 * 1024 * 1024

NT = (((1,), (1,)), ((), ()))
NN = (((1,), (0,)), ((), ()))
TN = (((0,), (0,)), ((), ()))


def dot(a, b, dims=NN):
    return lax.dot_general(a, b, dims, preferred_element_type=F32)


def params(steps=0):
    return pltpu.CompilerParams(
        vmem_limit_bytes=VMEM_BYTES,
        dimension_semantics=("arbitrary",) * steps if steps else None,
    )


def cost(flops, moved, exps=0):
    return pl.CostEstimate(flops=int(flops), bytes_accessed=int(moved), transcendentals=int(exps))


def whole(shape):
    zeros = (0,) * len(shape)
    return pl.BlockSpec(shape, lambda *_: zeros)


def norm_kernel(hid_ref, cot_ref, gain_ref, router_ref, sel_ref, xn_ref, s1_ref, fg_ref, mix_ref, slope_ref):
    parts, _, width = hid_ref.shape
    square = 0.0
    logit = 0.0
    for d in range(parts):
        x = hid_ref[d].astype(F32)
        square = square + jnp.sum(x * x, axis=-1, keepdims=True)
        logit = logit + jnp.sum(x * router_ref[d], axis=-1, keepdims=True)
    scale = lax.rsqrt(square / (parts * width) + EPSILON)
    chance = 1.0 / (1.0 + jnp.exp(-logit))
    mix = sel_ref[...] * chance
    s1_ref[...] = scale
    mix_ref[...] = mix
    slope_ref[...] = mix * (1.0 - chance)
    for d in range(parts):
        x = hid_ref[d].astype(F32)
        xn_ref[d] = (x * scale * gain_ref[d]).astype(BF16)
        fg_ref[d] = (cot_ref[d].astype(F32) * mix).astype(BF16)


def first_norm(hid4, cot4, gain, router, chosen):
    parts, tokens, width = hid4.shape
    rows = 128
    block = pl.BlockSpec((parts, rows, width), lambda i: (0, i, 0))
    column = pl.BlockSpec((rows, 1), lambda i: (i, 0))
    vector = whole((parts, 1, width))
    return pl.pallas_call(
        norm_kernel,
        grid=(tokens // rows,),
        in_specs=[block, block, vector, vector, column],
        out_specs=[block, column, block, column, column],
        out_shape=[
            jax.ShapeDtypeStruct(hid4.shape, BF16),
            jax.ShapeDtypeStruct((tokens, 1), F32),
            jax.ShapeDtypeStruct(hid4.shape, BF16),
            jax.ShapeDtypeStruct((tokens, 1), F32),
            jax.ShapeDtypeStruct((tokens, 1), F32),
        ],
        compiler_params=params(1),
        cost_estimate=cost(tokens * 960 * 10, tokens * 960 * 8),
        name="first_norm",
    )(hid4, cot4, gain, router, chosen)


def kv_kernel(xn_ref, w_ref, cos_ref, sin1_ref, sin2_ref, tag_ref, out_ref):
    rows = xn_ref.shape[1]
    total = 0.0
    for d in range(xn_ref.shape[0]):
        total = total + dot(xn_ref[d], w_ref[d], NT)
    for h in range(KV_HEADS):
        u = total[:, h * TILE : (h + 1) * TILE]
        turned = (
            u * cos_ref[...]
            + pltpu.roll(u, TILE - HEAD_DIM // 2, 1) * sin1_ref[...]
            + pltpu.roll(u, HEAD_DIM // 2, 1) * sin2_ref[...]
        )
        out_ref[:rows, h * TILE : (h + 1) * TILE] = turned.astype(BF16)
        out_ref[rows:, h * TILE : (h + 1) * TILE] = tag_ref[0]


def kv_project(groups, xn4, wkv, tables, tags):
    parts, tokens, width = xn4.shape
    rows = tokens // groups
    table = pl.BlockSpec((rows, TILE), lambda g: (g, 0))
    return pl.pallas_call(
        kv_kernel,
        grid=(groups,),
        in_specs=[
            pl.BlockSpec((parts, rows, width), lambda g: (0, g, 0)),
            whole(wkv.shape),
            table,
            table,
            table,
            pl.BlockSpec((1, 16, TILE), lambda g: (g, 0, 0)),
        ],
        out_specs=pl.BlockSpec((None, rows + 16, KV_HEADS * TILE), lambda g: (g, 0, 0)),
        out_shape=jax.ShapeDtypeStruct((groups, rows + 16, KV_HEADS * TILE), BF16),
        compiler_params=params(1),
        cost_estimate=cost(2 * tokens * 960 * 640, 3 * tokens * 960 * 2),
        name="kv_project",
    )(xn4, wkv, *tables, tags)


def q_kernel(xn_ref, w_ref, cos_ref, sin_ref, out_ref):
    for h in range(QUERY_HEADS):
        u = 0.0
        for d in range(xn_ref.shape[0]):
            u = u + dot(xn_ref[d], w_ref[d, h * TILE : (h + 1) * TILE], NT)
        turned = u * cos_ref[...] + pltpu.roll(u, HEAD_DIM, 1) * sin_ref[...]
        out_ref[:, h * TILE : (h + 1) * TILE] = turned.astype(BF16)


def q_project(xn4, wq_pad, cos_q, sin_q, groups):
    parts, tokens, width = xn4.shape
    rows = tokens // groups
    table = pl.BlockSpec((rows, TILE), lambda g: (g, 0))
    return pl.pallas_call(
        q_kernel,
        grid=(groups,),
        in_specs=[
            pl.BlockSpec((parts, rows, width), lambda g: (0, g, 0)),
            whole(wq_pad.shape),
            table,
            table,
        ],
        out_specs=pl.BlockSpec((rows, QUERY_HEADS * TILE), lambda g: (g, 0)),
        out_shape=jax.ShapeDtypeStruct((tokens, QUERY_HEADS * TILE), BF16),
        compiler_params=params(1),
        cost_estimate=cost(2 * tokens * 960 * 1920, 6 * tokens * 960 * 2),
        name="q_project",
    )(xn4, wq_pad, cos_q, sin_q)


def slot_needed(slot_ref, s, rows):
    own = slot_ref[0]
    block = slot_ref[s]
    prompt_blocks = PROMPT // rows
    reach = -(-(LONGEST - 1) // rows)
    near = (block < prompt_blocks) | (block >= own - reach)
    return (block >= 0) & (block <= own) & near


def fill_bias(slot_ref, seg_ref, kv_refs, pair_ref, key_ref, turned):
    pairs, rows, _ = pair_ref.shape
    for s, kv_ref in enumerate(kv_refs):
        needed = slot_needed(slot_ref, s, rows)
        for i in range(rows // TILE):
            here = slice(i * TILE, (i + 1) * TILE)
            tag_row = kv_ref[rows : rows + 16, 0:TILE].astype(F32)[i : i + 1]
            tag = jnp.where(needed, jnp.broadcast_to(tag_row, (TILE, TILE)).T, -1.0)
            if s >= pairs:
                lane = lax.broadcasted_iota(jnp.int32, (TILE, TILE), 1)
                hidden = (tag != 0.0) & (lane == HEAD_DIM)
                key_ref[s - pairs, here, :] = jnp.where(hidden, MINUS_LARGE, 0.0).astype(BF16)
                continue
            for j in range(rows // TILE):
                there = slice(j * TILE, (j + 1) * TILE)
                allowed = (tag == 0.0) | (tag == seg_ref[0, :, there])
                if s == 0:
                    key_row = i * TILE + lax.broadcasted_iota(jnp.int32, (TILE, TILE), 0)
                    query_row = j * TILE + lax.broadcasted_iota(jnp.int32, (TILE, TILE), 1)
                    allowed = (allowed & (key_row <= query_row)) | (key_row == query_row)
                bias = jnp.where(allowed, 0.0, MINUS_LARGE)
                if turned:
                    pair_ref[s, there, here] = bias.T
                else:
                    pair_ref[s, here, there] = bias


def lanes_of(dtype, shape, test):
    return jnp.where(test(lax.broadcasted_iota(jnp.int32, shape, 1)), 1.0, 0.0).astype(dtype)


def load_keys(kv_refs, pair_ref, key_ref):
    pairs, rows, _ = pair_ref.shape
    kvs = [ref[:rows, :] for ref in kv_refs]
    other = lanes_of(BF16, (1, TILE), lambda lane: lane != HEAD_DIM)
    marked = [kv * other + (key_ref[s - pairs] if s >= pairs else 0.0) for s, kv in enumerate(kvs)]
    return jnp.concatenate(kvs, axis=0), jnp.concatenate([m.astype(BF16) for m in marked], axis=0)


def mark(q):
    return q + lanes_of(BF16, (1, TILE), lambda lane: lane == HEAD_DIM)


def forward_kernel(slots, slot_ref, q_ref, seg_ref, *refs):
    kv_refs = refs[:slots]
    o_ref, lse_ref, pair_ref, key_ref = refs[slots:]
    rows = q_ref.shape[0]
    pairs = pair_ref.shape[0]

    @pl.when(pl.program_id(1) == 0)
    def _():
        fill_bias(slot_ref, seg_ref, kv_refs, pair_ref, key_ref, True)

    kvs, marked = load_keys(kv_refs, pair_ref, key_ref)
    low = lanes_of(BF16, (1, TILE), lambda lane: lane < HEAD_DIM)
    counted = kvs * (1.0 - low) + low
    lane = lax.broadcasted_iota(jnp.int32, (rows, TILE), 1)
    weights, peaks = [], []
    for j in range(SHARE):
        here = slice(j * TILE, (j + 1) * TILE)
        raw = dot(mark(q_ref[:, here]), marked, NT)
        parts = [raw[:, s * rows : (s + 1) * rows] + pair_ref[s] for s in range(pairs)]
        if slots > pairs:
            parts.append(raw[:, pairs * rows :])
        score = jnp.concatenate(parts, axis=1)
        peak = score[:, :TILE]
        for t in range(1, score.shape[1] // TILE):
            peak = jnp.maximum(peak, score[:, t * TILE : (t + 1) * TILE])
        peak = jnp.max(peak, axis=1, keepdims=True)
        peaks.append(peak)
        weights.append(jnp.exp(score - peak).astype(BF16))
    accs = dot(jnp.concatenate(weights, axis=0), counted)
    for j, peak in enumerate(peaks):
        here = slice(j * TILE, (j + 1) * TILE)
        acc = accs[j * rows : (j + 1) * rows]
        total = jnp.where(lane < HEAD_DIM, acc, 1.0)
        mixed = acc * pltpu.roll(1.0 / total, HEAD_DIM, 1)
        o_ref[:, here] = jnp.where(lane >= HEAD_DIM, mixed, 0.0).astype(BF16)
        lse_ref[0, 0, :, j * rows : (j + 1) * rows] = (peak + jnp.log(total)).T[0:1]


def attention_forward(slot_ids, q, seg, kvs, pairs):
    groups, _, rows = seg.shape
    slots = len(kvs)
    tokens = groups * rows
    wide = SHARE * rows
    heads = pl.BlockSpec((rows, SHARE * TILE), lambda g, h, _: (g, h))
    return pl.pallas_call(
        functools.partial(forward_kernel, slots),
        grid_spec=pltpu.PrefetchScalarGridSpec(
            num_scalar_prefetch=1,
            grid=(groups, KV_HEADS),
            in_specs=[heads, pl.BlockSpec((1, 1, rows), lambda g, h, _: (g, 0, 0))]
            + [pl.BlockSpec((None, rows + 16, TILE), lambda g, h, _: (g, 0, h))] * slots,
            out_specs=[heads, pl.BlockSpec((1, 1, 1, wide), lambda g, h, _: (g, h, 0, 0))],
            scratch_shapes=[
                pltpu.VMEM((pairs, rows, rows), F32),
                pltpu.VMEM((max(slots - pairs, 1), rows, TILE), BF16),
            ],
        ),
        out_shape=[
            jax.ShapeDtypeStruct(q.shape, BF16),
            jax.ShapeDtypeStruct((groups, KV_HEADS, 1, wide), F32),
        ],
        compiler_params=params(2),
        cost_estimate=cost(2 * 15 * tokens * 1536 * 256, 8 * tokens * 960 * 2, 15 * tokens * 1536),
        name="attention_forward",
    )(slot_ids, q, seg, *kvs)


def backward_kernel(slots, slot_ref, q_ref, do_ref, o_ref, lse_ref, seg_ref, cos_ref, sin1_ref, sin2_ref, *refs):
    kv_refs = refs[:slots]
    dq_ref = refs[slots]
    dkv_refs = refs[slots + 1 : -2]
    pair_ref, key_ref = refs[-2:]
    rows = q_ref.shape[0]

    @pl.when(pl.program_id(1) == 0)
    def _():
        fill_bias(slot_ref, seg_ref, kv_refs, pair_ref, key_ref, False)

    kvs, marked = load_keys(kv_refs, pair_ref, key_ref)
    pairs = pair_ref.shape[0]
    left, right = [], []
    for j in range(SHARE):
        here = slice(j * TILE, (j + 1) * TILE)
        q, do = q_ref[:, here], do_ref[:, here]
        delta = jnp.sum((do.astype(F32) * o_ref[:, here].astype(F32)).T, axis=0, keepdims=True)
        raw = dot(marked, mark(q), NT)
        parts = [raw[s * rows : (s + 1) * rows] + pair_ref[s] for s in range(pairs)]
        if slots > pairs:
            parts.append(raw[pairs * rows :])
        prob = jnp.exp(jnp.concatenate(parts, axis=0) - lse_ref[0, 0, :, j * rows : (j + 1) * rows])
        slope = (prob * (dot(kvs, do, NT) - delta)).astype(BF16)
        left += [slope, prob.astype(BF16)]
        right += [q, do]
        part = dot(slope, kvs, TN)
        back = (
            part * cos_ref[...]
            - pltpu.roll(part, TILE - HEAD_DIM // 2, 1) * sin1_ref[...]
            - pltpu.roll(part, HEAD_DIM // 2, 1) * sin2_ref[...]
        )
        dq_ref[:, here] = back.astype(BF16)
    right = jnp.concatenate(right, axis=0)
    for s in range(slots):
        band = jnp.concatenate([part[s * rows : (s + 1) * rows] for part in left], axis=1)
        dkv_refs[s][...] = dot(band, right).astype(BF16)


def attention_backward(slot_ids, q, do, o, lse, seg, tables, kvs, pairs):
    groups, _, rows = seg.shape
    slots = len(kvs)
    heads = pl.BlockSpec((rows, SHARE * TILE), lambda g, h, _: (g, h))
    seg_spec = pl.BlockSpec((1, 1, rows), lambda g, h, _: (g, 0, 0))
    kv_spec = pl.BlockSpec((None, rows + 16, TILE), lambda g, h, _: (g, 0, h))
    lse_spec = pl.BlockSpec((1, 1, 1, SHARE * rows), lambda g, h, _: (g, h, 0, 0))
    table = pl.BlockSpec((rows, TILE), lambda g, h, _: (g, 0))
    grad = pl.BlockSpec((None, rows, TILE), lambda g, h, _: (g, 0, h))
    tokens = groups * rows
    out = pl.pallas_call(
        functools.partial(backward_kernel, slots),
        grid_spec=pltpu.PrefetchScalarGridSpec(
            num_scalar_prefetch=1,
            grid=(groups, KV_HEADS),
            in_specs=[heads, heads, heads, lse_spec, seg_spec, table, table, table] + [kv_spec] * slots,
            out_specs=[heads] + [grad] * slots,
            scratch_shapes=[
                pltpu.VMEM((pairs, rows, rows), F32),
                pltpu.VMEM((max(slots - pairs, 1), rows, TILE), BF16),
            ],
        ),
        out_shape=[jax.ShapeDtypeStruct(q.shape, BF16)]
        + [jax.ShapeDtypeStruct((groups, rows, KV_HEADS * TILE), BF16)] * slots,
        compiler_params=params(2),
        cost_estimate=cost(5 * 15 * tokens * 1536 * 256, 16 * tokens * 960 * 2, 15 * tokens * 1536),
        name="attention_backward",
    )(slot_ids, q, do, o, lse, seg, *tables, *kvs)
    return out[0], out[1:]


def out_kernel(o_ref, w_ref, hid_ref, gain_ref, mid_ref, x2_ref, s2_ref):
    parts, _, width = hid_ref.shape
    o = o_ref[...]
    square = 0.0
    for d in range(parts):
        middle = hid_ref[d].astype(F32) + dot(o, w_ref[d])
        mid_ref[d] = middle
        square = square + jnp.sum(middle * middle, axis=-1, keepdims=True)
    scale = lax.rsqrt(square / (parts * width) + EPSILON)
    s2_ref[...] = scale
    for d in range(parts):
        x2_ref[d] = (mid_ref[d] * scale * gain_ref[d]).astype(BF16)


def out_project(o, wo_pad, hid4, gain):
    parts, tokens, width = hid4.shape
    rows = 128
    block = pl.BlockSpec((parts, rows, width), lambda i: (0, i, 0))
    column = pl.BlockSpec((rows, 1), lambda i: (i, 0))
    return pl.pallas_call(
        out_kernel,
        grid=(tokens // rows,),
        in_specs=[
            pl.BlockSpec((rows, o.shape[1]), lambda i: (i, 0)),
            whole(wo_pad.shape),
            block,
            whole((parts, 1, width)),
        ],
        out_specs=[block, block, column],
        out_shape=[
            jax.ShapeDtypeStruct(hid4.shape, F32),
            jax.ShapeDtypeStruct(hid4.shape, BF16),
            jax.ShapeDtypeStruct((tokens, 1), F32),
        ],
        compiler_params=params(1),
        cost_estimate=cost(2 * tokens * 960 * 1920, 8 * tokens * 960 * 2),
        name="out_project",
    )(o, wo_pad, hid4, gain)


def ffn_kernel(meta_ref, x_ref, fg_ref, w_ref, out_ref, xg_ref, keep_ref, send_ref):
    parts = x_ref.shape[0]
    count = w_ref.shape[1]
    rows = w_ref.shape[2] // 3
    width = w_ref.shape[3]
    my_part, my_place = meta_ref[0], meta_ref[2]
    bits = count.bit_length() - 1
    turn_bits = [sum((i >> b & 1) << (bits - 1 - b) for b in range(bits)) for i in range(count)]

    def tokens_of(ref, e):
        return ref[pl.ds(my_part ^ e, 1)].reshape(ref.shape[1:])

    def weight(e, which):
        part = pl.ds(my_part ^ e, 1)
        band = slice(which * rows, (which + 1) * rows)
        pieces = [w_ref[part, pl.ds(my_place ^ i, 1), band, :].reshape(rows, width) for i in turn_bits]
        return jnp.concatenate(pieces, axis=0)

    gate = 0.0
    up = 0.0
    hidden_grad = 0.0
    for e in range(parts):
        x = tokens_of(x_ref, e)
        gate = gate + dot(x, weight(e, 0), NT)
        up = up + dot(x, weight(e, 1), NT)
        hidden_grad = hidden_grad + dot(tokens_of(fg_ref, e), weight(e, 2), NT)
    chance = 1.0 / (1.0 + jnp.exp(-gate))
    silu = gate * chance
    hidden = (silu * up).astype(BF16)
    up_grad = (hidden_grad * silu).astype(BF16)
    gate_grad = (hidden_grad * up * chance * (1.0 + gate * (1.0 - chance))).astype(BF16)

    first = pl.program_id(0) == 0
    for e in range(parts):
        place = pl.ds(my_part ^ e, 1)
        out = dot(hidden, weight(e, 2))[None]
        back = (dot(gate_grad, weight(e, 0)) + dot(up_grad, weight(e, 1)))[None]

        @pl.when(first)
        def _(place=place, out=out, back=back):
            out_ref[place] = out
            xg_ref[place] = back

        @pl.when(jnp.logical_not(first))
        def _(place=place, out=out, back=back):
            out_ref[place] += out
            xg_ref[place] += back

    turned = (gate_grad.T, up_grad.T, hidden.T)
    for e in range(parts):
        target = send_ref if e % 2 else keep_ref
        for which in range(3):
            right = tokens_of(fg_ref if which == 2 else x_ref, e)
            grad = dot(turned[which], right).astype(BF16)
            for i in range(count):
                target[e // 2, i, which * rows : (which + 1) * rows, :] = grad[i * rows : (i + 1) * rows]


def ffn(my_part, my_shard, rows3, x4, fg4, weights, shard_first):
    parts, tokens, width = x4.shape
    half = weights.shape[1]
    block = pl.BlockSpec((parts, half, None, rows3, width), lambda j, m: (0, 0, m[1] ^ j, 0, 0))
    if shard_first:
        grad_block = pl.BlockSpec((None, parts // 2, half, rows3, width), lambda j, m: (j, 0, 0, 0, 0))
        grad = jax.ShapeDtypeStruct((2, parts // 2, half, rows3, width), BF16)
    else:
        grad_block = pl.BlockSpec((parts // 2, None, half, rows3, width), lambda j, m: (0, j, 0, 0, 0))
        grad = jax.ShapeDtypeStruct((parts // 2, 2, half, rows3, width), BF16)
    meta = jnp.stack([my_part, my_shard % 2, my_shard // 2]).astype(jnp.int32)
    return pl.pallas_call(
        ffn_kernel,
        grid_spec=pltpu.PrefetchScalarGridSpec(
            num_scalar_prefetch=1,
            grid=(2,),
            in_specs=[whole(x4.shape), whole(x4.shape), block],
            out_specs=[whole(x4.shape), whole(x4.shape), grad_block, grad_block],
        ),
        out_shape=[jax.ShapeDtypeStruct(x4.shape, F32)] * 2 + [grad, grad],
        compiler_params=params(1),
        cost_estimate=cost(12 * tokens * 960 * rows3 * half, 8 * tokens * 960 * 2 + 8 * 960 * rows3 * half),
        name="ffn",
    )(meta, x4, fg4, weights)


def middle_kernel(
    mid_ref, hid_ref, cot_ref, out_a_ref, out_b_ref, xg_a_ref, xg_b_ref, mix_ref, slope_ref, s2_ref, gain_ref, router_ref,
    hidden_ref, part_ref, ag_ref, router_grad_ref, gain_grad_ref,
):
    parts, rows, width = mid_ref.shape
    mix = mix_ref[...]
    scale = s2_ref[...]
    inner = 0.0
    mean = 0.0
    for d in range(parts):
        middle = mid_ref[d]
        inputs = hid_ref[d].astype(F32)
        branch = (middle - inputs) + (out_a_ref[d] + out_b_ref[d])
        upstream = cot_ref[d].astype(F32)
        inner = inner + jnp.sum(upstream * branch, axis=-1, keepdims=True)
        hidden_ref[d] = (inputs + mix * branch).astype(BF16)
        mean = mean + jnp.sum((xg_a_ref[d] + xg_b_ref[d]) * gain_ref[d] * middle, axis=-1, keepdims=True)
    logit_grad = slope_ref[...] * inner
    mean = mean / (parts * width) * (scale * scale * scale)
    first = pl.program_id(0) == 0
    for d in range(parts):
        middle = mid_ref[d]
        inputs = hid_ref[d].astype(F32)
        upstream = cot_ref[d].astype(F32)
        grad = xg_a_ref[d] + xg_b_ref[d]
        middle_grad = scale * (grad * gain_ref[d]) - middle * mean
        ag_ref[d] = (upstream * mix + middle_grad).astype(BF16)
        part_ref[d] = upstream + logit_grad * router_ref[d] + middle_grad
        router_grad = jnp.sum(logit_grad * inputs, axis=0, keepdims=True)
        gain_grad = jnp.sum(grad * middle * scale, axis=0, keepdims=True)

        @pl.when(first)
        def _(d=d, router_grad=router_grad, gain_grad=gain_grad):
            router_grad_ref[d] = router_grad
            gain_grad_ref[d] = gain_grad

        @pl.when(jnp.logical_not(first))
        def _(d=d, router_grad=router_grad, gain_grad=gain_grad):
            router_grad_ref[d] += router_grad
            gain_grad_ref[d] += gain_grad


def middle_step(mid4, hid4, cot4, outs, grads, mix, slope, s2, gain, router):
    parts, tokens, width = mid4.shape
    rows = 128
    block = pl.BlockSpec((parts, rows, width), lambda i: (0, i, 0))
    column = pl.BlockSpec((rows, 1), lambda i: (i, 0))
    vector = whole((parts, 1, width))
    return pl.pallas_call(
        middle_kernel,
        grid=(tokens // rows,),
        in_specs=[block] * 7 + [column] * 3 + [vector] * 2,
        out_specs=[block, block, block, vector, vector],
        out_shape=[
            jax.ShapeDtypeStruct(mid4.shape, BF16),
            jax.ShapeDtypeStruct(mid4.shape, F32),
            jax.ShapeDtypeStruct(mid4.shape, BF16),
            jax.ShapeDtypeStruct((parts, 1, width), F32),
            jax.ShapeDtypeStruct((parts, 1, width), F32),
        ],
        compiler_params=params(1),
        cost_estimate=cost(tokens * 960 * 30, tokens * 960 * 36),
        name="middle_step",
    )(mid4, hid4, cot4, *outs, *grads, mix, slope, s2, gain, router)


def compact(tile_major, upper):
    count = tile_major.shape[0] // TILE
    start = HEAD_DIM if upper else 0
    return jnp.concatenate(
        [tile_major[h * TILE + start : h * TILE + start + HEAD_DIM] for h in range(count)], axis=0
    )


def out_back_kernel(ag_ref, w_ref, do_ref):
    for h in range(QUERY_HEADS):
        total = 0.0
        for d in range(ag_ref.shape[0]):
            total = total + dot(ag_ref[d], w_ref[d, h * TILE : (h + 1) * TILE], NT)
        do_ref[:, h * TILE : (h + 1) * TILE] = total.astype(BF16)


def out_back(ag4, wo_pad):
    parts, tokens, width = ag4.shape
    rows = 256
    return pl.pallas_call(
        out_back_kernel,
        grid=(tokens // rows,),
        in_specs=[pl.BlockSpec((parts, rows, width), lambda i: (0, i, 0)), whole(wo_pad.shape)],
        out_specs=pl.BlockSpec((rows, wo_pad.shape[1]), lambda i: (i, 0)),
        out_shape=jax.ShapeDtypeStruct((tokens, wo_pad.shape[1]), BF16),
        compiler_params=params(1),
        cost_estimate=cost(2 * tokens * 960 * 1920, 6 * tokens * 960 * 2),
        name="out_back",
    )(ag4, wo_pad)


def qo_back_kernel(meta_ref, dq_ref, xn_ref, w_ref, o_ref, ag_ref, keep_ref, send_ref, xg_ref):
    parts = xn_ref.shape[0]
    sides = ((compact(dq_ref[...].T, False), xn_ref), (compact(o_ref[...].T, True), ag_ref))
    for e in range(parts):
        target = send_ref if e % 2 else keep_ref
        for i, (left, ref) in enumerate(sides):
            right = ref[pl.ds(meta_ref[0] ^ e, 1)].reshape(ref.shape[1:])
            target[e // 2, i] = dot(left, right).astype(BF16)
    for d in range(parts):
        xg_ref[d] = dot(dq_ref[...], w_ref[d])


def qo_back(my_part, dq, xn4, wq_pad, o, ag4):
    parts, tokens, width = xn4.shape
    grad = jax.ShapeDtypeStruct((parts // 2, 2, QUERY_HEADS * HEAD_DIM, width), BF16)
    return pl.pallas_call(
        qo_back_kernel,
        grid_spec=pltpu.PrefetchScalarGridSpec(
            num_scalar_prefetch=1,
            grid=(1,),
            in_specs=[whole(a.shape) for a in (dq, xn4, wq_pad, o, ag4)],
            out_specs=[whole(grad.shape), whole(grad.shape), whole(xn4.shape)],
        ),
        out_shape=[grad, grad, jax.ShapeDtypeStruct(xn4.shape, F32)],
        compiler_params=params(1),
        cost_estimate=cost(2 * tokens * 960 * 3840, 14 * tokens * 960 * 2),
        name="qo_back",
    )(my_part.reshape(1), dq, xn4, wq_pad, o, ag4)


def kv_back_kernel(meta_ref, dkv_ref, cos_ref, sin1_ref, sin2_ref, xn_ref, back_ref, keep_ref, send_ref):
    for h in range(KV_HEADS):
        u = dkv_ref[:, h * TILE : (h + 1) * TILE].astype(F32)
        back = (
            u * cos_ref[...]
            - pltpu.roll(u, TILE - HEAD_DIM // 2, 1) * sin1_ref[...]
            - pltpu.roll(u, HEAD_DIM // 2, 1) * sin2_ref[...]
        )
        back_ref[:, h * TILE : (h + 1) * TILE] = back.astype(BF16)
    turned = back_ref[...].T
    for e in range(xn_ref.shape[0]):
        x = xn_ref[pl.ds(meta_ref[0] ^ e, 1)].reshape(xn_ref.shape[1:])
        target = send_ref if e % 2 else keep_ref
        target[e // 2] = dot(turned, x).astype(BF16)


def kv_back(my_part, dkv, tables, xn4):
    parts, tokens, width = xn4.shape
    grad = jax.ShapeDtypeStruct((parts // 2, KV_HEADS * TILE, width), BF16)
    table = whole((tokens, TILE))
    return pl.pallas_call(
        kv_back_kernel,
        grid_spec=pltpu.PrefetchScalarGridSpec(
            num_scalar_prefetch=1,
            grid=(1,),
            in_specs=[whole(dkv.shape), table, table, table, whole(xn4.shape)],
            out_specs=[whole((tokens, KV_HEADS * TILE)), whole(grad.shape), whole(grad.shape)],
        ),
        out_shape=[jax.ShapeDtypeStruct((tokens, KV_HEADS * TILE), BF16), grad, grad],
        compiler_params=params(1),
        cost_estimate=cost(2 * tokens * 960 * 640, 6 * tokens * 960 * 2),
        name="kv_back",
    )(my_part.reshape(1), dkv, *tables, xn4)


def final_kernel(xg_ref, kvb_ref, wkv_ref, hid_ref, part_ref, s1_ref, gain_ref, out_ref, gain_grad_ref):
    parts, rows, width = hid_ref.shape
    scale = s1_ref[...]
    kvb = kvb_ref[...]
    mean = 0.0
    first = pl.program_id(0) == 0
    for d in range(parts):
        grad = xg_ref[d] + dot(kvb, wkv_ref[d])
        inputs = hid_ref[d].astype(F32)
        gain_grad = jnp.sum(grad * inputs * scale, axis=0, keepdims=True)
        scaled = grad * gain_ref[d]
        out_ref[d] = scaled
        mean = mean + jnp.sum(scaled * inputs, axis=-1, keepdims=True)

        @pl.when(first)
        def _(d=d, gain_grad=gain_grad):
            gain_grad_ref[d] = gain_grad

        @pl.when(jnp.logical_not(first))
        def _(d=d, gain_grad=gain_grad):
            gain_grad_ref[d] += gain_grad

    mean = mean / (parts * width) * (scale * scale * scale)
    for d in range(parts):
        out_ref[d] = part_ref[d] + scale * out_ref[d] - hid_ref[d].astype(F32) * mean


def final_step(xg4, kvb, wkv, hid4, part4, s1, gain):
    parts, tokens, width = hid4.shape
    rows = 128
    block = pl.BlockSpec((parts, rows, width), lambda i: (0, i, 0))
    column = pl.BlockSpec((rows, 1), lambda i: (i, 0))
    vector = whole((parts, 1, width))
    return pl.pallas_call(
        final_kernel,
        grid=(tokens // rows,),
        in_specs=[
            block,
            pl.BlockSpec((rows, kvb.shape[1]), lambda i: (i, 0)),
            whole(wkv.shape),
            block,
            block,
            column,
            vector,
        ],
        out_specs=[block, vector],
        out_shape=[
            jax.ShapeDtypeStruct(hid4.shape, F32),
            jax.ShapeDtypeStruct((parts, 1, width), F32),
        ],
        compiler_params=params(1),
        cost_estimate=cost(2 * tokens * 960 * 640, 10 * tokens * 960 * 2),
        name="final_step",
    )(xg4, kvb, wkv, hid4, part4, s1, gain)


class Clock:
    def __init__(self):
        self.token = jnp.zeros((8, TILE), F32)

    def at(self, *values):
        out = lax.optimization_barrier(values + (self.token,))
        self.token = out[-1]
        return out[0] if len(values) == 1 else out[:-1]

    def after(self, value):
        return lax.optimization_barrier((value, self.token))[0]


def add(mine, other, dtype=BF16):
    return (mine.astype(F32) + other.astype(F32)).astype(dtype)


class Net:
    def __init__(self, clock, parts, shards):
        self.clock = clock
        self.parts, self.shards = parts, shards
        self.size = parts * shards
        self.index = lax.axis_index("dp") * shards + lax.axis_index("fsdp")
        self.bits = self.size.bit_length() - 1
        self.core = shards.bit_length() - 1
        self.order = list(range(self.core - 1, -1, -1)) + list(range(self.core + 1, self.bits)) + [self.core]

    def swap(self, array, bit):
        flip = 1 << bit
        return lax.ppermute(self.clock.at(array), AXES, [(i, i ^ flip) for i in range(self.size)])

    def on(self, bit):
        return (self.index >> bit) & 1 == 1


class Gather:
    def __init__(self, net, array):
        self.net = net
        self.shape = array.shape
        self.array = array
        self.left = list(net.order)
        self.other = None

    def step(self):
        net = self.net
        if self.other is not None:
            bit = self.left.pop(0)
            other = net.clock.at(self.other)
            here = net.on(bit)
            self.array = jnp.stack([jnp.where(here, other, self.array), jnp.where(here, self.array, other)])
        if self.left:
            self.other = net.swap(self.array, self.left[0])

    def finish(self):
        while self.left:
            self.step()
        net = self.net
        place = {bit: net.bits - 1 - i for i, bit in enumerate(net.order)}
        high_first = [place[bit] for bit in range(net.bits - 1, -1, -1)]
        array = jnp.transpose(self.array, high_first + list(range(net.bits, self.array.ndim)))
        return array.reshape((net.parts, net.shards) + self.shape)


class Scatter:
    def __init__(self, net, keep, send, sections, rows, by_distance=None):
        self.net, self.relative = net, by_distance is not None
        self.left = [net.core] + (by_distance or list(reversed(net.order[:-1])))
        width = keep.shape[-1]
        if self.relative:
            shape = (-1, rows, width)
        else:
            shape = (net.parts // 2, sections, net.shards, rows, width)
        self.keep, self.other = keep.reshape(shape), net.swap(send, self.left.pop(0)).reshape(shape)

    def halves(self, array, bit):
        if self.relative or bit > self.net.core:
            half = array.shape[0] // 2
            return array[:half], array[half:]
        if array.ndim == 5:
            array = array[0]
        pairs = array.reshape((array.shape[0], -1, 2) + array.shape[2:])
        on = (self.net.index >> bit) & 1
        pick = lambda i: lax.dynamic_index_in_dim(pairs, i, 2, keepdims=False)
        return pick(on), pick(1 - on)

    def land(self):
        self.other = self.net.clock.at(self.other)

    def send(self):
        bit = self.left.pop(0)
        keep, send = self.halves(self.keep, bit)
        other_keep, other_send = self.halves(self.other, bit)
        self.keep = add(keep, other_keep)
        self.other = self.net.swap(add(send, other_send), bit)

    def step(self):
        if self.left:
            self.land()
            self.send()

    def result(self):
        while self.left:
            self.step()
        grad = add(self.keep, self.net.clock.at(self.other), F32)
        return grad[0] if self.relative else grad.reshape((grad.shape[-4],) + grad.shape[-2:])


class SumAll:
    def __init__(self, net, array):
        self.net, self.array = net, array
        self.left = list(reversed(net.order))
        self.other = None

    def step(self):
        if self.other is not None:
            self.array = self.array + self.net.clock.at(self.other)
            self.other = None
        if self.left:
            self.other = self.net.swap(self.array, self.left.pop(0))

    def result(self):
        while self.left or self.other is not None:
            self.step()
        return self.array


class EightShards:
    a_moves = [(2 * z, 2 * z + 1) for z in range(4)] + [(7, 6)]
    b_moves = [(2, 3), (3, 2), (4, 5), (5, 4), (6, 7), (7, 6)]
    c_moves = [(4, 5), (5, 4), (6, 7), (7, 6)]

    def __init__(self, clock, parts, shards):
        self.clock, self.parts, self.shards = clock, parts, shards
        self.shard = lax.axis_index("fsdp")
        self.z, self.y = self.shard // 2, self.shard % 2
        self.top, self.odd = self.z == 3, self.y == 1

    def move(self, array, moves):
        pairs = [(d * self.shards + a, d * self.shards + b) for d in range(self.parts) for a, b in moves]
        return lax.ppermute(self.clock.at(array), AXES, pairs)

    def up(self, array, lowest):
        return self.move(array, [(2 * z + y, 2 * z + y + 2) for z in range(lowest, 3) for y in range(2)])

    def down(self, array, lowest):
        return self.move(array, [(2 * z + y + 2, 2 * z + y) for z in range(lowest, 3) for y in range(2)])

    def slot_ids(self):
        shard, z, y = self.shard, self.z, self.y
        none = jnp.int32(-1)
        return jnp.stack(
            [
                shard,
                jnp.where(y == 1, shard - 1, jnp.where(z == 3, 5, none)),
                jnp.where(z == 3, 3 - y, jnp.where(z >= 1, 2 * (z - 1) + 1 - y, none)),
                jnp.where(z >= 2, shard - 4, none),
                jnp.where(z >= 2, 1 - y, none),
                jnp.where(z == 3, y, jnp.where(z >= 1, shard - 2, none)),
            ]
        ).astype(jnp.int32)

    def spread(self, own):
        at = self.clock.at
        up1 = self.up(own, 0)
        yield
        up1 = at(up1)
        up2 = self.up(up1, 1)
        a = self.move(jnp.where(self.top & self.odd, up1, own), self.a_moves)
        yield
        up2, a = at(up2, a)
        up3 = self.up(up2, 2)
        b = self.move(jnp.where(self.top, up2, up1), self.b_moves)
        yield
        up3, b = at(up3, b)
        c = self.move(jnp.where(self.top, up3, up2), self.c_moves)
        yield
        last = jnp.where(self.top, up3, up1)
        c = at(c)
        yield [own, a, b, up2, c, last]

    pairs = 2

    def collect(self, grads):
        at = self.clock.at
        own, a, b, up2, c, last = grads
        back = lambda moves: [(t, s) for s, t in moves]
        wide = lambda array: array.astype(F32)
        from_c, from_b = self.move(c, back(self.c_moves)), self.move(b, back(self.b_moves))
        yield
        from_c = wide(at(from_c))
        first = self.down((wide(last) + from_c).astype(BF16), 2)
        from_a = self.move(a, back(self.a_moves))
        yield
        from_b, first = at(from_b, first)
        from_b, first = wide(from_b), wide(first)
        second = self.down((wide(up2) + jnp.where(self.top, from_b, from_c + first)).astype(BF16), 1)
        yield
        from_a, second = at(from_a, second)
        from_a, second = wide(from_a), wide(second)
        late = self.top & self.odd
        level = jnp.where(self.top, jnp.where(self.odd, from_a, 0.0), wide(last) + from_b + second)
        third = self.down(level.astype(BF16), 0)
        yield
        third = wide(at(third))
        yield (wide(own) + jnp.where(late, 0.0, from_a) + third).astype(BF16)


class AnyShards:
    def __init__(self, clock, parts, shards):
        self.shards = shards
        self.pairs = shards
        self.shard = lax.axis_index("fsdp")

    def slot_ids(self):
        return (self.shard - jnp.arange(self.shards)).astype(jnp.int32)

    def pick(self, array, s):
        return lax.dynamic_index_in_dim(array, (self.shard - s) % self.shards, 0, keepdims=False)

    def spread(self, own):
        every = lax.all_gather(own, "fsdp", axis=0, tiled=False)
        yield from (None,) * 4
        yield [own] + [self.pick(every, s) for s in range(1, self.shards)]

    def collect(self, grads):
        every = jnp.stack(grads)
        order = jnp.stack([self.pick(every, s) for s in range(self.shards)])
        yield from (None,) * 4
        yield lax.psum_scatter(order, "fsdp", scatter_dimension=0, tiled=False)


def shards(
    hidden_in, segment, position, selected, gain_attn, gain_ffn, router,
    w_query, key_weight, value_weight, w_output, w_gate, w_up, w_down, cotangent,
):
    groups, rows, model = hidden_in.shape
    tokens = groups * rows
    parts, shard_count = lax.axis_size("dp"), lax.axis_size("fsdp")
    width = model // parts
    clock = Clock()
    at = clock.at
    net = Net(clock, parts, shard_count)
    my_part, my_shard = lax.axis_index("dp"), lax.axis_index("fsdp")
    ring = (EightShards if shard_count == 8 else AnyShards)(clock, parts, shard_count)

    small = jnp.concatenate([key_weight.T, value_weight.T, w_query.T], axis=0)
    kv_rows, q_rows = key_weight.shape[1], w_query.shape[1]
    gate_rows, up_rows = w_gate.T, w_up.T
    chunk_rows = w_down.shape[0] // 2
    large = [w[c * chunk_rows : (c + 1) * chunk_rows] for c in range(2) for w in (gate_rows, up_rows, w_down)]
    large = [jnp.concatenate(large[:3] + [w_output], axis=0), jnp.concatenate(large[3:], axis=0)]

    def heads_of(array, count):
        return array.reshape(parts, count, HEAD_DIM, width)

    def split(array):
        return jnp.transpose(array.reshape(tokens, parts, width), (1, 0, 2))

    def join(array):
        return jnp.transpose(array, (1, 0, 2)).reshape(groups, rows, model)

    half = HEAD_DIM // 2
    frequency = THETA ** (-(jnp.arange(half).astype(F32) * 2.0) / HEAD_DIM)
    angles = position.reshape(tokens).astype(F32)[:, None] * frequency[None, :]
    cos, sin = jnp.cos(angles), jnp.sin(angles)
    zero, one = jnp.zeros_like(cos), jnp.ones_like(cos)
    table = lambda *four: jnp.concatenate(four, axis=1)
    kv_tables = (table(cos, cos, one, one), table(-sin, zero, zero, zero), table(zero, sin, zero, zero))
    shrink = HEAD_DIM**-0.5
    q_tables = tuple(
        shrink * t
        for t in (table(cos, cos, zero, zero), table(-sin, zero, zero, zero), table(zero, sin, zero, zero))
    )
    seg_rows = segment.astype(F32).reshape(groups, 1, rows)
    tags = jnp.where(selected == 1, segment, -1).astype(BF16).reshape(groups, rows // TILE, TILE)
    tags = jnp.pad(tags, ((0, 0), (0, 16 - rows // TILE), (0, 0)))
    hid4, cot4 = split(hidden_in), split(cotangent)
    vector = lambda v: v.astype(F32).reshape(parts, 1, width)
    gain_one, gain_two, route = vector(gain_attn), vector(gain_ffn), vector(router)
    chosen = selected.reshape(tokens, 1).astype(F32)

    small_gather = Gather(net, small)
    small_gather.step()
    small_gather.step()
    small_gather.step()
    xn4, s1, fg4, mix, slope = first_norm(hid4, cot4, gain_one, route, chosen)
    xn4 = at(xn4)
    small_gather.step()
    first_all = lax.all_gather(clock.after(large[0]), AXES, axis=0, tiled=False)
    small_all = small_gather.finish()
    keys = heads_of(small_all[:, :, :kv_rows], KV_HEADS)
    values = heads_of(small_all[:, :, kv_rows : 2 * kv_rows], KV_HEADS)
    wkv = jnp.concatenate([keys, values], axis=2).reshape(parts, KV_HEADS * TILE, width)
    spread = ring.spread(kv_project(groups, xn4, wkv, kv_tables, tags))
    next(spread)
    queries = heads_of(small_all[:, :, 2 * kv_rows :], QUERY_HEADS)
    wq_pad = jnp.concatenate([queries, queries[:, :, half:], queries[:, :, :half]], axis=2)
    wq_pad = wq_pad.reshape(parts, QUERY_HEADS * TILE, width)
    q = at(q_project(xn4, wq_pad, q_tables[0], q_tables[1] + q_tables[2], groups))
    next(spread)
    second_all = lax.all_gather(clock.after(large[1]), AXES, axis=0, tiled=False)
    next(spread)
    next(spread)
    slot_ids = ring.slot_ids()
    kvs = next(spread)
    o, lse = at(*attention_forward(slot_ids, q, seg_rows, kvs, ring.pairs))
    outputs = heads_of(first_all[:, 3 * chunk_rows :], QUERY_HEADS)
    wo_pad = jnp.concatenate([jnp.zeros_like(outputs), outputs], axis=2)
    wo_pad = wo_pad.reshape(parts, QUERY_HEADS * TILE, width)
    mid4, x24, s2 = out_project(o, wo_pad, hid4, gain_two)
    x24 = at(x24)

    ffn_all = [a.reshape((parts, shard_count // 2, 2) + a.shape[1:]) for a in (first_all, second_all)]
    bits = net.order[:-1][::-1]
    parts_bits = [bit for bit in bits if bit > net.core]
    shards_bits = [bit for bit in bits if bit < net.core]
    out_a, xg_a, keep_a, send_a = ffn(my_part, my_shard, 3 * chunk_rows, x24, fg4, ffn_all[0], False)
    scatter_a = Scatter(net, keep_a, send_a, 1, 3 * chunk_rows, parts_bits + shards_bits)
    out_b, xg_b, keep_b, send_b = ffn(my_part, my_shard, 3 * chunk_rows, x24, fg4, ffn_all[1], True)
    scatter_b = Scatter(net, keep_b, send_b, 1, 3 * chunk_rows, shards_bits[:1] + parts_bits + shards_bits[1:])
    scatter_a.step()
    out_b = at(out_b)
    hidden4, part4, ag4, router_sum, gain_two_sum = middle_step(
        mid4, hid4, cot4, (out_a, out_b), (xg_a, xg_b), mix, slope, s2, gain_two, route
    )
    ag4 = at(ag4)
    scatter_b.step()
    do = at(out_back(ag4, wo_pad))
    dq, dkvs = attention_backward(slot_ids, q, do, o, lse, seg_rows, q_tables, kvs, ring.pairs)
    dq = at(dq)
    scatter_b.land()
    scatter_a.land()
    collect = ring.collect(dkvs)
    next(collect)
    scatter_b.send()
    keep_qo, send_qo, xg_q = qo_back(my_part, dq, xn4, wq_pad, o, ag4)
    xg_q = at(xg_q)
    next(collect)
    scatter_qo = Scatter(net, keep_qo, send_qo, 2, q_rows)
    next(collect)
    scatter_a.send()
    scatter_qo.step()
    next(collect)
    scatter_b.step()
    dkv = next(collect).reshape(tokens, KV_HEADS * TILE)
    kvb, keep_kv, send_kv = kv_back(my_part, dkv, kv_tables, xn4)

    def by_kind(array):
        tiles = array.reshape(array.shape[0], KV_HEADS, 2, HEAD_DIM, width)
        return jnp.transpose(tiles, (0, 2, 1, 3, 4))

    scatter_kv = Scatter(net, by_kind(keep_kv), by_kind(send_kv), 2, kv_rows)
    kvb = at(kvb)
    grad_in4, gain_one_sum = final_step(xg_q, kvb, wkv, hid4, part4, s1, gain_one)
    scatter_kv.step()
    scatter_a.step()
    scatter_qo.step()
    scatter_b.step()
    sums = SumAll(net, jnp.stack([gain_one_sum, gain_two_sum, router_sum]))
    sums.step()
    for _ in range(net.bits):
        scatter_kv.step()
        sums.step()
        scatter_qo.step()
        scatter_a.step()
        scatter_b.step()
    kv_grad = scatter_kv.result()
    sums = sums.result().reshape(3, model)
    q_grad, o_grad = scatter_qo.result()
    grads = [s.result().reshape(3, chunk_rows, width) for s in (scatter_a, scatter_b)]
    gate_grad, up_grad, down_grad = jnp.concatenate(grads, axis=1)
    return (
        join(hidden4),
        join(grad_in4),
        sums[0],
        sums[1],
        sums[2],
        q_grad.T,
        kv_grad[0].T,
        kv_grad[1].T,
        o_grad,
        gate_grad.T,
        up_grad.T,
        down_grad,
    )


def solution(mesh):
    tokens = P("dp", "fsdp")
    inner_first = P("fsdp", "dp")
    return jax.shard_map(
        shards,
        mesh=mesh,
        in_specs=(P("dp", "fsdp", None),) + (tokens,) * 3 + (P(),) * 3
        + (tokens,) * 3 + (inner_first,) + (tokens,) * 2 + (inner_first, P("dp", "fsdp", None)),
        out_specs=(P("dp", "fsdp", None),) * 2 + (P(),) * 3
        + (tokens,) * 3 + (inner_first,) + (tokens,) * 2 + (inner_first,),
        check_vma=False,
    )
```

```python
import functools

import jax
import jax.numpy as jnp
from jax import lax
from jax.experimental import pallas as pl
from jax.experimental.pallas import tpu as pltpu
from jax.sharding import PartitionSpec as P

MODEL_DIM = 960
QUERY_HEADS = 15
KV_HEADS = 5
SHARE = QUERY_HEADS // KV_HEADS
HEAD_DIM = 64
TILE = 128
PROMPT = 1024
LONGEST = 192
EPSILON = 1e-05
THETA = 10000.0
MINUS_LARGE = -1e30
AXES = ("dp", "fsdp")
F32 = jnp.float32
BF16 = jnp.bfloat16
VMEM_BYTES = 60 * 1024 * 1024

NT = (((1,), (1,)), ((), ()))
NN = (((1,), (0,)), ((), ()))
TN = (((0,), (0,)), ((), ()))


def dot(a, b, dims=NN):
    return lax.dot_general(a, b, dims, preferred_element_type=F32)


def params(steps=0):
    return pltpu.CompilerParams(
        vmem_limit_bytes=VMEM_BYTES,
        dimension_semantics=("arbitrary",) * steps if steps else None,
    )


def cost(flops, moved, exps=0):
    return pl.CostEstimate(flops=int(flops), bytes_accessed=int(moved), transcendentals=int(exps))


def whole(shape):
    zeros = (0,) * len(shape)
    return pl.BlockSpec(shape, lambda *_: zeros)


def side_by_side(ref):
    return jnp.concatenate([ref[d] for d in range(ref.shape[0])], axis=1)


def by_distance(ref, my_part):
    parts = ref.shape[0]
    return jnp.concatenate([ref[pl.ds(my_part ^ e, 1)].reshape(ref.shape[1:]) for e in range(parts)], axis=1)


def whole_rows(pieces):
    return jnp.concatenate([piece[:, : MODEL_DIM // len(pieces)] for piece in pieces], axis=1)


def norm_kernel(hid_ref, cot_ref, gain_ref, router_ref, sel_ref, xn_ref, s1_ref, fg_ref, mix_ref, slope_ref):
    parts, _, width = hid_ref.shape
    square = 0.0
    logit = 0.0
    for d in range(parts):
        x = hid_ref[d].astype(F32)
        square = square + jnp.sum(x * x, axis=-1, keepdims=True)
        logit = logit + jnp.sum(x * router_ref[d], axis=-1, keepdims=True)
    scale = lax.rsqrt(square / MODEL_DIM + EPSILON)
    chance = 1.0 / (1.0 + jnp.exp(-logit))
    mix = sel_ref[...] * chance
    s1_ref[...] = scale
    mix_ref[...] = mix
    slope_ref[...] = mix * (1.0 - chance)
    for d in range(parts):
        x = hid_ref[d].astype(F32)
        xn_ref[d] = (x * scale * gain_ref[d]).astype(BF16)
        fg_ref[d] = (cot_ref[d].astype(F32) * mix).astype(BF16)


def first_norm(hid4, cot4, gain, router, chosen):
    parts, tokens, width = hid4.shape
    rows = 128
    block = pl.BlockSpec((parts, rows, width), lambda i: (0, i, 0))
    column = pl.BlockSpec((rows, 1), lambda i: (i, 0))
    vector = whole((parts, 1, width))
    return pl.pallas_call(
        norm_kernel,
        grid=(tokens // rows,),
        in_specs=[block, block, vector, vector, column],
        out_specs=[block, column, block, column, column],
        out_shape=[
            jax.ShapeDtypeStruct(hid4.shape, BF16),
            jax.ShapeDtypeStruct((tokens, 1), F32),
            jax.ShapeDtypeStruct(hid4.shape, BF16),
            jax.ShapeDtypeStruct((tokens, 1), F32),
            jax.ShapeDtypeStruct((tokens, 1), F32),
        ],
        compiler_params=params(1),
        cost_estimate=cost(tokens * 960 * 10, tokens * 960 * 8),
        name="first_norm",
    )(hid4, cot4, gain, router, chosen)


def kv_kernel(xn_ref, w_ref, cos_ref, sin1_ref, sin2_ref, tag_ref, out_ref):
    rows = xn_ref.shape[1]
    total = dot(side_by_side(xn_ref), side_by_side(w_ref), NT)
    for h in range(KV_HEADS):
        u = total[:, h * TILE : (h + 1) * TILE]
        turned = (
            u * cos_ref[...]
            + pltpu.roll(u, TILE - HEAD_DIM // 2, 1) * sin1_ref[...]
            + pltpu.roll(u, HEAD_DIM // 2, 1) * sin2_ref[...]
        )
        out_ref[:rows, h * TILE : (h + 1) * TILE] = turned.astype(BF16)
        out_ref[rows:, h * TILE : (h + 1) * TILE] = tag_ref[0]


def kv_project(groups, xn4, wkv, tables, tags):
    parts, tokens, width = xn4.shape
    rows = tokens // groups
    table = pl.BlockSpec((rows, TILE), lambda g: (g, 0))
    return pl.pallas_call(
        kv_kernel,
        grid=(groups,),
        in_specs=[
            pl.BlockSpec((parts, rows, width), lambda g: (0, g, 0)),
            whole(wkv.shape),
            table,
            table,
            table,
            pl.BlockSpec((1, 16, TILE), lambda g: (g, 0, 0)),
        ],
        out_specs=pl.BlockSpec((None, rows + 16, KV_HEADS * TILE), lambda g: (g, 0, 0)),
        out_shape=jax.ShapeDtypeStruct((groups, rows + 16, KV_HEADS * TILE), BF16),
        compiler_params=params(1),
        cost_estimate=cost(2 * tokens * 960 * 640, 3 * tokens * 960 * 2),
        name="kv_project",
    )(xn4, wkv, *tables, tags)


def q_kernel(xn_ref, w_ref, cos_ref, sin_ref, out_ref):
    total = dot(side_by_side(xn_ref), side_by_side(w_ref), NT)
    for h in range(QUERY_HEADS):
        u = total[:, h * TILE : (h + 1) * TILE]
        turned = u * cos_ref[...] + pltpu.roll(u, HEAD_DIM, 1) * sin_ref[...]
        out_ref[:, h * TILE : (h + 1) * TILE] = turned.astype(BF16)


def q_project(xn4, wq_pad, cos_q, sin_q, groups):
    parts, tokens, width = xn4.shape
    rows = tokens // groups
    table = pl.BlockSpec((rows, TILE), lambda g: (g, 0))
    return pl.pallas_call(
        q_kernel,
        grid=(groups,),
        in_specs=[
            pl.BlockSpec((parts, rows, width), lambda g: (0, g, 0)),
            whole(wq_pad.shape),
            table,
            table,
        ],
        out_specs=pl.BlockSpec((rows, QUERY_HEADS * TILE), lambda g: (g, 0)),
        out_shape=jax.ShapeDtypeStruct((tokens, QUERY_HEADS * TILE), BF16),
        compiler_params=params(1),
        cost_estimate=cost(2 * tokens * 960 * 1920, 6 * tokens * 960 * 2),
        name="q_project",
    )(xn4, wq_pad, cos_q, sin_q)


def slot_needed(slot_ref, s, rows):
    own = slot_ref[0]
    block = slot_ref[s]
    prompt_blocks = PROMPT // rows
    reach = -(-(LONGEST - 1) // rows)
    near = (block < prompt_blocks) | (block >= own - reach)
    return (block >= 0) & (block <= own) & near


def fill_bias(slot_ref, seg_ref, kv_refs, pair_ref, key_ref, turned):
    pairs, rows, _ = pair_ref.shape
    for s, kv_ref in enumerate(kv_refs):
        needed = slot_needed(slot_ref, s, rows)
        for i in range(rows // TILE):
            here = slice(i * TILE, (i + 1) * TILE)
            tag_row = kv_ref[rows : rows + 16, 0:TILE].astype(F32)[i : i + 1]
            tag = jnp.where(needed, jnp.broadcast_to(tag_row, (TILE, TILE)).T, -1.0)
            if s >= pairs:
                lane = lax.broadcasted_iota(jnp.int32, (TILE, TILE), 1)
                hidden = (tag != 0.0) & (lane == HEAD_DIM)
                key_ref[s - pairs, here, :] = jnp.where(hidden, MINUS_LARGE, 0.0).astype(BF16)
                continue
            for j in range(rows // TILE):
                there = slice(j * TILE, (j + 1) * TILE)
                allowed = (tag == 0.0) | (tag == seg_ref[0, :, there])
                if s == 0:
                    key_row = i * TILE + lax.broadcasted_iota(jnp.int32, (TILE, TILE), 0)
                    query_row = j * TILE + lax.broadcasted_iota(jnp.int32, (TILE, TILE), 1)
                    allowed = (allowed & (key_row <= query_row)) | (key_row == query_row)
                bias = jnp.where(allowed, 0.0, MINUS_LARGE)
                if turned:
                    pair_ref[s, there, here] = bias.T
                else:
                    pair_ref[s, here, there] = bias


def lanes_of(dtype, shape, test):
    return jnp.where(test(lax.broadcasted_iota(jnp.int32, shape, 1)), 1.0, 0.0).astype(dtype)


def load_keys(kv_refs, pair_ref, key_ref):
    pairs, rows, _ = pair_ref.shape
    kvs = [ref[:rows, :] for ref in kv_refs]
    other = lanes_of(BF16, (1, TILE), lambda lane: lane != HEAD_DIM)
    marked = [kv * other + (key_ref[s - pairs] if s >= pairs else 0.0) for s, kv in enumerate(kvs)]
    return jnp.concatenate(kvs, axis=0), jnp.concatenate([m.astype(BF16) for m in marked], axis=0)


def mark(q):
    return q + lanes_of(BF16, (1, TILE), lambda lane: lane == HEAD_DIM)


def forward_kernel(slots, slot_ref, q_ref, seg_ref, *refs):
    kv_refs = refs[:slots]
    o_ref, lse_ref, pair_ref, key_ref = refs[slots:]
    rows = q_ref.shape[0]
    pairs = pair_ref.shape[0]

    @pl.when(pl.program_id(1) == 0)
    def _():
        fill_bias(slot_ref, seg_ref, kv_refs, pair_ref, key_ref, True)

    kvs, marked = load_keys(kv_refs, pair_ref, key_ref)
    low = lanes_of(BF16, (1, TILE), lambda lane: lane < HEAD_DIM)
    counted = kvs * (1.0 - low) + low
    lane = lax.broadcasted_iota(jnp.int32, (rows, TILE), 1)
    weights, peaks = [], []
    for j in range(SHARE):
        here = slice(j * TILE, (j + 1) * TILE)
        raw = dot(mark(q_ref[:, here]), marked, NT)
        parts = [raw[:, s * rows : (s + 1) * rows] + pair_ref[s] for s in range(pairs)]
        if slots > pairs:
            parts.append(raw[:, pairs * rows :])
        score = jnp.concatenate(parts, axis=1)
        peak = score[:, :TILE]
        for t in range(1, score.shape[1] // TILE):
            peak = jnp.maximum(peak, score[:, t * TILE : (t + 1) * TILE])
        peak = jnp.max(peak, axis=1, keepdims=True)
        peaks.append(peak)
        weights.append(jnp.exp(score - peak).astype(BF16))
    accs = dot(jnp.concatenate(weights, axis=0), counted)
    for j, peak in enumerate(peaks):
        here = slice(j * TILE, (j + 1) * TILE)
        acc = accs[j * rows : (j + 1) * rows]
        total = jnp.where(lane < HEAD_DIM, acc, 1.0)
        mixed = acc * pltpu.roll(1.0 / total, HEAD_DIM, 1)
        o_ref[:, here] = jnp.where(lane >= HEAD_DIM, mixed, 0.0).astype(BF16)
        lse_ref[0, 0, :, j * rows : (j + 1) * rows] = (peak + jnp.log(total)).T[0:1]


def attention_forward(slot_ids, q, seg, kvs, pairs):
    groups, _, rows = seg.shape
    slots = len(kvs)
    tokens = groups * rows
    wide = SHARE * rows
    heads = pl.BlockSpec((rows, SHARE * TILE), lambda g, h, _: (g, h))
    return pl.pallas_call(
        functools.partial(forward_kernel, slots),
        grid_spec=pltpu.PrefetchScalarGridSpec(
            num_scalar_prefetch=1,
            grid=(groups, KV_HEADS),
            in_specs=[heads, pl.BlockSpec((1, 1, rows), lambda g, h, _: (g, 0, 0))]
            + [pl.BlockSpec((None, rows + 16, TILE), lambda g, h, _: (g, 0, h))] * slots,
            out_specs=[heads, pl.BlockSpec((1, 1, 1, wide), lambda g, h, _: (g, h, 0, 0))],
            scratch_shapes=[
                pltpu.VMEM((pairs, rows, rows), F32),
                pltpu.VMEM((max(slots - pairs, 1), rows, TILE), BF16),
            ],
        ),
        out_shape=[
            jax.ShapeDtypeStruct(q.shape, BF16),
            jax.ShapeDtypeStruct((groups, KV_HEADS, 1, wide), F32),
        ],
        compiler_params=params(2),
        cost_estimate=cost(2 * 15 * tokens * 1536 * 256, 8 * tokens * 960 * 2, 15 * tokens * 1536),
        name="attention_forward",
    )(slot_ids, q, seg, *kvs)


def backward_kernel(slots, slot_ref, q_ref, do_ref, o_ref, lse_ref, seg_ref, cos_ref, sin1_ref, sin2_ref, *refs):
    kv_refs = refs[:slots]
    dq_ref = refs[slots]
    dkv_refs = refs[slots + 1 : -2]
    pair_ref, key_ref = refs[-2:]
    rows = q_ref.shape[0]

    @pl.when(pl.program_id(1) == 0)
    def _():
        fill_bias(slot_ref, seg_ref, kv_refs, pair_ref, key_ref, False)

    kvs, marked = load_keys(kv_refs, pair_ref, key_ref)
    pairs = pair_ref.shape[0]
    left, right = [], []
    for j in range(SHARE):
        here = slice(j * TILE, (j + 1) * TILE)
        q, do = q_ref[:, here], do_ref[:, here]
        delta = jnp.sum((do.astype(F32) * o_ref[:, here].astype(F32)).T, axis=0, keepdims=True)
        raw = dot(marked, mark(q), NT)
        parts = [raw[s * rows : (s + 1) * rows] + pair_ref[s] for s in range(pairs)]
        if slots > pairs:
            parts.append(raw[pairs * rows :])
        prob = jnp.exp(jnp.concatenate(parts, axis=0) - lse_ref[0, 0, :, j * rows : (j + 1) * rows])
        slope = (prob * (dot(kvs, do, NT) - delta)).astype(BF16)
        left += [slope, prob.astype(BF16)]
        right += [q, do]
        part = dot(slope, kvs, TN)
        back = (
            part * cos_ref[...]
            - pltpu.roll(part, TILE - HEAD_DIM // 2, 1) * sin1_ref[...]
            - pltpu.roll(part, HEAD_DIM // 2, 1) * sin2_ref[...]
        )
        dq_ref[:, here] = back.astype(BF16)
    right = jnp.concatenate(right, axis=0)
    for s in range(slots):
        band = jnp.concatenate([part[s * rows : (s + 1) * rows] for part in left], axis=1)
        dkv_refs[s][...] = dot(band, right).astype(BF16)


def attention_backward(slot_ids, q, do, o, lse, seg, tables, kvs, pairs):
    groups, _, rows = seg.shape
    slots = len(kvs)
    heads = pl.BlockSpec((rows, SHARE * TILE), lambda g, h, _: (g, h))
    seg_spec = pl.BlockSpec((1, 1, rows), lambda g, h, _: (g, 0, 0))
    kv_spec = pl.BlockSpec((None, rows + 16, TILE), lambda g, h, _: (g, 0, h))
    lse_spec = pl.BlockSpec((1, 1, 1, SHARE * rows), lambda g, h, _: (g, h, 0, 0))
    table = pl.BlockSpec((rows, TILE), lambda g, h, _: (g, 0))
    grad = pl.BlockSpec((None, rows, TILE), lambda g, h, _: (g, 0, h))
    tokens = groups * rows
    out = pl.pallas_call(
        functools.partial(backward_kernel, slots),
        grid_spec=pltpu.PrefetchScalarGridSpec(
            num_scalar_prefetch=1,
            grid=(groups, KV_HEADS),
            in_specs=[heads, heads, heads, lse_spec, seg_spec, table, table, table] + [kv_spec] * slots,
            out_specs=[heads] + [grad] * slots,
            scratch_shapes=[
                pltpu.VMEM((pairs, rows, rows), F32),
                pltpu.VMEM((max(slots - pairs, 1), rows, TILE), BF16),
            ],
        ),
        out_shape=[jax.ShapeDtypeStruct(q.shape, BF16)]
        + [jax.ShapeDtypeStruct((groups, rows, KV_HEADS * TILE), BF16)] * slots,
        compiler_params=params(2),
        cost_estimate=cost(5 * 15 * tokens * 1536 * 256, 16 * tokens * 960 * 2, 15 * tokens * 1536),
        name="attention_backward",
    )(slot_ids, q, do, o, lse, seg, *tables, *kvs)
    return out[0], out[1:]


def out_kernel(o_ref, w_ref, hid_ref, gain_ref, mid_ref, x2_ref, s2_ref):
    parts, _, width = hid_ref.shape
    out = dot(o_ref[...], side_by_side(w_ref))
    square = 0.0
    for d in range(parts):
        middle = hid_ref[d].astype(F32) + out[:, d * width : (d + 1) * width]
        mid_ref[d] = middle
        square = square + jnp.sum(middle * middle, axis=-1, keepdims=True)
    scale = lax.rsqrt(square / MODEL_DIM + EPSILON)
    s2_ref[...] = scale
    for d in range(parts):
        x2_ref[d] = (mid_ref[d] * scale * gain_ref[d]).astype(BF16)


def out_project(o, wo_pad, hid4, gain):
    parts, tokens, width = hid4.shape
    rows = 256
    block = pl.BlockSpec((parts, rows, width), lambda i: (0, i, 0))
    column = pl.BlockSpec((rows, 1), lambda i: (i, 0))
    return pl.pallas_call(
        out_kernel,
        grid=(tokens // rows,),
        in_specs=[
            pl.BlockSpec((rows, o.shape[1]), lambda i: (i, 0)),
            whole(wo_pad.shape),
            block,
            whole((parts, 1, width)),
        ],
        out_specs=[block, block, column],
        out_shape=[
            jax.ShapeDtypeStruct(hid4.shape, F32),
            jax.ShapeDtypeStruct(hid4.shape, BF16),
            jax.ShapeDtypeStruct((tokens, 1), F32),
        ],
        compiler_params=params(1),
        cost_estimate=cost(2 * tokens * 960 * 1920, 8 * tokens * 960 * 2),
        name="out_project",
    )(o, wo_pad, hid4, gain)


def ffn_kernel(meta_ref, x_ref, fg_ref, w_ref, out_ref, xg_ref, keep_ref, send_ref):
    parts, count, rows3, width = w_ref.shape
    rows = rows3 // 3
    my_part, my_place = meta_ref[0], meta_ref[2]
    bits = count.bit_length() - 1
    turn_bits = [sum((i >> b & 1) << (bits - 1 - b) for b in range(bits)) for i in range(count)]

    def weight(which):
        band = slice(which * rows, (which + 1) * rows)
        block = lambda d, i: w_ref[d, pl.ds(my_place ^ i, 1), band, :].reshape(rows, width)
        lines = [jnp.concatenate([block(d, i) for d in range(parts)], axis=1) for i in turn_bits]
        return jnp.concatenate(lines, axis=0)

    w_gate, w_up, w_down = (weight(which) for which in range(3))
    x, fg = side_by_side(x_ref), side_by_side(fg_ref)
    gate = dot(x, w_gate, NT)
    up = dot(x, w_up, NT)
    hidden_grad = dot(fg, w_down, NT)
    chance = 1.0 / (1.0 + jnp.exp(-gate))
    silu = gate * chance
    hidden = (silu * up).astype(BF16)
    up_grad = (hidden_grad * silu).astype(BF16)
    gate_grad = (hidden_grad * up * chance * (1.0 + gate * (1.0 - chance))).astype(BF16)

    first = pl.program_id(0) == 0
    out = dot(hidden, w_down)
    back = dot(jnp.concatenate([gate_grad, up_grad], axis=1), jnp.concatenate([w_gate, w_up], axis=0))
    for d in range(parts):
        here = slice(d * width, (d + 1) * width)

        @pl.when(first)
        def _(d=d, here=here):
            out_ref[d] = out[:, here]
            xg_ref[d] = back[:, here]

        @pl.when(jnp.logical_not(first))
        def _(d=d, here=here):
            out_ref[d] += out[:, here]
            xg_ref[d] += back[:, here]

    x, fg = by_distance(x_ref, my_part), by_distance(fg_ref, my_part)
    for which, left in enumerate((gate_grad, up_grad, hidden)):
        left, right = left.T, fg if which == 2 else x
        for i in range(count):
            grad = dot(left[i * rows : (i + 1) * rows], right).astype(BF16)
            for e in range(parts):
                target = send_ref if e % 2 else keep_ref
                target[e // 2, i, which * rows : (which + 1) * rows, :] = grad[:, e * width : (e + 1) * width]


def ffn(my_part, my_shard, rows3, x4, fg4, weights, shard_first):
    parts, tokens, width = x4.shape
    half = weights.shape[1]
    block = pl.BlockSpec((parts, half, None, rows3, width), lambda j, m: (0, 0, m[1] ^ j, 0, 0))
    if shard_first:
        grad_block = pl.BlockSpec((None, parts // 2, half, rows3, width), lambda j, m: (j, 0, 0, 0, 0))
        grad = jax.ShapeDtypeStruct((2, parts // 2, half, rows3, width), BF16)
    else:
        grad_block = pl.BlockSpec((parts // 2, None, half, rows3, width), lambda j, m: (0, j, 0, 0, 0))
        grad = jax.ShapeDtypeStruct((parts // 2, 2, half, rows3, width), BF16)
    meta = jnp.stack([my_part, my_shard % 2, my_shard // 2]).astype(jnp.int32)
    return pl.pallas_call(
        ffn_kernel,
        grid_spec=pltpu.PrefetchScalarGridSpec(
            num_scalar_prefetch=1,
            grid=(2,),
            in_specs=[whole(x4.shape), whole(x4.shape), block],
            out_specs=[whole(x4.shape), whole(x4.shape), grad_block, grad_block],
        ),
        out_shape=[jax.ShapeDtypeStruct(x4.shape, F32)] * 2 + [grad, grad],
        compiler_params=params(1),
        cost_estimate=cost(12 * tokens * 960 * rows3 * half, 8 * tokens * 960 * 2 + 8 * 960 * rows3 * half),
        name="ffn",
    )(meta, x4, fg4, weights)


def middle_kernel(
    mid_ref, hid_ref, cot_ref, out_a_ref, out_b_ref, xg_a_ref, xg_b_ref, mix_ref, slope_ref, s2_ref, gain_ref, router_ref,
    hidden_ref, part_ref, ag_ref, router_grad_ref, gain_grad_ref,
):
    parts, rows, width = mid_ref.shape
    mix = mix_ref[...]
    scale = s2_ref[...]
    inner = 0.0
    mean = 0.0
    rows_out = []
    for d in range(parts):
        middle = mid_ref[d]
        inputs = hid_ref[d].astype(F32)
        branch = (middle - inputs) + (out_a_ref[d] + out_b_ref[d])
        upstream = cot_ref[d].astype(F32)
        inner = inner + jnp.sum(upstream * branch, axis=-1, keepdims=True)
        rows_out.append(inputs + mix * branch)
        mean = mean + jnp.sum((xg_a_ref[d] + xg_b_ref[d]) * gain_ref[d] * middle, axis=-1, keepdims=True)
    hidden_ref[...] = whole_rows(rows_out).astype(BF16)
    logit_grad = slope_ref[...] * inner
    mean = mean / MODEL_DIM * (scale * scale * scale)
    first = pl.program_id(0) == 0
    for d in range(parts):
        middle = mid_ref[d]
        inputs = hid_ref[d].astype(F32)
        upstream = cot_ref[d].astype(F32)
        grad = xg_a_ref[d] + xg_b_ref[d]
        middle_grad = scale * (grad * gain_ref[d]) - middle * mean
        ag_ref[d] = (upstream * mix + middle_grad).astype(BF16)
        part_ref[d] = upstream + logit_grad * router_ref[d] + middle_grad
        router_grad = jnp.sum(logit_grad * inputs, axis=0, keepdims=True)
        gain_grad = jnp.sum(grad * middle * scale, axis=0, keepdims=True)

        @pl.when(first)
        def _(d=d, router_grad=router_grad, gain_grad=gain_grad):
            router_grad_ref[d] = router_grad
            gain_grad_ref[d] = gain_grad

        @pl.when(jnp.logical_not(first))
        def _(d=d, router_grad=router_grad, gain_grad=gain_grad):
            router_grad_ref[d] += router_grad
            gain_grad_ref[d] += gain_grad


def middle_step(mid4, hid4, cot4, outs, grads, mix, slope, s2, gain, router):
    parts, tokens, width = mid4.shape
    rows = 128
    block = pl.BlockSpec((parts, rows, width), lambda i: (0, i, 0))
    column = pl.BlockSpec((rows, 1), lambda i: (i, 0))
    vector = whole((parts, 1, width))
    return pl.pallas_call(
        middle_kernel,
        grid=(tokens // rows,),
        in_specs=[block] * 7 + [column] * 3 + [vector] * 2,
        out_specs=[pl.BlockSpec((rows, MODEL_DIM), lambda i: (i, 0)), block, block, vector, vector],
        out_shape=[
            jax.ShapeDtypeStruct((tokens, MODEL_DIM), BF16),
            jax.ShapeDtypeStruct(mid4.shape, F32),
            jax.ShapeDtypeStruct(mid4.shape, BF16),
            jax.ShapeDtypeStruct((parts, 1, width), F32),
            jax.ShapeDtypeStruct((parts, 1, width), F32),
        ],
        compiler_params=params(1),
        cost_estimate=cost(tokens * 960 * 30, tokens * 960 * 36),
        name="middle_step",
    )(mid4, hid4, cot4, *outs, *grads, mix, slope, s2, gain, router)


def compact(tile_major, upper):
    count = tile_major.shape[0] // TILE
    start = HEAD_DIM if upper else 0
    return jnp.concatenate(
        [tile_major[h * TILE + start : h * TILE + start + HEAD_DIM] for h in range(count)], axis=0
    )


def out_back_kernel(ag_ref, w_ref, do_ref):
    do_ref[...] = dot(side_by_side(ag_ref), side_by_side(w_ref), NT).astype(BF16)


def out_back(ag4, wo_pad):
    parts, tokens, width = ag4.shape
    rows = 256
    return pl.pallas_call(
        out_back_kernel,
        grid=(tokens // rows,),
        in_specs=[pl.BlockSpec((parts, rows, width), lambda i: (0, i, 0)), whole(wo_pad.shape)],
        out_specs=pl.BlockSpec((rows, wo_pad.shape[1]), lambda i: (i, 0)),
        out_shape=jax.ShapeDtypeStruct((tokens, wo_pad.shape[1]), BF16),
        compiler_params=params(1),
        cost_estimate=cost(2 * tokens * 960 * 1920, 6 * tokens * 960 * 2),
        name="out_back",
    )(ag4, wo_pad)


def part_grads(left, ref, my_part, targets):
    parts, _, width = ref.shape
    right = by_distance(ref, my_part)
    rows = left.shape[0]
    step = rows // 4
    for r in range(0, rows, step):
        grad = dot(left[r : r + step], right).astype(BF16)
        for e in range(parts):
            targets[e % 2][e // 2, r : r + step] = grad[:, e * width : (e + 1) * width]


def qo_back_kernel(meta_ref, dq_ref, xn_ref, w_ref, o_ref, ag_ref, keep_ref, send_ref, xg_ref):
    parts, _, width = xn_ref.shape
    sides = ((compact(dq_ref[...].T, False), xn_ref), (compact(o_ref[...].T, True), ag_ref))
    for i, (left, ref) in enumerate(sides):
        part_grads(left, ref, meta_ref[0], (keep_ref.at[:, i], send_ref.at[:, i]))
    back = dot(dq_ref[...], side_by_side(w_ref))
    for d in range(parts):
        xg_ref[d] = back[:, d * width : (d + 1) * width]


def qo_back(my_part, dq, xn4, wq_pad, o, ag4):
    parts, tokens, width = xn4.shape
    grad = jax.ShapeDtypeStruct((parts // 2, 2, QUERY_HEADS * HEAD_DIM, width), BF16)
    return pl.pallas_call(
        qo_back_kernel,
        grid_spec=pltpu.PrefetchScalarGridSpec(
            num_scalar_prefetch=1,
            grid=(1,),
            in_specs=[whole(a.shape) for a in (dq, xn4, wq_pad, o, ag4)],
            out_specs=[whole(grad.shape), whole(grad.shape), whole(xn4.shape)],
        ),
        out_shape=[grad, grad, jax.ShapeDtypeStruct(xn4.shape, F32)],
        compiler_params=params(1),
        cost_estimate=cost(2 * tokens * 960 * 3840, 14 * tokens * 960 * 2),
        name="qo_back",
    )(my_part.reshape(1), dq, xn4, wq_pad, o, ag4)


def kv_back_kernel(meta_ref, dkv_ref, cos_ref, sin1_ref, sin2_ref, xn_ref, back_ref, keep_ref, send_ref):
    for h in range(KV_HEADS):
        u = dkv_ref[:, h * TILE : (h + 1) * TILE].astype(F32)
        back = (
            u * cos_ref[...]
            - pltpu.roll(u, TILE - HEAD_DIM // 2, 1) * sin1_ref[...]
            - pltpu.roll(u, HEAD_DIM // 2, 1) * sin2_ref[...]
        )
        back_ref[:, h * TILE : (h + 1) * TILE] = back.astype(BF16)
    part_grads(back_ref[...].T, xn_ref, meta_ref[0], (keep_ref, send_ref))


def kv_back(my_part, dkv, tables, xn4):
    parts, tokens, width = xn4.shape
    grad = jax.ShapeDtypeStruct((parts // 2, KV_HEADS * TILE, width), BF16)
    table = whole((tokens, TILE))
    return pl.pallas_call(
        kv_back_kernel,
        grid_spec=pltpu.PrefetchScalarGridSpec(
            num_scalar_prefetch=1,
            grid=(1,),
            in_specs=[whole(dkv.shape), table, table, table, whole(xn4.shape)],
            out_specs=[whole((tokens, KV_HEADS * TILE)), whole(grad.shape), whole(grad.shape)],
        ),
        out_shape=[jax.ShapeDtypeStruct((tokens, KV_HEADS * TILE), BF16), grad, grad],
        compiler_params=params(1),
        cost_estimate=cost(2 * tokens * 960 * 640, 6 * tokens * 960 * 2),
        name="kv_back",
    )(my_part.reshape(1), dkv, *tables, xn4)


def final_kernel(xg_ref, kvb_ref, wkv_ref, hid_ref, part_ref, s1_ref, gain_ref, out_ref, gain_grad_ref):
    parts, rows, width = hid_ref.shape
    scale = s1_ref[...]
    back = dot(kvb_ref[...], side_by_side(wkv_ref))
    scaled_rows = []
    mean = 0.0
    first = pl.program_id(0) == 0
    for d in range(parts):
        grad = xg_ref[d] + back[:, d * width : (d + 1) * width]
        inputs = hid_ref[d].astype(F32)
        gain_grad = jnp.sum(grad * inputs * scale, axis=0, keepdims=True)
        scaled = grad * gain_ref[d]
        scaled_rows.append(scaled)
        mean = mean + jnp.sum(scaled * inputs, axis=-1, keepdims=True)

        @pl.when(first)
        def _(d=d, gain_grad=gain_grad):
            gain_grad_ref[d] = gain_grad

        @pl.when(jnp.logical_not(first))
        def _(d=d, gain_grad=gain_grad):
            gain_grad_ref[d] += gain_grad

    mean = mean / MODEL_DIM * (scale * scale * scale)
    out_ref[...] = whole_rows(
        [part_ref[d] + scale * scaled_rows[d] - hid_ref[d].astype(F32) * mean for d in range(parts)]
    )


def final_step(xg4, kvb, wkv, hid4, part4, s1, gain):
    parts, tokens, width = hid4.shape
    rows = 256
    block = pl.BlockSpec((parts, rows, width), lambda i: (0, i, 0))
    column = pl.BlockSpec((rows, 1), lambda i: (i, 0))
    vector = whole((parts, 1, width))
    return pl.pallas_call(
        final_kernel,
        grid=(tokens // rows,),
        in_specs=[
            block,
            pl.BlockSpec((rows, kvb.shape[1]), lambda i: (i, 0)),
            whole(wkv.shape),
            block,
            block,
            column,
            vector,
        ],
        out_specs=[pl.BlockSpec((rows, MODEL_DIM), lambda i: (i, 0)), vector],
        out_shape=[
            jax.ShapeDtypeStruct((tokens, MODEL_DIM), F32),
            jax.ShapeDtypeStruct((parts, 1, width), F32),
        ],
        compiler_params=params(1),
        cost_estimate=cost(2 * tokens * 960 * 640, 10 * tokens * 960 * 2),
        name="final_step",
    )(xg4, kvb, wkv, hid4, part4, s1, gain)


class Clock:
    def __init__(self):
        self.token = jnp.zeros((8, TILE), F32)

    def at(self, *values):
        out = lax.optimization_barrier(values + (self.token,))
        self.token = out[-1]
        return out[0] if len(values) == 1 else out[:-1]

    def after(self, value):
        return lax.optimization_barrier((value, self.token))[0]


def add(mine, other, dtype=BF16):
    return (mine.astype(F32) + other.astype(F32)).astype(dtype)


class Net:
    def __init__(self, clock, parts, shards):
        self.clock = clock
        self.parts, self.shards = parts, shards
        self.size = parts * shards
        self.index = lax.axis_index("dp") * shards + lax.axis_index("fsdp")
        self.bits = self.size.bit_length() - 1
        self.core = shards.bit_length() - 1
        self.order = list(range(self.core - 1, -1, -1)) + list(range(self.core + 1, self.bits)) + [self.core]

    def swap(self, array, bit):
        flip = 1 << bit
        return lax.ppermute(self.clock.at(array), AXES, [(i, i ^ flip) for i in range(self.size)])

    def on(self, bit):
        return (self.index >> bit) & 1 == 1


class Gather:
    def __init__(self, net, array):
        self.net = net
        self.shape = array.shape
        self.array = array
        self.left = list(net.order)
        self.other = None

    def step(self):
        net = self.net
        if self.other is not None:
            bit = self.left.pop(0)
            other = net.clock.at(self.other)
            here = net.on(bit)
            self.array = jnp.stack([jnp.where(here, other, self.array), jnp.where(here, self.array, other)])
        if self.left:
            self.other = net.swap(self.array, self.left[0])

    def finish(self):
        while self.left:
            self.step()
        net = self.net
        place = {bit: net.bits - 1 - i for i, bit in enumerate(net.order)}
        high_first = [place[bit] for bit in range(net.bits - 1, -1, -1)]
        array = jnp.transpose(self.array, high_first + list(range(net.bits, self.array.ndim)))
        return array.reshape((net.parts, net.shards) + self.shape)


class Scatter:
    def __init__(self, net, keep, send, sections, rows, by_distance=None):
        self.net, self.relative = net, by_distance is not None
        self.left = [net.core] + (by_distance or list(reversed(net.order[:-1])))
        width = keep.shape[-1]
        if self.relative:
            shape = (-1, rows, width)
        else:
            shape = (net.parts // 2, sections, net.shards, rows, width)
        self.keep, self.other = keep.reshape(shape), net.swap(send, self.left.pop(0)).reshape(shape)

    def halves(self, array, bit):
        if self.relative or bit > self.net.core:
            half = array.shape[0] // 2
            return array[:half], array[half:]
        if array.ndim == 5:
            array = array[0]
        pairs = array.reshape((array.shape[0], -1, 2) + array.shape[2:])
        on = (self.net.index >> bit) & 1
        pick = lambda i: lax.dynamic_index_in_dim(pairs, i, 2, keepdims=False)
        return pick(on), pick(1 - on)

    def land(self):
        self.other = self.net.clock.at(self.other)

    def send(self):
        bit = self.left.pop(0)
        keep, send = self.halves(self.keep, bit)
        other_keep, other_send = self.halves(self.other, bit)
        self.keep = add(keep, other_keep)
        self.other = self.net.swap(add(send, other_send), bit)

    def step(self):
        if self.left:
            self.land()
            self.send()

    def result(self):
        while self.left:
            self.step()
        grad = add(self.keep, self.net.clock.at(self.other), F32)
        return grad[0] if self.relative else grad.reshape((grad.shape[-4],) + grad.shape[-2:])


class SumAll:
    def __init__(self, net, array):
        self.net, self.array = net, array
        self.left = list(reversed(net.order))
        self.other = None

    def step(self):
        if self.other is not None:
            self.array = self.array + self.net.clock.at(self.other)
            self.other = None
        if self.left:
            self.other = self.net.swap(self.array, self.left.pop(0))

    def result(self):
        while self.left or self.other is not None:
            self.step()
        return self.array


class EightShards:
    a_moves = [(2 * z, 2 * z + 1) for z in range(4)] + [(7, 6)]
    b_moves = [(2, 3), (3, 2), (4, 5), (5, 4), (6, 7), (7, 6)]
    c_moves = [(4, 5), (5, 4), (6, 7), (7, 6)]

    def __init__(self, clock, parts, shards):
        self.clock, self.parts, self.shards = clock, parts, shards
        self.shard = lax.axis_index("fsdp")
        self.z, self.y = self.shard // 2, self.shard % 2
        self.top, self.odd = self.z == 3, self.y == 1

    def move(self, array, moves):
        pairs = [(d * self.shards + a, d * self.shards + b) for d in range(self.parts) for a, b in moves]
        return lax.ppermute(self.clock.at(array), AXES, pairs)

    def up(self, array, lowest):
        return self.move(array, [(2 * z + y, 2 * z + y + 2) for z in range(lowest, 3) for y in range(2)])

    def down(self, array, lowest):
        return self.move(array, [(2 * z + y + 2, 2 * z + y) for z in range(lowest, 3) for y in range(2)])

    def slot_ids(self):
        shard, z, y = self.shard, self.z, self.y
        none = jnp.int32(-1)
        return jnp.stack(
            [
                shard,
                jnp.where(y == 1, shard - 1, jnp.where(z == 3, 5, none)),
                jnp.where(z == 3, 3 - y, jnp.where(z >= 1, 2 * (z - 1) + 1 - y, none)),
                jnp.where(z >= 2, shard - 4, none),
                jnp.where(z >= 2, 1 - y, none),
                jnp.where(z == 3, y, jnp.where(z >= 1, shard - 2, none)),
            ]
        ).astype(jnp.int32)

    def spread(self, own):
        at = self.clock.at
        up1 = self.up(own, 0)
        yield
        up1 = at(up1)
        up2 = self.up(up1, 1)
        a = self.move(jnp.where(self.top & self.odd, up1, own), self.a_moves)
        yield
        up2, a = at(up2, a)
        up3 = self.up(up2, 2)
        b = self.move(jnp.where(self.top, up2, up1), self.b_moves)
        yield
        up3, b = at(up3, b)
        c = self.move(jnp.where(self.top, up3, up2), self.c_moves)
        yield
        last = jnp.where(self.top, up3, up1)
        c = at(c)
        yield [own, a, b, up2, c, last]

    pairs = 2

    def collect(self, grads):
        at = self.clock.at
        own, a, b, up2, c, last = grads
        back = lambda moves: [(t, s) for s, t in moves]
        wide = lambda array: array.astype(F32)
        from_c, from_b = self.move(c, back(self.c_moves)), self.move(b, back(self.b_moves))
        yield
        from_c = wide(at(from_c))
        first = self.down((wide(last) + from_c).astype(BF16), 2)
        from_a = self.move(a, back(self.a_moves))
        yield
        from_b, first = at(from_b, first)
        from_b, first = wide(from_b), wide(first)
        second = self.down((wide(up2) + jnp.where(self.top, from_b, from_c + first)).astype(BF16), 1)
        yield
        from_a, second = at(from_a, second)
        from_a, second = wide(from_a), wide(second)
        late = self.top & self.odd
        level = jnp.where(self.top, jnp.where(self.odd, from_a, 0.0), wide(last) + from_b + second)
        third = self.down(level.astype(BF16), 0)
        yield
        third = wide(at(third))
        yield (wide(own) + jnp.where(late, 0.0, from_a) + third).astype(BF16)


class AnyShards:
    def __init__(self, clock, parts, shards):
        self.shards = shards
        self.pairs = shards
        self.shard = lax.axis_index("fsdp")

    def slot_ids(self):
        return (self.shard - jnp.arange(self.shards)).astype(jnp.int32)

    def pick(self, array, s):
        return lax.dynamic_index_in_dim(array, (self.shard - s) % self.shards, 0, keepdims=False)

    def spread(self, own):
        every = lax.all_gather(own, "fsdp", axis=0, tiled=False)
        yield from (None,) * 4
        yield [own] + [self.pick(every, s) for s in range(1, self.shards)]

    def collect(self, grads):
        every = jnp.stack(grads)
        order = jnp.stack([self.pick(every, s) for s in range(self.shards)])
        yield from (None,) * 4
        yield lax.psum_scatter(order, "fsdp", scatter_dimension=0, tiled=False)


def shards(
    hidden_in, segment, position, selected, gain_attn, gain_ffn, router,
    w_query, key_weight, value_weight, w_output, w_gate, w_up, w_down, cotangent,
):
    groups, rows, model = hidden_in.shape
    tokens = groups * rows
    parts, shard_count = lax.axis_size("dp"), lax.axis_size("fsdp")
    columns = model // parts
    width = -(-columns // TILE) * TILE
    fill = lambda array: jnp.pad(array, ((0, 0),) * (array.ndim - 1) + ((0, width - columns),))
    clock = Clock()
    at = clock.at
    net = Net(clock, parts, shard_count)
    my_part, my_shard = lax.axis_index("dp"), lax.axis_index("fsdp")
    ring = (EightShards if shard_count == 8 else AnyShards)(clock, parts, shard_count)

    small = fill(jnp.concatenate([key_weight.T, value_weight.T, w_query.T], axis=0))
    kv_rows, q_rows = key_weight.shape[1], w_query.shape[1]
    gate_rows, up_rows = w_gate.T, w_up.T
    chunk_rows = w_down.shape[0] // 2
    large = [w[c * chunk_rows : (c + 1) * chunk_rows] for c in range(2) for w in (gate_rows, up_rows, w_down)]
    large = [fill(jnp.concatenate(large[:3] + [w_output], axis=0)), fill(jnp.concatenate(large[3:], axis=0))]

    def heads_of(array, count):
        return array.reshape(parts, count, HEAD_DIM, width)

    def split(array):
        return fill(jnp.transpose(array.reshape(tokens, parts, columns), (1, 0, 2)))

    half = HEAD_DIM // 2
    frequency = THETA ** (-(jnp.arange(half).astype(F32) * 2.0) / HEAD_DIM)
    angles = position.reshape(tokens).astype(F32)[:, None] * frequency[None, :]
    cos, sin = jnp.cos(angles), jnp.sin(angles)
    zero, one = jnp.zeros_like(cos), jnp.ones_like(cos)
    table = lambda *four: jnp.concatenate(four, axis=1)
    kv_tables = (table(cos, cos, one, one), table(-sin, zero, zero, zero), table(zero, sin, zero, zero))
    shrink = HEAD_DIM**-0.5
    q_tables = tuple(
        shrink * t
        for t in (table(cos, cos, zero, zero), table(-sin, zero, zero, zero), table(zero, sin, zero, zero))
    )
    seg_rows = segment.astype(F32).reshape(groups, 1, rows)
    tags = jnp.where(selected == 1, segment, -1).astype(BF16).reshape(groups, rows // TILE, TILE)
    tags = jnp.pad(tags, ((0, 0), (0, 16 - rows // TILE), (0, 0)))
    hid4, cot4 = split(hidden_in), split(cotangent)
    vector = lambda v: fill(v.astype(F32).reshape(parts, 1, columns))
    gain_one, gain_two, route = vector(gain_attn), vector(gain_ffn), vector(router)
    chosen = selected.reshape(tokens, 1).astype(F32)

    small_gather = Gather(net, small)
    small_gather.step()
    small_gather.step()
    small_gather.step()
    xn4, s1, fg4, mix, slope = first_norm(hid4, cot4, gain_one, route, chosen)
    xn4 = at(xn4)
    small_gather.step()
    first_all = lax.all_gather(clock.after(large[0]), AXES, axis=0, tiled=False)
    small_all = small_gather.finish()
    keys = heads_of(small_all[:, :, :kv_rows], KV_HEADS)
    values = heads_of(small_all[:, :, kv_rows : 2 * kv_rows], KV_HEADS)
    wkv = jnp.concatenate([keys, values], axis=2).reshape(parts, KV_HEADS * TILE, width)
    spread = ring.spread(kv_project(groups, xn4, wkv, kv_tables, tags))
    next(spread)
    queries = heads_of(small_all[:, :, 2 * kv_rows :], QUERY_HEADS)
    wq_pad = jnp.concatenate([queries, queries[:, :, half:], queries[:, :, :half]], axis=2)
    wq_pad = wq_pad.reshape(parts, QUERY_HEADS * TILE, width)
    q = at(q_project(xn4, wq_pad, q_tables[0], q_tables[1] + q_tables[2], groups))
    next(spread)
    second_all = lax.all_gather(clock.after(large[1]), AXES, axis=0, tiled=False)
    next(spread)
    next(spread)
    slot_ids = ring.slot_ids()
    kvs = next(spread)
    o, lse = at(*attention_forward(slot_ids, q, seg_rows, kvs, ring.pairs))
    outputs = heads_of(first_all[:, 3 * chunk_rows :], QUERY_HEADS)
    wo_pad = jnp.concatenate([jnp.zeros_like(outputs), outputs], axis=2)
    wo_pad = wo_pad.reshape(parts, QUERY_HEADS * TILE, width)
    mid4, x24, s2 = out_project(o, wo_pad, hid4, gain_two)
    x24 = at(x24)

    ffn_all = [a.reshape((parts, shard_count // 2, 2) + a.shape[1:]) for a in (first_all, second_all)]
    bits = net.order[:-1][::-1]
    parts_bits = [bit for bit in bits if bit > net.core]
    shards_bits = [bit for bit in bits if bit < net.core]
    out_a, xg_a, keep_a, send_a = ffn(my_part, my_shard, 3 * chunk_rows, x24, fg4, ffn_all[0], False)
    scatter_a = Scatter(net, keep_a, send_a, 1, 3 * chunk_rows, parts_bits + shards_bits)
    out_b, xg_b, keep_b, send_b = ffn(my_part, my_shard, 3 * chunk_rows, x24, fg4, ffn_all[1], True)
    scatter_b = Scatter(net, keep_b, send_b, 1, 3 * chunk_rows, shards_bits[:1] + parts_bits + shards_bits[1:])
    scatter_a.step()
    out_b = at(out_b)
    hidden_out, part4, ag4, router_sum, gain_two_sum = middle_step(
        mid4, hid4, cot4, (out_a, out_b), (xg_a, xg_b), mix, slope, s2, gain_two, route
    )
    ag4 = at(ag4)
    scatter_b.step()
    do = at(out_back(ag4, wo_pad))
    dq, dkvs = attention_backward(slot_ids, q, do, o, lse, seg_rows, q_tables, kvs, ring.pairs)
    dq = at(dq)
    scatter_b.land()
    scatter_a.land()
    collect = ring.collect(dkvs)
    next(collect)
    scatter_b.send()
    keep_qo, send_qo, xg_q = qo_back(my_part, dq, xn4, wq_pad, o, ag4)
    xg_q = at(xg_q)
    next(collect)
    scatter_qo = Scatter(net, keep_qo, send_qo, 2, q_rows)
    next(collect)
    scatter_a.send()
    scatter_qo.step()
    next(collect)
    scatter_b.step()
    scatter_qo.step()
    dkv = next(collect).reshape(tokens, KV_HEADS * TILE)
    kvb, keep_kv, send_kv = kv_back(my_part, dkv, kv_tables, xn4)

    def by_kind(array):
        tiles = array.reshape(array.shape[0], KV_HEADS, 2, HEAD_DIM, width)
        return jnp.transpose(tiles, (0, 2, 1, 3, 4))

    scatter_kv = Scatter(net, by_kind(keep_kv), by_kind(send_kv), 2, kv_rows)
    kvb = at(kvb)
    scatter_b.step()
    scatter_a.step()
    scatter_qo.step()
    grad_in, gain_one_sum = final_step(xg_q, kvb, wkv, hid4, part4, s1, gain_one)
    scatter_kv.step()
    sums = SumAll(net, jnp.stack([gain_one_sum, gain_two_sum, router_sum]))
    sums.step()
    scatter_b.land()
    scatter_a.step()
    scatter_qo.step()
    scatter_kv.step()
    sums.step()
    scatter_a.land()
    scatter_qo.land()
    for _ in range(net.bits):
        scatter_kv.step()
        sums.step()
    kv_grad = scatter_kv.result()
    sums = sums.result()[..., :columns].reshape(3, model)
    kv_grad = kv_grad[..., :columns]
    q_grad, o_grad = scatter_qo.result()[..., :columns]
    grads = [s.result().reshape(3, chunk_rows, width)[..., :columns] for s in (scatter_a, scatter_b)]
    gate_grad, up_grad, down_grad = jnp.concatenate(grads, axis=1)
    sums = sums + clock.token[0, 0]
    return (
        hidden_out.reshape(groups, rows, model),
        grad_in.reshape(groups, rows, model),
        sums[0],
        sums[1],
        sums[2],
        q_grad.T,
        kv_grad[0].T,
        kv_grad[1].T,
        o_grad,
        gate_grad.T,
        up_grad.T,
        down_grad,
    )


def solution(mesh):
    tokens = P("dp", "fsdp")
    inner_first = P("fsdp", "dp")
    return jax.shard_map(
        shards,
        mesh=mesh,
        in_specs=(P("dp", "fsdp", None),) + (tokens,) * 3 + (P(),) * 3
        + (tokens,) * 3 + (inner_first,) + (tokens,) * 2 + (inner_first, P("dp", "fsdp", None)),
        out_specs=(P("dp", "fsdp", None),) * 2 + (P(),) * 3
        + (tokens,) * 3 + (inner_first,) + (tokens,) * 2 + (inner_first,),
        check_vma=False,
    )
```

```python
import functools

import jax
import jax.numpy as jnp
from jax import lax
from jax.experimental import pallas as pl
from jax.experimental.pallas import tpu as pltpu
from jax.sharding import PartitionSpec as P

MODEL_DIM = 960
QUERY_HEADS = 15
KV_HEADS = 5
SHARE = QUERY_HEADS // KV_HEADS
HEAD_DIM = 64
TILE = 128
PROMPT = 1024
LONGEST = 192
EPSILON = 1e-05
THETA = 10000.0
MINUS_LARGE = -1e30
AXES = ("dp", "fsdp")
F32 = jnp.float32
BF16 = jnp.bfloat16
VMEM_BYTES = 60 * 1024 * 1024

NT = (((1,), (1,)), ((), ()))
NN = (((1,), (0,)), ((), ()))
TN = (((0,), (0,)), ((), ()))


def dot(a, b, dims=NN):
    return lax.dot_general(a, b, dims, preferred_element_type=F32)


def params(steps=0):
    return pltpu.CompilerParams(
        vmem_limit_bytes=VMEM_BYTES,
        dimension_semantics=("arbitrary",) * steps if steps else None,
    )


def cost(flops, moved, exps=0):
    return pl.CostEstimate(flops=int(flops), bytes_accessed=int(moved), transcendentals=int(exps))


def whole(shape):
    zeros = (0,) * len(shape)
    return pl.BlockSpec(shape, lambda *_: zeros)


def side_by_side(ref):
    return jnp.concatenate([ref[d] for d in range(ref.shape[0])], axis=1)


def by_distance(ref, my_part):
    parts = ref.shape[0]
    return jnp.concatenate([ref[pl.ds(my_part ^ e, 1)].reshape(ref.shape[1:]) for e in range(parts)], axis=1)


def whole_rows(pieces):
    return jnp.concatenate([piece[:, : MODEL_DIM // len(pieces)] for piece in pieces], axis=1)


def norm_kernel(hid_ref, cot_ref, gain_ref, router_ref, sel_ref, xn_ref, s1_ref, fg_ref, mix_ref, slope_ref):
    parts, _, width = hid_ref.shape
    square = 0.0
    logit = 0.0
    for d in range(parts):
        x = hid_ref[d].astype(F32)
        square = square + jnp.sum(x * x, axis=-1, keepdims=True)
        logit = logit + jnp.sum(x * router_ref[d], axis=-1, keepdims=True)
    scale = lax.rsqrt(square / MODEL_DIM + EPSILON)
    chance = 1.0 / (1.0 + jnp.exp(-logit))
    mix = sel_ref[...] * chance
    s1_ref[...] = scale
    mix_ref[...] = mix
    slope_ref[...] = mix * (1.0 - chance)
    for d in range(parts):
        x = hid_ref[d].astype(F32)
        xn_ref[d] = (x * scale * gain_ref[d]).astype(BF16)
        fg_ref[d] = (cot_ref[d].astype(F32) * mix).astype(BF16)


def first_norm(hid4, cot4, gain, router, chosen):
    parts, tokens, width = hid4.shape
    rows = 128
    block = pl.BlockSpec((parts, rows, width), lambda i: (0, i, 0))
    column = pl.BlockSpec((rows, 1), lambda i: (i, 0))
    vector = whole((parts, 1, width))
    return pl.pallas_call(
        norm_kernel,
        grid=(tokens // rows,),
        in_specs=[block, block, vector, vector, column],
        out_specs=[block, column, block, column, column],
        out_shape=[
            jax.ShapeDtypeStruct(hid4.shape, BF16),
            jax.ShapeDtypeStruct((tokens, 1), F32),
            jax.ShapeDtypeStruct(hid4.shape, BF16),
            jax.ShapeDtypeStruct((tokens, 1), F32),
            jax.ShapeDtypeStruct((tokens, 1), F32),
        ],
        compiler_params=params(1),
        cost_estimate=cost(tokens * 960 * 10, tokens * 960 * 8),
        name="first_norm",
    )(hid4, cot4, gain, router, chosen)


def kv_kernel(xn_ref, w_ref, cos_ref, sin1_ref, sin2_ref, tag_ref, out_ref):
    rows = xn_ref.shape[1]
    total = dot(side_by_side(xn_ref), side_by_side(w_ref), NT)
    for h in range(KV_HEADS):
        u = total[:, h * TILE : (h + 1) * TILE]
        turned = (
            u * cos_ref[...]
            + pltpu.roll(u, TILE - HEAD_DIM // 2, 1) * sin1_ref[...]
            + pltpu.roll(u, HEAD_DIM // 2, 1) * sin2_ref[...]
        )
        out_ref[:rows, h * TILE : (h + 1) * TILE] = turned.astype(BF16)
        out_ref[rows:, h * TILE : (h + 1) * TILE] = tag_ref[0]


def kv_project(groups, xn4, wkv, tables, tags):
    parts, tokens, width = xn4.shape
    rows = tokens // groups
    table = pl.BlockSpec((rows, TILE), lambda g: (g, 0))
    return pl.pallas_call(
        kv_kernel,
        grid=(groups,),
        in_specs=[
            pl.BlockSpec((parts, rows, width), lambda g: (0, g, 0)),
            whole(wkv.shape),
            table,
            table,
            table,
            pl.BlockSpec((1, 16, TILE), lambda g: (g, 0, 0)),
        ],
        out_specs=pl.BlockSpec((None, rows + 16, KV_HEADS * TILE), lambda g: (g, 0, 0)),
        out_shape=jax.ShapeDtypeStruct((groups, rows + 16, KV_HEADS * TILE), BF16),
        compiler_params=params(1),
        cost_estimate=cost(2 * tokens * 960 * 640, 3 * tokens * 960 * 2),
        name="kv_project",
    )(xn4, wkv, *tables, tags)


def q_kernel(xn_ref, w_ref, cos_ref, sin_ref, out_ref):
    total = dot(side_by_side(xn_ref), side_by_side(w_ref), NT)
    for h in range(QUERY_HEADS):
        u = total[:, h * TILE : (h + 1) * TILE]
        turned = u * cos_ref[...] + pltpu.roll(u, HEAD_DIM, 1) * sin_ref[...]
        out_ref[:, h * TILE : (h + 1) * TILE] = turned.astype(BF16)


def q_project(xn4, wq_pad, cos_q, sin_q, groups):
    parts, tokens, width = xn4.shape
    rows = tokens // groups
    table = pl.BlockSpec((rows, TILE), lambda g: (g, 0))
    return pl.pallas_call(
        q_kernel,
        grid=(groups,),
        in_specs=[
            pl.BlockSpec((parts, rows, width), lambda g: (0, g, 0)),
            whole(wq_pad.shape),
            table,
            table,
        ],
        out_specs=pl.BlockSpec((rows, QUERY_HEADS * TILE), lambda g: (g, 0)),
        out_shape=jax.ShapeDtypeStruct((tokens, QUERY_HEADS * TILE), BF16),
        compiler_params=params(1),
        cost_estimate=cost(2 * tokens * 960 * 1920, 6 * tokens * 960 * 2),
        name="q_project",
    )(xn4, wq_pad, cos_q, sin_q)


def slot_needed(slot_ref, s, rows):
    own = slot_ref[0]
    block = slot_ref[s]
    prompt_blocks = PROMPT // rows
    reach = -(-(LONGEST - 1) // rows)
    near = (block < prompt_blocks) | (block >= own - reach)
    return (block >= 0) & (block <= own) & near


def fill_bias(slot_ref, seg_ref, kv_refs, pair_ref, key_ref, turned):
    pairs, rows, _ = pair_ref.shape
    for s, kv_ref in enumerate(kv_refs):
        needed = slot_needed(slot_ref, s, rows)
        for i in range(rows // TILE):
            here = slice(i * TILE, (i + 1) * TILE)
            tag_row = kv_ref[rows : rows + 16, 0:TILE].astype(F32)[i : i + 1]
            tag = jnp.where(needed, jnp.broadcast_to(tag_row, (TILE, TILE)).T, -1.0)
            if s >= pairs:
                lane = lax.broadcasted_iota(jnp.int32, (TILE, TILE), 1)
                hidden = (tag != 0.0) & (lane == HEAD_DIM)
                key_ref[s - pairs, here, :] = jnp.where(hidden, MINUS_LARGE, 0.0).astype(BF16)
                continue
            for j in range(rows // TILE):
                there = slice(j * TILE, (j + 1) * TILE)
                allowed = (tag == 0.0) | (tag == seg_ref[0, :, there])
                if s == 0:
                    key_row = i * TILE + lax.broadcasted_iota(jnp.int32, (TILE, TILE), 0)
                    query_row = j * TILE + lax.broadcasted_iota(jnp.int32, (TILE, TILE), 1)
                    allowed = (allowed & (key_row <= query_row)) | (key_row == query_row)
                bias = jnp.where(allowed, 0.0, MINUS_LARGE)
                if turned:
                    pair_ref[s, there, here] = bias.T
                else:
                    pair_ref[s, here, there] = bias


def lanes_of(dtype, shape, test):
    return jnp.where(test(lax.broadcasted_iota(jnp.int32, shape, 1)), 1.0, 0.0).astype(dtype)


def load_keys(kv_refs, pair_ref, key_ref):
    pairs, rows, _ = pair_ref.shape
    kvs = [ref[:rows, :] for ref in kv_refs]
    other = lanes_of(BF16, (1, TILE), lambda lane: lane != HEAD_DIM)
    marked = [kv * other + (key_ref[s - pairs] if s >= pairs else 0.0) for s, kv in enumerate(kvs)]
    return jnp.concatenate(kvs, axis=0), jnp.concatenate([m.astype(BF16) for m in marked], axis=0)


def mark(q):
    return q + lanes_of(BF16, (1, TILE), lambda lane: lane == HEAD_DIM)


def forward_kernel(slots, slot_ref, q_ref, seg_ref, *refs):
    kv_refs = refs[:slots]
    o_ref, lse_ref, pair_ref, key_ref = refs[slots:]
    rows = q_ref.shape[0]
    pairs = pair_ref.shape[0]

    @pl.when(pl.program_id(1) == 0)
    def _():
        fill_bias(slot_ref, seg_ref, kv_refs, pair_ref, key_ref, True)

    kvs, marked = load_keys(kv_refs, pair_ref, key_ref)
    low = lanes_of(BF16, (1, TILE), lambda lane: lane < HEAD_DIM)
    counted = kvs * (1.0 - low) + low
    lane = lax.broadcasted_iota(jnp.int32, (rows, TILE), 1)
    weights, peaks = [], []
    for j in range(SHARE):
        here = slice(j * TILE, (j + 1) * TILE)
        raw = dot(mark(q_ref[:, here]), marked, NT)
        parts = [raw[:, s * rows : (s + 1) * rows] + pair_ref[s] for s in range(pairs)]
        if slots > pairs:
            parts.append(raw[:, pairs * rows :])
        score = jnp.concatenate(parts, axis=1)
        peak = score[:, :TILE]
        for t in range(1, score.shape[1] // TILE):
            peak = jnp.maximum(peak, score[:, t * TILE : (t + 1) * TILE])
        peak = jnp.max(peak, axis=1, keepdims=True)
        peaks.append(peak)
        weights.append(jnp.exp(score - peak).astype(BF16))
    accs = dot(jnp.concatenate(weights, axis=0), counted)
    for j, peak in enumerate(peaks):
        here = slice(j * TILE, (j + 1) * TILE)
        acc = accs[j * rows : (j + 1) * rows]
        total = jnp.where(lane < HEAD_DIM, acc, 1.0)
        mixed = acc * pltpu.roll(1.0 / total, HEAD_DIM, 1)
        o_ref[:, here] = jnp.where(lane >= HEAD_DIM, mixed, 0.0).astype(BF16)
        lse_ref[0, 0, :, j * rows : (j + 1) * rows] = (peak + jnp.log(total)).T[0:1]


def attention_forward(slot_ids, q, seg, kvs, pairs):
    groups, _, rows = seg.shape
    slots = len(kvs)
    tokens = groups * rows
    wide = SHARE * rows
    heads = pl.BlockSpec((rows, SHARE * TILE), lambda g, h, _: (g, h))
    return pl.pallas_call(
        functools.partial(forward_kernel, slots),
        grid_spec=pltpu.PrefetchScalarGridSpec(
            num_scalar_prefetch=1,
            grid=(groups, KV_HEADS),
            in_specs=[heads, pl.BlockSpec((1, 1, rows), lambda g, h, _: (g, 0, 0))]
            + [pl.BlockSpec((None, rows + 16, TILE), lambda g, h, _: (g, 0, h))] * slots,
            out_specs=[heads, pl.BlockSpec((1, 1, 1, wide), lambda g, h, _: (g, h, 0, 0))],
            scratch_shapes=[
                pltpu.VMEM((pairs, rows, rows), F32),
                pltpu.VMEM((max(slots - pairs, 1), rows, TILE), BF16),
            ],
        ),
        out_shape=[
            jax.ShapeDtypeStruct(q.shape, BF16),
            jax.ShapeDtypeStruct((groups, KV_HEADS, 1, wide), F32),
        ],
        compiler_params=params(2),
        cost_estimate=cost(2 * 15 * tokens * 1536 * 256, 8 * tokens * 960 * 2, 15 * tokens * 1536),
        name="attention_forward",
    )(slot_ids, q, seg, *kvs)


def backward_kernel(slots, slot_ref, q_ref, do_ref, o_ref, lse_ref, seg_ref, cos_ref, sin1_ref, sin2_ref, *refs):
    kv_refs = refs[:slots]
    dq_ref = refs[slots]
    dkv_refs = refs[slots + 1 : -2]
    pair_ref, key_ref = refs[-2:]
    rows = q_ref.shape[0]

    @pl.when(pl.program_id(1) == 0)
    def _():
        fill_bias(slot_ref, seg_ref, kv_refs, pair_ref, key_ref, False)

    kvs, marked = load_keys(kv_refs, pair_ref, key_ref)
    pairs = pair_ref.shape[0]
    left, right = [], []
    for j in range(SHARE):
        here = slice(j * TILE, (j + 1) * TILE)
        q, do = q_ref[:, here], do_ref[:, here]
        delta = jnp.sum((do.astype(F32) * o_ref[:, here].astype(F32)).T, axis=0, keepdims=True)
        raw = dot(marked, mark(q), NT)
        parts = [raw[s * rows : (s + 1) * rows] + pair_ref[s] for s in range(pairs)]
        if slots > pairs:
            parts.append(raw[pairs * rows :])
        prob = jnp.exp(jnp.concatenate(parts, axis=0) - lse_ref[0, 0, :, j * rows : (j + 1) * rows])
        slope = (prob * (dot(kvs, do, NT) - delta)).astype(BF16)
        left += [slope, prob.astype(BF16)]
        right += [q, do]
        part = dot(slope, kvs, TN)
        back = (
            part * cos_ref[...]
            - pltpu.roll(part, TILE - HEAD_DIM // 2, 1) * sin1_ref[...]
            - pltpu.roll(part, HEAD_DIM // 2, 1) * sin2_ref[...]
        )
        dq_ref[:, here] = back.astype(BF16)
    right = jnp.concatenate(right, axis=0)
    for s in range(slots):
        band = jnp.concatenate([part[s * rows : (s + 1) * rows] for part in left], axis=1)
        dkv_refs[s][...] = dot(band, right).astype(BF16)


def attention_backward(slot_ids, q, do, o, lse, seg, tables, kvs, pairs):
    groups, _, rows = seg.shape
    slots = len(kvs)
    heads = pl.BlockSpec((rows, SHARE * TILE), lambda g, h, _: (g, h))
    seg_spec = pl.BlockSpec((1, 1, rows), lambda g, h, _: (g, 0, 0))
    kv_spec = pl.BlockSpec((None, rows + 16, TILE), lambda g, h, _: (g, 0, h))
    lse_spec = pl.BlockSpec((1, 1, 1, SHARE * rows), lambda g, h, _: (g, h, 0, 0))
    table = pl.BlockSpec((rows, TILE), lambda g, h, _: (g, 0))
    grad = pl.BlockSpec((None, rows, TILE), lambda g, h, _: (g, 0, h))
    tokens = groups * rows
    out = pl.pallas_call(
        functools.partial(backward_kernel, slots),
        grid_spec=pltpu.PrefetchScalarGridSpec(
            num_scalar_prefetch=1,
            grid=(groups, KV_HEADS),
            in_specs=[heads, heads, heads, lse_spec, seg_spec, table, table, table] + [kv_spec] * slots,
            out_specs=[heads] + [grad] * slots,
            scratch_shapes=[
                pltpu.VMEM((pairs, rows, rows), F32),
                pltpu.VMEM((max(slots - pairs, 1), rows, TILE), BF16),
            ],
        ),
        out_shape=[jax.ShapeDtypeStruct(q.shape, BF16)]
        + [jax.ShapeDtypeStruct((groups, rows, KV_HEADS * TILE), BF16)] * slots,
        compiler_params=params(2),
        cost_estimate=cost(5 * 15 * tokens * 1536 * 256, 16 * tokens * 960 * 2, 15 * tokens * 1536),
        name="attention_backward",
    )(slot_ids, q, do, o, lse, seg, *tables, *kvs)
    return out[0], out[1:]


def out_kernel(o_ref, w_ref, hid_ref, gain_ref, mid_ref, x2_ref, s2_ref):
    parts, _, width = hid_ref.shape
    out = dot(o_ref[...], side_by_side(w_ref))
    square = 0.0
    for d in range(parts):
        middle = hid_ref[d].astype(F32) + out[:, d * width : (d + 1) * width]
        mid_ref[d] = middle
        square = square + jnp.sum(middle * middle, axis=-1, keepdims=True)
    scale = lax.rsqrt(square / MODEL_DIM + EPSILON)
    s2_ref[...] = scale
    for d in range(parts):
        x2_ref[d] = (mid_ref[d] * scale * gain_ref[d]).astype(BF16)


def out_project(o, wo_pad, hid4, gain):
    parts, tokens, width = hid4.shape
    rows = 256
    block = pl.BlockSpec((parts, rows, width), lambda i: (0, i, 0))
    column = pl.BlockSpec((rows, 1), lambda i: (i, 0))
    return pl.pallas_call(
        out_kernel,
        grid=(tokens // rows,),
        in_specs=[
            pl.BlockSpec((rows, o.shape[1]), lambda i: (i, 0)),
            whole(wo_pad.shape),
            block,
            whole((parts, 1, width)),
        ],
        out_specs=[block, block, column],
        out_shape=[
            jax.ShapeDtypeStruct(hid4.shape, F32),
            jax.ShapeDtypeStruct(hid4.shape, BF16),
            jax.ShapeDtypeStruct((tokens, 1), F32),
        ],
        compiler_params=params(1),
        cost_estimate=cost(2 * tokens * 960 * 1920, 8 * tokens * 960 * 2),
        name="out_project",
    )(o, wo_pad, hid4, gain)


def ffn_kernel(meta_ref, x_ref, fg_ref, w_ref, out_ref, xg_ref, keep_ref, send_ref):
    parts, count, rows3, width = w_ref.shape
    rows = rows3 // 3
    my_part, my_place = meta_ref[0], meta_ref[2]
    bits = count.bit_length() - 1
    turn_bits = [sum((i >> b & 1) << (bits - 1 - b) for b in range(bits)) for i in range(count)]

    def weight(which):
        band = slice(which * rows, (which + 1) * rows)
        block = lambda d, i: w_ref[d, pl.ds(my_place ^ i, 1), band, :].reshape(rows, width)
        lines = [jnp.concatenate([block(d, i) for d in range(parts)], axis=1) for i in turn_bits]
        return jnp.concatenate(lines, axis=0)

    w_gate, w_up, w_down = (weight(which) for which in range(3))
    x, fg = side_by_side(x_ref), side_by_side(fg_ref)
    gate = dot(x, w_gate, NT)
    up = dot(x, w_up, NT)
    hidden_grad = dot(fg, w_down, NT)
    chance = 1.0 / (1.0 + jnp.exp(-gate))
    silu = gate * chance
    hidden = (silu * up).astype(BF16)
    up_grad = (hidden_grad * silu).astype(BF16)
    gate_grad = (hidden_grad * up * chance * (1.0 + gate * (1.0 - chance))).astype(BF16)

    first = pl.program_id(0) == 0
    out = dot(hidden, w_down)
    back = dot(jnp.concatenate([gate_grad, up_grad], axis=1), jnp.concatenate([w_gate, w_up], axis=0))
    for d in range(parts):
        here = slice(d * width, (d + 1) * width)

        @pl.when(first)
        def _(d=d, here=here):
            out_ref[d] = out[:, here]
            xg_ref[d] = back[:, here]

        @pl.when(jnp.logical_not(first))
        def _(d=d, here=here):
            out_ref[d] += out[:, here]
            xg_ref[d] += back[:, here]

    x, fg = by_distance(x_ref, my_part), by_distance(fg_ref, my_part)
    for which, left in enumerate((gate_grad, up_grad, hidden)):
        left, right = left.T, fg if which == 2 else x
        for i in range(count):
            grad = dot(left[i * rows : (i + 1) * rows], right).astype(BF16)
            for e in range(parts):
                target = send_ref if e % 2 else keep_ref
                target[e // 2, i, which * rows : (which + 1) * rows, :] = grad[:, e * width : (e + 1) * width]


def ffn(my_part, my_shard, chunk, rows3, x4, fg4, weights, shard_first):
    parts, tokens, width = x4.shape
    half = weights.shape[1]
    block = pl.BlockSpec((parts, half, None, rows3, width), lambda j, m: (0, 0, m[1] ^ j, chunk, 0))
    if shard_first:
        grad_block = pl.BlockSpec((None, parts // 2, half, rows3, width), lambda j, m: (j, 0, 0, 0, 0))
        grad = jax.ShapeDtypeStruct((2, parts // 2, half, rows3, width), BF16)
    else:
        grad_block = pl.BlockSpec((parts // 2, None, half, rows3, width), lambda j, m: (0, j, 0, 0, 0))
        grad = jax.ShapeDtypeStruct((parts // 2, 2, half, rows3, width), BF16)
    meta = jnp.stack([my_part, my_shard % 2, my_shard // 2]).astype(jnp.int32)
    return pl.pallas_call(
        ffn_kernel,
        grid_spec=pltpu.PrefetchScalarGridSpec(
            num_scalar_prefetch=1,
            grid=(2,),
            in_specs=[whole(x4.shape), whole(x4.shape), block],
            out_specs=[whole(x4.shape), whole(x4.shape), grad_block, grad_block],
        ),
        out_shape=[jax.ShapeDtypeStruct(x4.shape, F32)] * 2 + [grad, grad],
        compiler_params=params(1),
        cost_estimate=cost(12 * tokens * 960 * rows3 * half, 8 * tokens * 960 * 2 + 8 * 960 * rows3 * half),
        name="ffn",
    )(meta, x4, fg4, weights)


def middle_kernel(
    mid_ref, hid_ref, cot_ref, out_a_ref, out_b_ref, xg_a_ref, xg_b_ref, mix_ref, slope_ref, s2_ref, gain_ref, router_ref,
    hidden_ref, part_ref, ag_ref, router_grad_ref, gain_grad_ref,
):
    parts, rows, width = mid_ref.shape
    mix = mix_ref[...]
    scale = s2_ref[...]
    inner = 0.0
    mean = 0.0
    rows_out = []
    for d in range(parts):
        middle = mid_ref[d]
        inputs = hid_ref[d].astype(F32)
        branch = (middle - inputs) + (out_a_ref[d] + out_b_ref[d])
        upstream = cot_ref[d].astype(F32)
        inner = inner + jnp.sum(upstream * branch, axis=-1, keepdims=True)
        rows_out.append(inputs + mix * branch)
        mean = mean + jnp.sum((xg_a_ref[d] + xg_b_ref[d]) * gain_ref[d] * middle, axis=-1, keepdims=True)
    hidden_ref[...] = whole_rows(rows_out).astype(BF16)
    logit_grad = slope_ref[...] * inner
    mean = mean / MODEL_DIM * (scale * scale * scale)
    first = pl.program_id(0) == 0
    for d in range(parts):
        middle = mid_ref[d]
        inputs = hid_ref[d].astype(F32)
        upstream = cot_ref[d].astype(F32)
        grad = xg_a_ref[d] + xg_b_ref[d]
        middle_grad = scale * (grad * gain_ref[d]) - middle * mean
        ag_ref[d] = (upstream * mix + middle_grad).astype(BF16)
        part_ref[d] = upstream + logit_grad * router_ref[d] + middle_grad
        router_grad = jnp.sum(logit_grad * inputs, axis=0, keepdims=True)
        gain_grad = jnp.sum(grad * middle * scale, axis=0, keepdims=True)

        @pl.when(first)
        def _(d=d, router_grad=router_grad, gain_grad=gain_grad):
            router_grad_ref[d] = router_grad
            gain_grad_ref[d] = gain_grad

        @pl.when(jnp.logical_not(first))
        def _(d=d, router_grad=router_grad, gain_grad=gain_grad):
            router_grad_ref[d] += router_grad
            gain_grad_ref[d] += gain_grad


def middle_step(mid4, hid4, cot4, outs, grads, mix, slope, s2, gain, router):
    parts, tokens, width = mid4.shape
    rows = 128
    block = pl.BlockSpec((parts, rows, width), lambda i: (0, i, 0))
    column = pl.BlockSpec((rows, 1), lambda i: (i, 0))
    vector = whole((parts, 1, width))
    return pl.pallas_call(
        middle_kernel,
        grid=(tokens // rows,),
        in_specs=[block] * 7 + [column] * 3 + [vector] * 2,
        out_specs=[pl.BlockSpec((rows, MODEL_DIM), lambda i: (i, 0)), block, block, vector, vector],
        out_shape=[
            jax.ShapeDtypeStruct((tokens, MODEL_DIM), BF16),
            jax.ShapeDtypeStruct(mid4.shape, F32),
            jax.ShapeDtypeStruct(mid4.shape, BF16),
            jax.ShapeDtypeStruct((parts, 1, width), F32),
            jax.ShapeDtypeStruct((parts, 1, width), F32),
        ],
        compiler_params=params(1),
        cost_estimate=cost(tokens * 960 * 30, tokens * 960 * 36),
        name="middle_step",
    )(mid4, hid4, cot4, *outs, *grads, mix, slope, s2, gain, router)


def compact(tile_major, upper):
    count = tile_major.shape[0] // TILE
    start = HEAD_DIM if upper else 0
    return jnp.concatenate(
        [tile_major[h * TILE + start : h * TILE + start + HEAD_DIM] for h in range(count)], axis=0
    )


def out_back_kernel(ag_ref, w_ref, do_ref):
    do_ref[...] = dot(side_by_side(ag_ref), side_by_side(w_ref), NT).astype(BF16)


def out_back(ag4, wo_pad):
    parts, tokens, width = ag4.shape
    rows = 256
    return pl.pallas_call(
        out_back_kernel,
        grid=(tokens // rows,),
        in_specs=[pl.BlockSpec((parts, rows, width), lambda i: (0, i, 0)), whole(wo_pad.shape)],
        out_specs=pl.BlockSpec((rows, wo_pad.shape[1]), lambda i: (i, 0)),
        out_shape=jax.ShapeDtypeStruct((tokens, wo_pad.shape[1]), BF16),
        compiler_params=params(1),
        cost_estimate=cost(2 * tokens * 960 * 1920, 6 * tokens * 960 * 2),
        name="out_back",
    )(ag4, wo_pad)


def part_grads(left, ref, my_part, targets):
    parts, _, width = ref.shape
    right = by_distance(ref, my_part)
    rows = left.shape[0]
    step = rows // 4
    for r in range(0, rows, step):
        grad = dot(left[r : r + step], right).astype(BF16)
        for e in range(parts):
            targets[e % 2][e // 2, r : r + step] = grad[:, e * width : (e + 1) * width]


def qo_back_kernel(meta_ref, dq_ref, xn_ref, w_ref, o_ref, ag_ref, keep_ref, send_ref, xg_ref):
    parts, _, width = xn_ref.shape
    sides = ((compact(dq_ref[...].T, False), xn_ref), (compact(o_ref[...].T, True), ag_ref))
    for i, (left, ref) in enumerate(sides):
        part_grads(left, ref, meta_ref[0], (keep_ref.at[:, i], send_ref.at[:, i]))
    back = dot(dq_ref[...], side_by_side(w_ref))
    for d in range(parts):
        xg_ref[d] = back[:, d * width : (d + 1) * width]


def qo_back(my_part, dq, xn4, wq_pad, o, ag4):
    parts, tokens, width = xn4.shape
    grad = jax.ShapeDtypeStruct((parts // 2, 2, QUERY_HEADS * HEAD_DIM, width), BF16)
    return pl.pallas_call(
        qo_back_kernel,
        grid_spec=pltpu.PrefetchScalarGridSpec(
            num_scalar_prefetch=1,
            grid=(1,),
            in_specs=[whole(a.shape) for a in (dq, xn4, wq_pad, o, ag4)],
            out_specs=[whole(grad.shape), whole(grad.shape), whole(xn4.shape)],
        ),
        out_shape=[grad, grad, jax.ShapeDtypeStruct(xn4.shape, F32)],
        compiler_params=params(1),
        cost_estimate=cost(2 * tokens * 960 * 3840, 14 * tokens * 960 * 2),
        name="qo_back",
    )(my_part.reshape(1), dq, xn4, wq_pad, o, ag4)


def kv_back_kernel(meta_ref, dkv_ref, cos_ref, sin1_ref, sin2_ref, xn_ref, back_ref, keep_ref, send_ref):
    for h in range(KV_HEADS):
        u = dkv_ref[:, h * TILE : (h + 1) * TILE].astype(F32)
        back = (
            u * cos_ref[...]
            - pltpu.roll(u, TILE - HEAD_DIM // 2, 1) * sin1_ref[...]
            - pltpu.roll(u, HEAD_DIM // 2, 1) * sin2_ref[...]
        )
        back_ref[:, h * TILE : (h + 1) * TILE] = back.astype(BF16)
    part_grads(back_ref[...].T, xn_ref, meta_ref[0], (keep_ref, send_ref))


def kv_back(my_part, dkv, tables, xn4):
    parts, tokens, width = xn4.shape
    grad = jax.ShapeDtypeStruct((parts // 2, KV_HEADS * TILE, width), BF16)
    table = whole((tokens, TILE))
    return pl.pallas_call(
        kv_back_kernel,
        grid_spec=pltpu.PrefetchScalarGridSpec(
            num_scalar_prefetch=1,
            grid=(1,),
            in_specs=[whole(dkv.shape), table, table, table, whole(xn4.shape)],
            out_specs=[whole((tokens, KV_HEADS * TILE)), whole(grad.shape), whole(grad.shape)],
        ),
        out_shape=[jax.ShapeDtypeStruct((tokens, KV_HEADS * TILE), BF16), grad, grad],
        compiler_params=params(1),
        cost_estimate=cost(2 * tokens * 960 * 640, 6 * tokens * 960 * 2),
        name="kv_back",
    )(my_part.reshape(1), dkv, *tables, xn4)


def final_kernel(xg_ref, kvb_ref, wkv_ref, hid_ref, part_ref, s1_ref, gain_ref, out_ref, gain_grad_ref):
    parts, rows, width = hid_ref.shape
    scale = s1_ref[...]
    back = dot(kvb_ref[...], side_by_side(wkv_ref))
    scaled_rows = []
    mean = 0.0
    first = pl.program_id(0) == 0
    for d in range(parts):
        grad = xg_ref[d] + back[:, d * width : (d + 1) * width]
        inputs = hid_ref[d].astype(F32)
        gain_grad = jnp.sum(grad * inputs * scale, axis=0, keepdims=True)
        scaled = grad * gain_ref[d]
        scaled_rows.append(scaled)
        mean = mean + jnp.sum(scaled * inputs, axis=-1, keepdims=True)

        @pl.when(first)
        def _(d=d, gain_grad=gain_grad):
            gain_grad_ref[d] = gain_grad

        @pl.when(jnp.logical_not(first))
        def _(d=d, gain_grad=gain_grad):
            gain_grad_ref[d] += gain_grad

    mean = mean / MODEL_DIM * (scale * scale * scale)
    out_ref[...] = whole_rows(
        [part_ref[d] + scale * scaled_rows[d] - hid_ref[d].astype(F32) * mean for d in range(parts)]
    )


def final_step(xg4, kvb, wkv, hid4, part4, s1, gain):
    parts, tokens, width = hid4.shape
    rows = 256
    block = pl.BlockSpec((parts, rows, width), lambda i: (0, i, 0))
    column = pl.BlockSpec((rows, 1), lambda i: (i, 0))
    vector = whole((parts, 1, width))
    return pl.pallas_call(
        final_kernel,
        grid=(tokens // rows,),
        in_specs=[
            block,
            pl.BlockSpec((rows, kvb.shape[1]), lambda i: (i, 0)),
            whole(wkv.shape),
            block,
            block,
            column,
            vector,
        ],
        out_specs=[pl.BlockSpec((rows, MODEL_DIM), lambda i: (i, 0)), vector],
        out_shape=[
            jax.ShapeDtypeStruct((tokens, MODEL_DIM), F32),
            jax.ShapeDtypeStruct((parts, 1, width), F32),
        ],
        compiler_params=params(1),
        cost_estimate=cost(2 * tokens * 960 * 640, 10 * tokens * 960 * 2),
        name="final_step",
    )(xg4, kvb, wkv, hid4, part4, s1, gain)


class Clock:
    def __init__(self):
        self.token = jnp.zeros((8, TILE), F32)

    def at(self, *values):
        out = lax.optimization_barrier(values + (self.token,))
        self.token = out[-1]
        return out[0] if len(values) == 1 else out[:-1]

    def after(self, value):
        return lax.optimization_barrier((value, self.token))[0]


def add(mine, other, dtype=BF16):
    return (mine.astype(F32) + other.astype(F32)).astype(dtype)


class Net:
    def __init__(self, clock, parts, shards):
        self.clock = clock
        self.parts, self.shards = parts, shards
        self.size = parts * shards
        self.index = lax.axis_index("dp") * shards + lax.axis_index("fsdp")
        self.bits = self.size.bit_length() - 1
        self.core = shards.bit_length() - 1
        self.order = list(range(self.core - 1, -1, -1)) + list(range(self.core + 1, self.bits)) + [self.core]

    def swap(self, array, bit):
        flip = 1 << bit
        return lax.ppermute(self.clock.at(array), AXES, [(i, i ^ flip) for i in range(self.size)])

    def on(self, bit):
        return (self.index >> bit) & 1 == 1


class Gather:
    def __init__(self, net, array):
        self.net = net
        self.shape = array.shape
        self.array = array
        self.left = list(net.order)
        self.other = None

    def step(self):
        net = self.net
        if self.other is not None:
            bit = self.left.pop(0)
            other = net.clock.at(self.other)
            here = net.on(bit)
            self.array = jnp.stack([jnp.where(here, other, self.array), jnp.where(here, self.array, other)])
        if self.left:
            self.other = net.swap(self.array, self.left[0])

    def finish(self):
        while self.left:
            self.step()
        net = self.net
        place = {bit: net.bits - 1 - i for i, bit in enumerate(net.order)}
        high_first = [place[bit] for bit in range(net.bits - 1, -1, -1)]
        array = jnp.transpose(self.array, high_first + list(range(net.bits, self.array.ndim)))
        return array.reshape((net.parts, net.shards) + self.shape)


class Scatter:
    def __init__(self, net, keep, send, sections, rows, by_distance=None):
        self.net, self.relative = net, by_distance is not None
        self.left = [net.core] + (by_distance or list(reversed(net.order[:-1])))
        width = keep.shape[-1]
        if self.relative:
            shape = (-1, rows, width)
        else:
            shape = (net.parts // 2, sections, net.shards, rows, width)
        self.keep, self.other = keep.reshape(shape), net.swap(send, self.left.pop(0)).reshape(shape)

    def halves(self, array, bit):
        if self.relative or bit > self.net.core:
            half = array.shape[0] // 2
            return array[:half], array[half:]
        if array.ndim == 5:
            array = array[0]
        pairs = array.reshape((array.shape[0], -1, 2) + array.shape[2:])
        on = (self.net.index >> bit) & 1
        pick = lambda i: lax.dynamic_index_in_dim(pairs, i, 2, keepdims=False)
        return pick(on), pick(1 - on)

    def land(self):
        self.other = self.net.clock.at(self.other)

    def send(self):
        bit = self.left.pop(0)
        keep, send = self.halves(self.keep, bit)
        other_keep, other_send = self.halves(self.other, bit)
        self.keep = add(keep, other_keep)
        self.other = self.net.swap(add(send, other_send), bit)

    def step(self):
        if self.left:
            self.land()
            self.send()

    def result(self):
        while self.left:
            self.step()
        grad = add(self.keep, self.net.clock.at(self.other), F32)
        return grad[0] if self.relative else grad.reshape((grad.shape[-4],) + grad.shape[-2:])


class SumAll:
    def __init__(self, net, array):
        self.net, self.array = net, array
        self.left = list(reversed(net.order))
        self.other = None

    def step(self):
        if self.other is not None:
            self.array = self.array + self.net.clock.at(self.other)
            self.other = None
        if self.left:
            self.other = self.net.swap(self.array, self.left.pop(0))

    def result(self):
        while self.left or self.other is not None:
            self.step()
        return self.array


class EightShards:
    a_moves = [(2 * z, 2 * z + 1) for z in range(4)] + [(7, 6)]
    b_moves = [(2, 3), (3, 2), (4, 5), (5, 4), (6, 7), (7, 6)]
    c_moves = [(4, 5), (5, 4), (6, 7), (7, 6)]

    def __init__(self, clock, parts, shards):
        self.clock, self.parts, self.shards = clock, parts, shards
        self.shard = lax.axis_index("fsdp")
        self.z, self.y = self.shard // 2, self.shard % 2
        self.top, self.odd = self.z == 3, self.y == 1

    def move(self, array, moves):
        pairs = [(d * self.shards + a, d * self.shards + b) for d in range(self.parts) for a, b in moves]
        return lax.ppermute(self.clock.at(array), AXES, pairs)

    def up(self, array, lowest):
        return self.move(array, [(2 * z + y, 2 * z + y + 2) for z in range(lowest, 3) for y in range(2)])

    def down(self, array, lowest):
        return self.move(array, [(2 * z + y + 2, 2 * z + y) for z in range(lowest, 3) for y in range(2)])

    def slot_ids(self):
        shard, z, y = self.shard, self.z, self.y
        none = jnp.int32(-1)
        return jnp.stack(
            [
                shard,
                jnp.where(y == 1, shard - 1, jnp.where(z == 3, 5, none)),
                jnp.where(z == 3, 3 - y, jnp.where(z >= 1, 2 * (z - 1) + 1 - y, none)),
                jnp.where(z >= 2, shard - 4, none),
                jnp.where(z >= 2, 1 - y, none),
                jnp.where(z == 3, y, jnp.where(z >= 1, shard - 2, none)),
            ]
        ).astype(jnp.int32)

    def spread(self, own):
        at = self.clock.at
        up1 = self.up(own, 0)
        yield
        up1 = at(up1)
        up2 = self.up(up1, 1)
        a = self.move(jnp.where(self.top & self.odd, up1, own), self.a_moves)
        yield
        up2, a = at(up2, a)
        up3 = self.up(up2, 2)
        b = self.move(jnp.where(self.top, up2, up1), self.b_moves)
        yield
        up3, b = at(up3, b)
        c = self.move(jnp.where(self.top, up3, up2), self.c_moves)
        yield
        last = jnp.where(self.top, up3, up1)
        c = at(c)
        yield [own, a, b, up2, c, last]

    pairs = 2

    def collect(self, grads):
        at = self.clock.at
        own, a, b, up2, c, last = grads
        back = lambda moves: [(t, s) for s, t in moves]
        wide = lambda array: array.astype(F32)
        from_c, from_b = self.move(c, back(self.c_moves)), self.move(b, back(self.b_moves))
        yield
        from_c = wide(at(from_c))
        first = self.down((wide(last) + from_c).astype(BF16), 2)
        from_a = self.move(a, back(self.a_moves))
        yield
        from_b, first = at(from_b, first)
        from_b, first = wide(from_b), wide(first)
        second = self.down((wide(up2) + jnp.where(self.top, from_b, from_c + first)).astype(BF16), 1)
        yield
        from_a, second = at(from_a, second)
        from_a, second = wide(from_a), wide(second)
        late = self.top & self.odd
        level = jnp.where(self.top, jnp.where(self.odd, from_a, 0.0), wide(last) + from_b + second)
        third = self.down(level.astype(BF16), 0)
        yield
        third = wide(at(third))
        yield (wide(own) + jnp.where(late, 0.0, from_a) + third).astype(BF16)


class AnyShards:
    def __init__(self, clock, parts, shards):
        self.shards = shards
        self.pairs = shards
        self.shard = lax.axis_index("fsdp")

    def slot_ids(self):
        return (self.shard - jnp.arange(self.shards)).astype(jnp.int32)

    def pick(self, array, s):
        return lax.dynamic_index_in_dim(array, (self.shard - s) % self.shards, 0, keepdims=False)

    def spread(self, own):
        every = lax.all_gather(own, "fsdp", axis=0, tiled=False)
        yield from (None,) * 4
        yield [own] + [self.pick(every, s) for s in range(1, self.shards)]

    def collect(self, grads):
        every = jnp.stack(grads)
        order = jnp.stack([self.pick(every, s) for s in range(self.shards)])
        yield from (None,) * 4
        yield lax.psum_scatter(order, "fsdp", scatter_dimension=0, tiled=False)


def shards(
    hidden_in, segment, position, selected, gain_attn, gain_ffn, router,
    w_query, key_weight, value_weight, w_output, w_gate, w_up, w_down, cotangent,
):
    groups, rows, model = hidden_in.shape
    tokens = groups * rows
    parts, shard_count = lax.axis_size("dp"), lax.axis_size("fsdp")
    columns = model // parts
    width = -(-columns // TILE) * TILE
    fill = lambda array: jnp.pad(array, ((0, 0),) * (array.ndim - 1) + ((0, width - columns),))
    clock = Clock()
    at = clock.at
    net = Net(clock, parts, shard_count)
    my_part, my_shard = lax.axis_index("dp"), lax.axis_index("fsdp")
    ring = (EightShards if shard_count == 8 else AnyShards)(clock, parts, shard_count)

    small = fill(jnp.concatenate([key_weight.T, value_weight.T], axis=0))
    medium = fill(jnp.concatenate([w_query.T, w_output], axis=0))
    kv_rows, q_rows = key_weight.shape[1], w_query.shape[1]
    gate_rows, up_rows = w_gate.T, w_up.T
    chunk_rows = w_down.shape[0] // 2
    large = [w[c * chunk_rows : (c + 1) * chunk_rows] for c in range(2) for w in (gate_rows, up_rows, w_down)]
    large = fill(jnp.concatenate(large, axis=0))

    def heads_of(array, count):
        return array.reshape(parts, count, HEAD_DIM, width)

    def split(array):
        return fill(jnp.transpose(array.reshape(tokens, parts, columns), (1, 0, 2)))

    half = HEAD_DIM // 2
    frequency = THETA ** (-(jnp.arange(half).astype(F32) * 2.0) / HEAD_DIM)
    angles = position.reshape(tokens).astype(F32)[:, None] * frequency[None, :]
    cos, sin = jnp.cos(angles), jnp.sin(angles)
    zero, one = jnp.zeros_like(cos), jnp.ones_like(cos)
    table = lambda *four: jnp.concatenate(four, axis=1)
    kv_tables = (table(cos, cos, one, one), table(-sin, zero, zero, zero), table(zero, sin, zero, zero))
    shrink = HEAD_DIM**-0.5
    q_tables = tuple(
        shrink * t
        for t in (table(cos, cos, zero, zero), table(-sin, zero, zero, zero), table(zero, sin, zero, zero))
    )
    seg_rows = segment.astype(F32).reshape(groups, 1, rows)
    tags = jnp.where(selected == 1, segment, -1).astype(BF16).reshape(groups, rows // TILE, TILE)
    tags = jnp.pad(tags, ((0, 0), (0, 16 - rows // TILE), (0, 0)))
    hid4, cot4 = split(hidden_in), split(cotangent)
    vector = lambda v: fill(v.astype(F32).reshape(parts, 1, columns))
    gain_one, gain_two, route = vector(gain_attn), vector(gain_ffn), vector(router)
    chosen = selected.reshape(tokens, 1).astype(F32)

    small_gather = Gather(net, small)
    medium_all = lax.all_gather(medium, AXES, axis=0, tiled=False)
    small_gather.step()
    small_gather.step()
    small_gather.step()
    xn4, s1, fg4, mix, slope = first_norm(hid4, cot4, gain_one, route, chosen)
    xn4 = at(xn4)
    small_gather.step()
    small_all = small_gather.finish()
    keys = heads_of(small_all[:, :, :kv_rows], KV_HEADS)
    values = heads_of(small_all[:, :, kv_rows:], KV_HEADS)
    wkv = jnp.concatenate([keys, values], axis=2).reshape(parts, KV_HEADS * TILE, width)
    spread = ring.spread(kv_project(groups, xn4, wkv, kv_tables, tags))
    next(spread)
    large_all = lax.all_gather(clock.after(large), AXES, axis=0, tiled=False)
    next(spread)
    queries = heads_of(medium_all[:, :q_rows], QUERY_HEADS)
    wq_pad = jnp.concatenate([queries, queries[:, :, half:], queries[:, :, :half]], axis=2)
    wq_pad = wq_pad.reshape(parts, QUERY_HEADS * TILE, width)
    q = at(q_project(xn4, wq_pad, q_tables[0], q_tables[1] + q_tables[2], groups))
    next(spread)
    next(spread)
    slot_ids = ring.slot_ids()
    kvs = next(spread)
    o, lse = at(*attention_forward(slot_ids, q, seg_rows, kvs, ring.pairs))
    outputs = heads_of(medium_all[:, q_rows:], QUERY_HEADS)
    wo_pad = jnp.concatenate([jnp.zeros_like(outputs), outputs], axis=2)
    wo_pad = wo_pad.reshape(parts, QUERY_HEADS * TILE, width)
    mid4, x24, s2 = out_project(o, wo_pad, hid4, gain_two)
    x24 = at(x24)

    ffn_all = large_all.reshape((parts, shard_count // 2, 2) + large.shape)
    bits = net.order[:-1][::-1]
    parts_bits = [bit for bit in bits if bit > net.core]
    shards_bits = [bit for bit in bits if bit < net.core]
    out_a, xg_a, keep_a, send_a = ffn(my_part, my_shard, 0, 3 * chunk_rows, x24, fg4, ffn_all, False)
    scatter_a = Scatter(net, keep_a, send_a, 1, 3 * chunk_rows, parts_bits + shards_bits)
    out_b, xg_b, keep_b, send_b = ffn(my_part, my_shard, 1, 3 * chunk_rows, x24, fg4, ffn_all, True)
    scatter_b = Scatter(net, keep_b, send_b, 1, 3 * chunk_rows, shards_bits[:1] + parts_bits + shards_bits[1:])
    scatter_a.step()
    out_b = at(out_b)
    hidden_out, part4, ag4, router_sum, gain_two_sum = middle_step(
        mid4, hid4, cot4, (out_a, out_b), (xg_a, xg_b), mix, slope, s2, gain_two, route
    )
    ag4 = at(ag4)
    scatter_b.step()
    do = at(out_back(ag4, wo_pad))
    dq, dkvs = attention_backward(slot_ids, q, do, o, lse, seg_rows, q_tables, kvs, ring.pairs)
    dq = at(dq)
    scatter_b.land()
    scatter_a.land()
    collect = ring.collect(dkvs)
    next(collect)
    scatter_b.send()
    keep_qo, send_qo, xg_q = qo_back(my_part, dq, xn4, wq_pad, o, ag4)
    xg_q = at(xg_q)
    next(collect)
    scatter_qo = Scatter(net, keep_qo, send_qo, 2, q_rows)
    next(collect)
    scatter_a.send()
    scatter_qo.step()
    next(collect)
    scatter_b.step()
    scatter_qo.step()
    dkv = next(collect).reshape(tokens, KV_HEADS * TILE)
    kvb, keep_kv, send_kv = kv_back(my_part, dkv, kv_tables, xn4)

    def by_kind(array):
        tiles = array.reshape(array.shape[0], KV_HEADS, 2, HEAD_DIM, width)
        return jnp.transpose(tiles, (0, 2, 1, 3, 4))

    scatter_kv = Scatter(net, by_kind(keep_kv), by_kind(send_kv), 2, kv_rows)
    kvb = at(kvb)
    grad_in, gain_one_sum = final_step(xg_q, kvb, wkv, hid4, part4, s1, gain_one)
    scatter_kv.step()
    scatter_b.step()
    scatter_a.step()
    scatter_qo.step()
    sums = SumAll(net, jnp.stack([gain_one_sum, gain_two_sum, router_sum]))
    sums.step()
    scatter_kv.step()
    sums.step()
    scatter_a.step()
    scatter_qo.step()
    scatter_kv.step()
    sums.step()
    scatter_b.land()
    scatter_kv.step()
    sums.step()
    scatter_a.land()
    scatter_qo.land()
    for _ in range(net.bits):
        scatter_kv.step()
        sums.step()
    kv_grad = scatter_kv.result()
    sums = sums.result()[..., :columns].reshape(3, model)
    kv_grad = kv_grad[..., :columns]
    q_grad, o_grad = scatter_qo.result()[..., :columns]
    grads = [s.result().reshape(3, chunk_rows, width)[..., :columns] for s in (scatter_a, scatter_b)]
    gate_grad, up_grad, down_grad = jnp.concatenate(grads, axis=1)
    sums = sums + clock.token[0, 0]
    return (
        hidden_out.reshape(groups, rows, model),
        grad_in.reshape(groups, rows, model),
        sums[0],
        sums[1],
        sums[2],
        q_grad.T,
        kv_grad[0].T,
        kv_grad[1].T,
        o_grad,
        gate_grad.T,
        up_grad.T,
        down_grad,
    )


def solution(mesh):
    tokens = P("dp", "fsdp")
    inner_first = P("fsdp", "dp")
    return jax.shard_map(
        shards,
        mesh=mesh,
        in_specs=(P("dp", "fsdp", None),) + (tokens,) * 3 + (P(),) * 3
        + (tokens,) * 3 + (inner_first,) + (tokens,) * 2 + (inner_first, P("dp", "fsdp", None)),
        out_specs=(P("dp", "fsdp", None),) * 2 + (P(),) * 3
        + (tokens,) * 3 + (inner_first,) + (tokens,) * 2 + (inner_first,),
        check_vma=False,
    )
```

```python
import functools

import jax
import jax.numpy as jnp
from jax import lax
from jax.experimental import pallas as pl
from jax.experimental.pallas import tpu as pltpu
from jax.sharding import PartitionSpec as P

MODEL_DIM = 960
QUERY_HEADS = 15
KV_HEADS = 5
SHARE = QUERY_HEADS // KV_HEADS
HEAD_DIM = 64
TILE = 128
PROMPT = 1024
LONGEST = 192
EPSILON = 1e-05
THETA = 10000.0
MINUS_LARGE = -1e30
AXES = ("dp", "fsdp")
F32 = jnp.float32
BF16 = jnp.bfloat16
VMEM_BYTES = 60 * 1024 * 1024

NT = (((1,), (1,)), ((), ()))
NN = (((1,), (0,)), ((), ()))
TN = (((0,), (0,)), ((), ()))


def dot(a, b, dims=NN):
    return lax.dot_general(a, b, dims, preferred_element_type=F32)


def params(steps=0):
    return pltpu.CompilerParams(
        vmem_limit_bytes=VMEM_BYTES,
        dimension_semantics=("arbitrary",) * steps if steps else None,
    )


def cost(flops, moved, exps=0):
    return pl.CostEstimate(flops=int(flops), bytes_accessed=int(moved), transcendentals=int(exps))


def whole(shape):
    zeros = (0,) * len(shape)
    return pl.BlockSpec(shape, lambda *_: zeros)


def side_by_side(ref):
    return jnp.concatenate([ref[d] for d in range(ref.shape[0])], axis=1)


def by_distance(ref, my_part):
    parts = ref.shape[0]
    return jnp.concatenate([ref[pl.ds(my_part ^ e, 1)].reshape(ref.shape[1:]) for e in range(parts)], axis=1)


def whole_rows(pieces):
    return jnp.concatenate([piece[:, : MODEL_DIM // len(pieces)] for piece in pieces], axis=1)


def norm_kernel(hid_ref, cot_ref, gain_ref, router_ref, sel_ref, xn_ref, s1_ref, fg_ref, mix_ref, slope_ref):
    parts, _, width = hid_ref.shape
    square = 0.0
    logit = 0.0
    for d in range(parts):
        x = hid_ref[d].astype(F32)
        square = square + jnp.sum(x * x, axis=-1, keepdims=True)
        logit = logit + jnp.sum(x * router_ref[d], axis=-1, keepdims=True)
    scale = lax.rsqrt(square / MODEL_DIM + EPSILON)
    chance = 1.0 / (1.0 + jnp.exp(-logit))
    mix = sel_ref[...] * chance
    s1_ref[...] = scale
    mix_ref[...] = mix
    slope_ref[...] = mix * (1.0 - chance)
    for d in range(parts):
        x = hid_ref[d].astype(F32)
        xn_ref[d] = (x * scale * gain_ref[d]).astype(BF16)
        fg_ref[d] = (cot_ref[d].astype(F32) * mix).astype(BF16)


def first_norm(hid4, cot4, gain, router, chosen):
    parts, tokens, width = hid4.shape
    rows = 128
    block = pl.BlockSpec((parts, rows, width), lambda i: (0, i, 0))
    column = pl.BlockSpec((rows, 1), lambda i: (i, 0))
    vector = whole((parts, 1, width))
    return pl.pallas_call(
        norm_kernel,
        grid=(tokens // rows,),
        in_specs=[block, block, vector, vector, column],
        out_specs=[block, column, block, column, column],
        out_shape=[
            jax.ShapeDtypeStruct(hid4.shape, BF16),
            jax.ShapeDtypeStruct((tokens, 1), F32),
            jax.ShapeDtypeStruct(hid4.shape, BF16),
            jax.ShapeDtypeStruct((tokens, 1), F32),
            jax.ShapeDtypeStruct((tokens, 1), F32),
        ],
        compiler_params=params(1),
        cost_estimate=cost(tokens * 960 * 10, tokens * 960 * 8),
        name="first_norm",
    )(hid4, cot4, gain, router, chosen)


def kv_kernel(xn_ref, w_ref, cos_ref, sin1_ref, sin2_ref, tag_ref, out_ref):
    rows = xn_ref.shape[1]
    total = dot(side_by_side(xn_ref), side_by_side(w_ref), NT)
    for h in range(KV_HEADS):
        u = total[:, h * TILE : (h + 1) * TILE]
        turned = (
            u * cos_ref[...]
            + pltpu.roll(u, TILE - HEAD_DIM // 2, 1) * sin1_ref[...]
            + pltpu.roll(u, HEAD_DIM // 2, 1) * sin2_ref[...]
        )
        out_ref[:rows, h * TILE : (h + 1) * TILE] = turned.astype(BF16)
        out_ref[rows:, h * TILE : (h + 1) * TILE] = tag_ref[0]


def kv_project(groups, xn4, wkv, tables, tags):
    parts, tokens, width = xn4.shape
    rows = tokens // groups
    table = pl.BlockSpec((rows, TILE), lambda g: (g, 0))
    return pl.pallas_call(
        kv_kernel,
        grid=(groups,),
        in_specs=[
            pl.BlockSpec((parts, rows, width), lambda g: (0, g, 0)),
            whole(wkv.shape),
            table,
            table,
            table,
            pl.BlockSpec((1, 16, TILE), lambda g: (g, 0, 0)),
        ],
        out_specs=pl.BlockSpec((None, rows + 16, KV_HEADS * TILE), lambda g: (g, 0, 0)),
        out_shape=jax.ShapeDtypeStruct((groups, rows + 16, KV_HEADS * TILE), BF16),
        compiler_params=params(1),
        cost_estimate=cost(2 * tokens * 960 * 640, 3 * tokens * 960 * 2),
        name="kv_project",
    )(xn4, wkv, *tables, tags)


def q_kernel(xn_ref, w_ref, cos_ref, sin_ref, out_ref):
    total = dot(side_by_side(xn_ref), side_by_side(w_ref), NT)
    for h in range(QUERY_HEADS):
        u = total[:, h * TILE : (h + 1) * TILE]
        turned = u * cos_ref[...] + pltpu.roll(u, HEAD_DIM, 1) * sin_ref[...]
        out_ref[:, h * TILE : (h + 1) * TILE] = turned.astype(BF16)


def q_project(xn4, wq_pad, cos_q, sin_q, groups):
    parts, tokens, width = xn4.shape
    rows = tokens // groups
    table = pl.BlockSpec((rows, TILE), lambda g: (g, 0))
    return pl.pallas_call(
        q_kernel,
        grid=(groups,),
        in_specs=[
            pl.BlockSpec((parts, rows, width), lambda g: (0, g, 0)),
            whole(wq_pad.shape),
            table,
            table,
        ],
        out_specs=pl.BlockSpec((rows, QUERY_HEADS * TILE), lambda g: (g, 0)),
        out_shape=jax.ShapeDtypeStruct((tokens, QUERY_HEADS * TILE), BF16),
        compiler_params=params(1),
        cost_estimate=cost(2 * tokens * 960 * 1920, 6 * tokens * 960 * 2),
        name="q_project",
    )(xn4, wq_pad, cos_q, sin_q)


def slot_needed(slot_ref, s, rows):
    own = slot_ref[0]
    block = slot_ref[s]
    prompt_blocks = PROMPT // rows
    reach = -(-(LONGEST - 1) // rows)
    near = (block < prompt_blocks) | (block >= own - reach)
    return (block >= 0) & (block <= own) & near


def fill_bias(slot_ref, seg_ref, kv_refs, pair_ref, key_ref, turned):
    pairs, rows, _ = pair_ref.shape
    for s, kv_ref in enumerate(kv_refs):
        needed = slot_needed(slot_ref, s, rows)
        for i in range(rows // TILE):
            here = slice(i * TILE, (i + 1) * TILE)
            tag_row = kv_ref[rows : rows + 16, 0:TILE].astype(F32)[i : i + 1]
            tag = jnp.where(needed, jnp.broadcast_to(tag_row, (TILE, TILE)).T, -1.0)
            if s >= pairs:
                lane = lax.broadcasted_iota(jnp.int32, (TILE, TILE), 1)
                hidden = (tag != 0.0) & (lane == HEAD_DIM)
                key_ref[s - pairs, here, :] = jnp.where(hidden, MINUS_LARGE, 0.0).astype(BF16)
                continue
            for j in range(rows // TILE):
                there = slice(j * TILE, (j + 1) * TILE)
                allowed = (tag == 0.0) | (tag == seg_ref[0, :, there])
                if s == 0:
                    key_row = i * TILE + lax.broadcasted_iota(jnp.int32, (TILE, TILE), 0)
                    query_row = j * TILE + lax.broadcasted_iota(jnp.int32, (TILE, TILE), 1)
                    allowed = (allowed & (key_row <= query_row)) | (key_row == query_row)
                bias = jnp.where(allowed, 0.0, MINUS_LARGE)
                if turned:
                    pair_ref[s, there, here] = bias.T
                else:
                    pair_ref[s, here, there] = bias


def lanes_of(dtype, shape, test):
    return jnp.where(test(lax.broadcasted_iota(jnp.int32, shape, 1)), 1.0, 0.0).astype(dtype)


def load_keys(kv_refs, pair_ref, key_ref):
    pairs, rows, _ = pair_ref.shape
    kvs = [ref[:rows, :] for ref in kv_refs]
    other = lanes_of(BF16, (1, TILE), lambda lane: lane != HEAD_DIM)
    marked = [kv * other + (key_ref[s - pairs] if s >= pairs else 0.0) for s, kv in enumerate(kvs)]
    return jnp.concatenate(kvs, axis=0), jnp.concatenate([m.astype(BF16) for m in marked], axis=0)


def mark(q):
    return q + lanes_of(BF16, (1, TILE), lambda lane: lane == HEAD_DIM)


def forward_kernel(slots, slot_ref, q_ref, seg_ref, *refs):
    kv_refs = refs[:slots]
    o_ref, lse_ref, pair_ref, key_ref = refs[slots:]
    rows = q_ref.shape[0]
    pairs = pair_ref.shape[0]

    @pl.when(pl.program_id(1) == 0)
    def _():
        fill_bias(slot_ref, seg_ref, kv_refs, pair_ref, key_ref, True)

    kvs, marked = load_keys(kv_refs, pair_ref, key_ref)
    low = lanes_of(BF16, (1, TILE), lambda lane: lane < HEAD_DIM)
    counted = kvs * (1.0 - low) + low
    lane = lax.broadcasted_iota(jnp.int32, (rows, TILE), 1)
    weights, peaks = [], []
    for j in range(SHARE):
        here = slice(j * TILE, (j + 1) * TILE)
        raw = dot(mark(q_ref[:, here]), marked, NT)
        parts = [raw[:, s * rows : (s + 1) * rows] + pair_ref[s] for s in range(pairs)]
        if slots > pairs:
            parts.append(raw[:, pairs * rows :])
        score = jnp.concatenate(parts, axis=1)
        peak = score[:, :TILE]
        for t in range(1, score.shape[1] // TILE):
            peak = jnp.maximum(peak, score[:, t * TILE : (t + 1) * TILE])
        peak = jnp.max(peak, axis=1, keepdims=True)
        peaks.append(peak)
        weights.append(jnp.exp(score - peak).astype(BF16))
    accs = dot(jnp.concatenate(weights, axis=0), counted)
    for j, peak in enumerate(peaks):
        here = slice(j * TILE, (j + 1) * TILE)
        acc = accs[j * rows : (j + 1) * rows]
        total = jnp.where(lane < HEAD_DIM, acc, 1.0)
        mixed = acc * pltpu.roll(1.0 / total, HEAD_DIM, 1)
        o_ref[:, here] = jnp.where(lane >= HEAD_DIM, mixed, 0.0).astype(BF16)
        lse_ref[0, 0, :, j * rows : (j + 1) * rows] = (peak + jnp.log(total)).T[0:1]


def attention_forward(slot_ids, q, seg, kvs, pairs):
    groups, _, rows = seg.shape
    slots = len(kvs)
    tokens = groups * rows
    wide = SHARE * rows
    heads = pl.BlockSpec((rows, SHARE * TILE), lambda g, h, _: (g, h))
    return pl.pallas_call(
        functools.partial(forward_kernel, slots),
        grid_spec=pltpu.PrefetchScalarGridSpec(
            num_scalar_prefetch=1,
            grid=(groups, KV_HEADS),
            in_specs=[heads, pl.BlockSpec((1, 1, rows), lambda g, h, _: (g, 0, 0))]
            + [pl.BlockSpec((None, rows + 16, TILE), lambda g, h, _: (g, 0, h))] * slots,
            out_specs=[heads, pl.BlockSpec((1, 1, 1, wide), lambda g, h, _: (g, h, 0, 0))],
            scratch_shapes=[
                pltpu.VMEM((pairs, rows, rows), F32),
                pltpu.VMEM((max(slots - pairs, 1), rows, TILE), BF16),
            ],
        ),
        out_shape=[
            jax.ShapeDtypeStruct(q.shape, BF16),
            jax.ShapeDtypeStruct((groups, KV_HEADS, 1, wide), F32),
        ],
        compiler_params=params(2),
        cost_estimate=cost(2 * 15 * tokens * 1536 * 256, 8 * tokens * 960 * 2, 15 * tokens * 1536),
        name="attention_forward",
    )(slot_ids, q, seg, *kvs)


def backward_kernel(slots, slot_ref, q_ref, do_ref, o_ref, lse_ref, seg_ref, cos_ref, sin1_ref, sin2_ref, *refs):
    kv_refs = refs[:slots]
    dq_ref = refs[slots]
    dkv_refs = refs[slots + 1 : -2]
    pair_ref, key_ref = refs[-2:]
    rows = q_ref.shape[0]

    @pl.when(pl.program_id(1) == 0)
    def _():
        fill_bias(slot_ref, seg_ref, kv_refs, pair_ref, key_ref, False)

    kvs, marked = load_keys(kv_refs, pair_ref, key_ref)
    pairs = pair_ref.shape[0]
    left, right = [], []
    for j in range(SHARE):
        here = slice(j * TILE, (j + 1) * TILE)
        q, do = q_ref[:, here], do_ref[:, here]
        delta = jnp.sum((do.astype(F32) * o_ref[:, here].astype(F32)).T, axis=0, keepdims=True)
        raw = dot(marked, mark(q), NT)
        parts = [raw[s * rows : (s + 1) * rows] + pair_ref[s] for s in range(pairs)]
        if slots > pairs:
            parts.append(raw[pairs * rows :])
        prob = jnp.exp(jnp.concatenate(parts, axis=0) - lse_ref[0, 0, :, j * rows : (j + 1) * rows])
        slope = (prob * (dot(kvs, do, NT) - delta)).astype(BF16)
        left += [slope, prob.astype(BF16)]
        right += [q, do]
        part = dot(slope, kvs, TN)
        back = (
            part * cos_ref[...]
            - pltpu.roll(part, TILE - HEAD_DIM // 2, 1) * sin1_ref[...]
            - pltpu.roll(part, HEAD_DIM // 2, 1) * sin2_ref[...]
        )
        dq_ref[:, here] = back.astype(BF16)
    right = jnp.concatenate(right, axis=0)
    for s in range(slots):
        band = jnp.concatenate([part[s * rows : (s + 1) * rows] for part in left], axis=1)
        dkv_refs[s][...] = dot(band, right).astype(BF16)


def attention_backward(slot_ids, q, do, o, lse, seg, tables, kvs, pairs):
    groups, _, rows = seg.shape
    slots = len(kvs)
    heads = pl.BlockSpec((rows, SHARE * TILE), lambda g, h, _: (g, h))
    seg_spec = pl.BlockSpec((1, 1, rows), lambda g, h, _: (g, 0, 0))
    kv_spec = pl.BlockSpec((None, rows + 16, TILE), lambda g, h, _: (g, 0, h))
    lse_spec = pl.BlockSpec((1, 1, 1, SHARE * rows), lambda g, h, _: (g, h, 0, 0))
    table = pl.BlockSpec((rows, TILE), lambda g, h, _: (g, 0))
    grad = pl.BlockSpec((None, rows, TILE), lambda g, h, _: (g, 0, h))
    tokens = groups * rows
    out = pl.pallas_call(
        functools.partial(backward_kernel, slots),
        grid_spec=pltpu.PrefetchScalarGridSpec(
            num_scalar_prefetch=1,
            grid=(groups, KV_HEADS),
            in_specs=[heads, heads, heads, lse_spec, seg_spec, table, table, table] + [kv_spec] * slots,
            out_specs=[heads] + [grad] * slots,
            scratch_shapes=[
                pltpu.VMEM((pairs, rows, rows), F32),
                pltpu.VMEM((max(slots - pairs, 1), rows, TILE), BF16),
            ],
        ),
        out_shape=[jax.ShapeDtypeStruct(q.shape, BF16)]
        + [jax.ShapeDtypeStruct((groups, rows, KV_HEADS * TILE), BF16)] * slots,
        compiler_params=params(2),
        cost_estimate=cost(5 * 15 * tokens * 1536 * 256, 16 * tokens * 960 * 2, 15 * tokens * 1536),
        name="attention_backward",
    )(slot_ids, q, do, o, lse, seg, *tables, *kvs)
    return out[0], out[1:]


def out_kernel(o_ref, w_ref, hid_ref, gain_ref, mid_ref, x2_ref, s2_ref):
    parts, _, width = hid_ref.shape
    out = dot(o_ref[...], side_by_side(w_ref))
    square = 0.0
    for d in range(parts):
        middle = hid_ref[d].astype(F32) + out[:, d * width : (d + 1) * width]
        mid_ref[d] = middle
        square = square + jnp.sum(middle * middle, axis=-1, keepdims=True)
    scale = lax.rsqrt(square / MODEL_DIM + EPSILON)
    s2_ref[...] = scale
    for d in range(parts):
        x2_ref[d] = (mid_ref[d] * scale * gain_ref[d]).astype(BF16)


def out_project(o, wo_pad, hid4, gain):
    parts, tokens, width = hid4.shape
    rows = min(512, tokens)
    block = pl.BlockSpec((parts, rows, width), lambda i: (0, i, 0))
    column = pl.BlockSpec((rows, 1), lambda i: (i, 0))
    return pl.pallas_call(
        out_kernel,
        grid=(tokens // rows,),
        in_specs=[
            pl.BlockSpec((rows, o.shape[1]), lambda i: (i, 0)),
            whole(wo_pad.shape),
            block,
            whole((parts, 1, width)),
        ],
        out_specs=[block, block, column],
        out_shape=[
            jax.ShapeDtypeStruct(hid4.shape, F32),
            jax.ShapeDtypeStruct(hid4.shape, BF16),
            jax.ShapeDtypeStruct((tokens, 1), F32),
        ],
        compiler_params=params(1),
        cost_estimate=cost(2 * tokens * 960 * 1920, 8 * tokens * 960 * 2),
        name="out_project",
    )(o, wo_pad, hid4, gain)


def ffn_kernel(meta_ref, x_ref, fg_ref, w_ref, out_ref, xg_ref, keep_ref, send_ref):
    parts, count, rows3, width = w_ref.shape
    rows = rows3 // 3
    my_part, my_place = meta_ref[0], meta_ref[2]
    bits = count.bit_length() - 1
    turn_bits = [sum((i >> b & 1) << (bits - 1 - b) for b in range(bits)) for i in range(count)]

    def weight(which):
        band = slice(which * rows, (which + 1) * rows)
        block = lambda d, i: w_ref[d, pl.ds(my_place ^ i, 1), band, :].reshape(rows, width)
        lines = [jnp.concatenate([block(d, i) for d in range(parts)], axis=1) for i in turn_bits]
        return jnp.concatenate(lines, axis=0)

    w_gate, w_up, w_down = (weight(which) for which in range(3))
    x, fg = side_by_side(x_ref), side_by_side(fg_ref)
    gate = dot(x, w_gate, NT)
    up = dot(x, w_up, NT)
    hidden_grad = dot(fg, w_down, NT)
    chance = 1.0 / (1.0 + jnp.exp(-gate))
    silu = gate * chance
    hidden = (silu * up).astype(BF16)
    up_grad = (hidden_grad * silu).astype(BF16)
    gate_grad = (hidden_grad * up * chance * (1.0 + gate * (1.0 - chance))).astype(BF16)

    first = pl.program_id(0) == 0
    out = dot(hidden, w_down)
    back = dot(jnp.concatenate([gate_grad, up_grad], axis=1), jnp.concatenate([w_gate, w_up], axis=0))
    for d in range(parts):
        here = slice(d * width, (d + 1) * width)

        @pl.when(first)
        def _(d=d, here=here):
            out_ref[d] = out[:, here]
            xg_ref[d] = back[:, here]

        @pl.when(jnp.logical_not(first))
        def _(d=d, here=here):
            out_ref[d] += out[:, here]
            xg_ref[d] += back[:, here]

    x, fg = by_distance(x_ref, my_part), by_distance(fg_ref, my_part)
    for which, left in enumerate((gate_grad, up_grad, hidden)):
        left, right = left.T, fg if which == 2 else x
        for i in range(count):
            grad = dot(left[i * rows : (i + 1) * rows], right).astype(BF16)
            for e in range(parts):
                target = send_ref if e % 2 else keep_ref
                target[e // 2, i, which * rows : (which + 1) * rows, :] = grad[:, e * width : (e + 1) * width]


def ffn(my_part, my_shard, chunk, rows3, x4, fg4, weights, shard_first):
    parts, tokens, width = x4.shape
    half = weights.shape[1]
    block = pl.BlockSpec((parts, half, None, rows3, width), lambda j, m: (0, 0, m[1] ^ j, chunk, 0))
    if shard_first:
        grad_block = pl.BlockSpec((None, parts // 2, half, rows3, width), lambda j, m: (j, 0, 0, 0, 0))
        grad = jax.ShapeDtypeStruct((2, parts // 2, half, rows3, width), BF16)
    else:
        grad_block = pl.BlockSpec((parts // 2, None, half, rows3, width), lambda j, m: (0, j, 0, 0, 0))
        grad = jax.ShapeDtypeStruct((parts // 2, 2, half, rows3, width), BF16)
    meta = jnp.stack([my_part, my_shard % 2, my_shard // 2]).astype(jnp.int32)
    return pl.pallas_call(
        ffn_kernel,
        grid_spec=pltpu.PrefetchScalarGridSpec(
            num_scalar_prefetch=1,
            grid=(2,),
            in_specs=[whole(x4.shape), whole(x4.shape), block],
            out_specs=[whole(x4.shape), whole(x4.shape), grad_block, grad_block],
        ),
        out_shape=[jax.ShapeDtypeStruct(x4.shape, F32)] * 2 + [grad, grad],
        compiler_params=params(1),
        cost_estimate=cost(12 * tokens * 960 * rows3 * half, 8 * tokens * 960 * 2 + 8 * 960 * rows3 * half),
        name="ffn",
    )(meta, x4, fg4, weights)


def middle_kernel(
    mid_ref, hid_ref, cot_ref, out_a_ref, out_b_ref, xg_a_ref, xg_b_ref, mix_ref, slope_ref, s2_ref, gain_ref, router_ref,
    hidden_ref, part_ref, ag_ref, router_grad_ref, gain_grad_ref,
):
    parts, rows, width = mid_ref.shape
    mix = mix_ref[...]
    scale = s2_ref[...]
    inner = 0.0
    mean = 0.0
    rows_out = []
    for d in range(parts):
        middle = mid_ref[d]
        inputs = hid_ref[d].astype(F32)
        branch = (middle - inputs) + (out_a_ref[d] + out_b_ref[d])
        upstream = cot_ref[d].astype(F32)
        inner = inner + jnp.sum(upstream * branch, axis=-1, keepdims=True)
        rows_out.append(inputs + mix * branch)
        mean = mean + jnp.sum((xg_a_ref[d] + xg_b_ref[d]) * gain_ref[d] * middle, axis=-1, keepdims=True)
    hidden_ref[...] = whole_rows(rows_out).astype(BF16)
    logit_grad = slope_ref[...] * inner
    mean = mean / MODEL_DIM * (scale * scale * scale)
    first = pl.program_id(0) == 0
    for d in range(parts):
        middle = mid_ref[d]
        inputs = hid_ref[d].astype(F32)
        upstream = cot_ref[d].astype(F32)
        grad = xg_a_ref[d] + xg_b_ref[d]
        middle_grad = scale * (grad * gain_ref[d]) - middle * mean
        ag_ref[d] = (upstream * mix + middle_grad).astype(BF16)
        part_ref[d] = upstream + logit_grad * router_ref[d] + middle_grad
        router_grad = jnp.sum(logit_grad * inputs, axis=0, keepdims=True)
        gain_grad = jnp.sum(grad * middle * scale, axis=0, keepdims=True)

        @pl.when(first)
        def _(d=d, router_grad=router_grad, gain_grad=gain_grad):
            router_grad_ref[d] = router_grad
            gain_grad_ref[d] = gain_grad

        @pl.when(jnp.logical_not(first))
        def _(d=d, router_grad=router_grad, gain_grad=gain_grad):
            router_grad_ref[d] += router_grad
            gain_grad_ref[d] += gain_grad


def middle_step(mid4, hid4, cot4, outs, grads, mix, slope, s2, gain, router):
    parts, tokens, width = mid4.shape
    rows = 128
    block = pl.BlockSpec((parts, rows, width), lambda i: (0, i, 0))
    column = pl.BlockSpec((rows, 1), lambda i: (i, 0))
    vector = whole((parts, 1, width))
    return pl.pallas_call(
        middle_kernel,
        grid=(tokens // rows,),
        in_specs=[block] * 7 + [column] * 3 + [vector] * 2,
        out_specs=[pl.BlockSpec((rows, MODEL_DIM), lambda i: (i, 0)), block, block, vector, vector],
        out_shape=[
            jax.ShapeDtypeStruct((tokens, MODEL_DIM), BF16),
            jax.ShapeDtypeStruct(mid4.shape, F32),
            jax.ShapeDtypeStruct(mid4.shape, BF16),
            jax.ShapeDtypeStruct((parts, 1, width), F32),
            jax.ShapeDtypeStruct((parts, 1, width), F32),
        ],
        compiler_params=params(1),
        cost_estimate=cost(tokens * 960 * 30, tokens * 960 * 36),
        name="middle_step",
    )(mid4, hid4, cot4, *outs, *grads, mix, slope, s2, gain, router)


def compact(tile_major, upper):
    count = tile_major.shape[0] // TILE
    start = HEAD_DIM if upper else 0
    return jnp.concatenate(
        [tile_major[h * TILE + start : h * TILE + start + HEAD_DIM] for h in range(count)], axis=0
    )


def out_back_kernel(ag_ref, w_ref, do_ref):
    do_ref[...] = dot(side_by_side(ag_ref), side_by_side(w_ref), NT).astype(BF16)


def out_back(ag4, wo_pad):
    parts, tokens, width = ag4.shape
    rows = min(512, tokens)
    return pl.pallas_call(
        out_back_kernel,
        grid=(tokens // rows,),
        in_specs=[pl.BlockSpec((parts, rows, width), lambda i: (0, i, 0)), whole(wo_pad.shape)],
        out_specs=pl.BlockSpec((rows, wo_pad.shape[1]), lambda i: (i, 0)),
        out_shape=jax.ShapeDtypeStruct((tokens, wo_pad.shape[1]), BF16),
        compiler_params=params(1),
        cost_estimate=cost(2 * tokens * 960 * 1920, 6 * tokens * 960 * 2),
        name="out_back",
    )(ag4, wo_pad)


def part_grads(left, ref, my_part, targets):
    parts, _, width = ref.shape
    right = by_distance(ref, my_part)
    rows = left.shape[0]
    step = rows // 4
    for r in range(0, rows, step):
        grad = dot(left[r : r + step], right).astype(BF16)
        for e in range(parts):
            targets[e % 2][e // 2, r : r + step] = grad[:, e * width : (e + 1) * width]


def qo_back_kernel(meta_ref, dq_ref, xn_ref, w_ref, o_ref, ag_ref, keep_ref, send_ref, xg_ref):
    parts, _, width = xn_ref.shape
    sides = ((compact(dq_ref[...].T, False), xn_ref), (compact(o_ref[...].T, True), ag_ref))
    for i, (left, ref) in enumerate(sides):
        part_grads(left, ref, meta_ref[0], (keep_ref.at[:, i], send_ref.at[:, i]))
    back = dot(dq_ref[...], side_by_side(w_ref))
    for d in range(parts):
        xg_ref[d] = back[:, d * width : (d + 1) * width]


def qo_back(my_part, dq, xn4, wq_pad, o, ag4):
    parts, tokens, width = xn4.shape
    grad = jax.ShapeDtypeStruct((parts // 2, 2, QUERY_HEADS * HEAD_DIM, width), BF16)
    return pl.pallas_call(
        qo_back_kernel,
        grid_spec=pltpu.PrefetchScalarGridSpec(
            num_scalar_prefetch=1,
            grid=(1,),
            in_specs=[whole(a.shape) for a in (dq, xn4, wq_pad, o, ag4)],
            out_specs=[whole(grad.shape), whole(grad.shape), whole(xn4.shape)],
        ),
        out_shape=[grad, grad, jax.ShapeDtypeStruct(xn4.shape, F32)],
        compiler_params=params(1),
        cost_estimate=cost(2 * tokens * 960 * 3840, 14 * tokens * 960 * 2),
        name="qo_back",
    )(my_part.reshape(1), dq, xn4, wq_pad, o, ag4)


def kv_back_kernel(meta_ref, dkv_ref, cos_ref, sin1_ref, sin2_ref, xn_ref, back_ref, keep_ref, send_ref):
    for h in range(KV_HEADS):
        u = dkv_ref[:, h * TILE : (h + 1) * TILE].astype(F32)
        back = (
            u * cos_ref[...]
            - pltpu.roll(u, TILE - HEAD_DIM // 2, 1) * sin1_ref[...]
            - pltpu.roll(u, HEAD_DIM // 2, 1) * sin2_ref[...]
        )
        back_ref[:, h * TILE : (h + 1) * TILE] = back.astype(BF16)
    part_grads(back_ref[...].T, xn_ref, meta_ref[0], (keep_ref, send_ref))


def kv_back(my_part, dkv, tables, xn4):
    parts, tokens, width = xn4.shape
    grad = jax.ShapeDtypeStruct((parts // 2, KV_HEADS * TILE, width), BF16)
    table = whole((tokens, TILE))
    return pl.pallas_call(
        kv_back_kernel,
        grid_spec=pltpu.PrefetchScalarGridSpec(
            num_scalar_prefetch=1,
            grid=(1,),
            in_specs=[whole(dkv.shape), table, table, table, whole(xn4.shape)],
            out_specs=[whole((tokens, KV_HEADS * TILE)), whole(grad.shape), whole(grad.shape)],
        ),
        out_shape=[jax.ShapeDtypeStruct((tokens, KV_HEADS * TILE), BF16), grad, grad],
        compiler_params=params(1),
        cost_estimate=cost(2 * tokens * 960 * 640, 6 * tokens * 960 * 2),
        name="kv_back",
    )(my_part.reshape(1), dkv, *tables, xn4)


def final_kernel(xg_ref, kvb_ref, wkv_ref, hid_ref, part_ref, s1_ref, gain_ref, out_ref, gain_grad_ref):
    parts, rows, width = hid_ref.shape
    scale = s1_ref[...]
    back = dot(kvb_ref[...], side_by_side(wkv_ref))
    scaled_rows = []
    mean = 0.0
    first = pl.program_id(0) == 0
    for d in range(parts):
        grad = xg_ref[d] + back[:, d * width : (d + 1) * width]
        inputs = hid_ref[d].astype(F32)
        gain_grad = jnp.sum(grad * inputs * scale, axis=0, keepdims=True)
        scaled = grad * gain_ref[d]
        scaled_rows.append(scaled)
        mean = mean + jnp.sum(scaled * inputs, axis=-1, keepdims=True)

        @pl.when(first)
        def _(d=d, gain_grad=gain_grad):
            gain_grad_ref[d] = gain_grad

        @pl.when(jnp.logical_not(first))
        def _(d=d, gain_grad=gain_grad):
            gain_grad_ref[d] += gain_grad

    mean = mean / MODEL_DIM * (scale * scale * scale)
    out_ref[...] = whole_rows(
        [part_ref[d] + scale * scaled_rows[d] - hid_ref[d].astype(F32) * mean for d in range(parts)]
    )


def final_step(xg4, kvb, wkv, hid4, part4, s1, gain):
    parts, tokens, width = hid4.shape
    rows = 256
    block = pl.BlockSpec((parts, rows, width), lambda i: (0, i, 0))
    column = pl.BlockSpec((rows, 1), lambda i: (i, 0))
    vector = whole((parts, 1, width))
    return pl.pallas_call(
        final_kernel,
        grid=(tokens // rows,),
        in_specs=[
            block,
            pl.BlockSpec((rows, kvb.shape[1]), lambda i: (i, 0)),
            whole(wkv.shape),
            block,
            block,
            column,
            vector,
        ],
        out_specs=[pl.BlockSpec((rows, MODEL_DIM), lambda i: (i, 0)), vector],
        out_shape=[
            jax.ShapeDtypeStruct((tokens, MODEL_DIM), F32),
            jax.ShapeDtypeStruct((parts, 1, width), F32),
        ],
        compiler_params=params(1),
        cost_estimate=cost(2 * tokens * 960 * 640, 10 * tokens * 960 * 2),
        name="final_step",
    )(xg4, kvb, wkv, hid4, part4, s1, gain)


class Clock:
    def __init__(self):
        self.token = jnp.zeros((8, TILE), F32)

    def at(self, *values):
        out = lax.optimization_barrier(values + (self.token,))
        self.token = out[-1]
        return out[0] if len(values) == 1 else out[:-1]

    def after(self, value):
        return lax.optimization_barrier((value, self.token))[0]


def add(mine, other, dtype=BF16):
    return (mine.astype(F32) + other.astype(F32)).astype(dtype)


class Net:
    def __init__(self, clock, parts, shards):
        self.clock = clock
        self.parts, self.shards = parts, shards
        self.size = parts * shards
        self.index = lax.axis_index("dp") * shards + lax.axis_index("fsdp")
        self.bits = self.size.bit_length() - 1
        self.core = shards.bit_length() - 1
        self.order = list(range(self.core - 1, -1, -1)) + list(range(self.core + 1, self.bits)) + [self.core]

    def swap(self, array, bit):
        flip = 1 << bit
        return lax.ppermute(self.clock.at(array), AXES, [(i, i ^ flip) for i in range(self.size)])

    def on(self, bit):
        return (self.index >> bit) & 1 == 1


class Gather:
    def __init__(self, net, array):
        self.net = net
        self.shape = array.shape
        self.array = array
        self.left = list(net.order)
        self.other = None

    def step(self):
        net = self.net
        if self.other is not None:
            bit = self.left.pop(0)
            other = net.clock.at(self.other)
            here = net.on(bit)
            self.array = jnp.stack([jnp.where(here, other, self.array), jnp.where(here, self.array, other)])
        if self.left:
            self.other = net.swap(self.array, self.left[0])

    def finish(self):
        while self.left:
            self.step()
        net = self.net
        place = {bit: net.bits - 1 - i for i, bit in enumerate(net.order)}
        high_first = [place[bit] for bit in range(net.bits - 1, -1, -1)]
        array = jnp.transpose(self.array, high_first + list(range(net.bits, self.array.ndim)))
        return array.reshape((net.parts, net.shards) + self.shape)


class Scatter:
    def __init__(self, net, keep, send, sections, rows, by_distance=None):
        self.net, self.relative = net, by_distance is not None
        self.left = [net.core] + (by_distance or list(reversed(net.order[:-1])))
        width = keep.shape[-1]
        if self.relative:
            shape = (-1, rows, width)
        else:
            shape = (net.parts // 2, sections, net.shards, rows, width)
        self.keep, self.other = keep.reshape(shape), net.swap(send, self.left.pop(0)).reshape(shape)

    def halves(self, array, bit):
        if self.relative or bit > self.net.core:
            half = array.shape[0] // 2
            return array[:half], array[half:]
        if array.ndim == 5:
            array = array[0]
        pairs = array.reshape((array.shape[0], -1, 2) + array.shape[2:])
        on = (self.net.index >> bit) & 1
        pick = lambda i: lax.dynamic_index_in_dim(pairs, i, 2, keepdims=False)
        return pick(on), pick(1 - on)

    def land(self):
        self.other = self.net.clock.at(self.other)

    def send(self):
        bit = self.left.pop(0)
        keep, send = self.halves(self.keep, bit)
        other_keep, other_send = self.halves(self.other, bit)
        self.keep = add(keep, other_keep)
        self.other = self.net.swap(add(send, other_send), bit)

    def step(self):
        if self.left:
            self.land()
            self.send()

    def result(self):
        while self.left:
            self.step()
        grad = add(self.keep, self.net.clock.at(self.other), F32)
        return grad[0] if self.relative else grad.reshape((grad.shape[-4],) + grad.shape[-2:])


class SumAll:
    def __init__(self, net, array):
        self.net, self.array = net, array
        self.left = list(reversed(net.order))
        self.other = None

    def step(self):
        if self.other is not None:
            self.array = self.array + self.net.clock.at(self.other)
            self.other = None
        if self.left:
            self.other = self.net.swap(self.array, self.left.pop(0))

    def result(self):
        while self.left or self.other is not None:
            self.step()
        return self.array


class EightShards:
    a_moves = [(2 * z, 2 * z + 1) for z in range(4)] + [(7, 6)]
    b_moves = [(2, 3), (3, 2), (4, 5), (5, 4), (6, 7), (7, 6)]
    c_moves = [(4, 5), (5, 4), (6, 7), (7, 6)]

    def __init__(self, clock, parts, shards):
        self.clock, self.parts, self.shards = clock, parts, shards
        self.shard = lax.axis_index("fsdp")
        self.z, self.y = self.shard // 2, self.shard % 2
        self.top, self.odd = self.z == 3, self.y == 1

    def move(self, array, moves):
        pairs = [(d * self.shards + a, d * self.shards + b) for d in range(self.parts) for a, b in moves]
        return lax.ppermute(self.clock.at(array), AXES, pairs)

    def up(self, array, lowest):
        return self.move(array, [(2 * z + y, 2 * z + y + 2) for z in range(lowest, 3) for y in range(2)])

    def down(self, array, lowest):
        return self.move(array, [(2 * z + y + 2, 2 * z + y) for z in range(lowest, 3) for y in range(2)])

    def slot_ids(self):
        shard, z, y = self.shard, self.z, self.y
        none = jnp.int32(-1)
        return jnp.stack(
            [
                shard,
                jnp.where(y == 1, shard - 1, jnp.where(z == 3, 5, none)),
                jnp.where(z == 3, 3 - y, jnp.where(z >= 1, 2 * (z - 1) + 1 - y, none)),
                jnp.where(z >= 2, shard - 4, none),
                jnp.where(z >= 2, 1 - y, none),
                jnp.where(z == 3, y, jnp.where(z >= 1, shard - 2, none)),
            ]
        ).astype(jnp.int32)

    def spread(self, own):
        at = self.clock.at
        up1 = self.up(own, 0)
        yield
        up1 = at(up1)
        up2 = self.up(up1, 1)
        a = self.move(jnp.where(self.top & self.odd, up1, own), self.a_moves)
        yield
        up2, a = at(up2, a)
        up3 = self.up(up2, 2)
        b = self.move(jnp.where(self.top, up2, up1), self.b_moves)
        yield
        up3, b = at(up3, b)
        c = self.move(jnp.where(self.top, up3, up2), self.c_moves)
        yield
        last = jnp.where(self.top, up3, up1)
        c = at(c)
        yield [own, a, b, up2, c, last]

    pairs = 2

    def collect(self, grads):
        at = self.clock.at
        own, a, b, up2, c, last = grads
        back = lambda moves: [(t, s) for s, t in moves]
        wide = lambda array: array.astype(F32)
        from_c, from_b = self.move(c, back(self.c_moves)), self.move(b, back(self.b_moves))
        yield
        from_c = wide(at(from_c))
        first = self.down((wide(last) + from_c).astype(BF16), 2)
        from_a = self.move(a, back(self.a_moves))
        yield
        from_b, first = at(from_b, first)
        from_b, first = wide(from_b), wide(first)
        second = self.down((wide(up2) + jnp.where(self.top, from_b, from_c + first)).astype(BF16), 1)
        yield
        from_a, second = at(from_a, second)
        from_a, second = wide(from_a), wide(second)
        late = self.top & self.odd
        level = jnp.where(self.top, jnp.where(self.odd, from_a, 0.0), wide(last) + from_b + second)
        third = self.down(level.astype(BF16), 0)
        yield
        third = wide(at(third))
        yield (wide(own) + jnp.where(late, 0.0, from_a) + third).astype(BF16)


class AnyShards:
    def __init__(self, clock, parts, shards):
        self.shards = shards
        self.pairs = shards
        self.shard = lax.axis_index("fsdp")

    def slot_ids(self):
        return (self.shard - jnp.arange(self.shards)).astype(jnp.int32)

    def pick(self, array, s):
        return lax.dynamic_index_in_dim(array, (self.shard - s) % self.shards, 0, keepdims=False)

    def spread(self, own):
        every = lax.all_gather(own, "fsdp", axis=0, tiled=False)
        yield from (None,) * 4
        yield [own] + [self.pick(every, s) for s in range(1, self.shards)]

    def collect(self, grads):
        every = jnp.stack(grads)
        order = jnp.stack([self.pick(every, s) for s in range(self.shards)])
        yield from (None,) * 4
        yield lax.psum_scatter(order, "fsdp", scatter_dimension=0, tiled=False)


def shards(
    hidden_in, segment, position, selected, gain_attn, gain_ffn, router,
    w_query, key_weight, value_weight, w_output, w_gate, w_up, w_down, cotangent,
):
    groups, rows, model = hidden_in.shape
    tokens = groups * rows
    parts, shard_count = lax.axis_size("dp"), lax.axis_size("fsdp")
    columns = model // parts
    width = -(-columns // TILE) * TILE
    fill = lambda array: jnp.pad(array, ((0, 0),) * (array.ndim - 1) + ((0, width - columns),))
    clock = Clock()
    at = clock.at
    net = Net(clock, parts, shard_count)
    my_part, my_shard = lax.axis_index("dp"), lax.axis_index("fsdp")
    ring = (EightShards if shard_count == 8 else AnyShards)(clock, parts, shard_count)

    small = fill(jnp.concatenate([key_weight.T, value_weight.T], axis=0))
    medium = fill(jnp.concatenate([w_query.T, w_output], axis=0))
    kv_rows, q_rows = key_weight.shape[1], w_query.shape[1]
    gate_rows, up_rows = w_gate.T, w_up.T
    chunk_rows = w_down.shape[0] // 2
    large = [w[c * chunk_rows : (c + 1) * chunk_rows] for c in range(2) for w in (gate_rows, up_rows, w_down)]
    large = fill(jnp.concatenate(large, axis=0))

    def heads_of(array, count):
        return array.reshape(parts, count, HEAD_DIM, width)

    def split(array):
        return fill(jnp.transpose(array.reshape(tokens, parts, columns), (1, 0, 2)))

    half = HEAD_DIM // 2
    frequency = THETA ** (-(jnp.arange(half).astype(F32) * 2.0) / HEAD_DIM)
    angles = position.reshape(tokens).astype(F32)[:, None] * frequency[None, :]
    cos, sin = jnp.cos(angles), jnp.sin(angles)
    zero, one = jnp.zeros_like(cos), jnp.ones_like(cos)
    table = lambda *four: jnp.concatenate(four, axis=1)
    kv_tables = (table(cos, cos, one, one), table(-sin, zero, zero, zero), table(zero, sin, zero, zero))
    shrink = HEAD_DIM**-0.5
    q_tables = tuple(
        shrink * t
        for t in (table(cos, cos, zero, zero), table(-sin, zero, zero, zero), table(zero, sin, zero, zero))
    )
    seg_rows = segment.astype(F32).reshape(groups, 1, rows)
    tags = jnp.where(selected == 1, segment, -1).astype(BF16).reshape(groups, rows // TILE, TILE)
    tags = jnp.pad(tags, ((0, 0), (0, 16 - rows // TILE), (0, 0)))
    hid4, cot4 = split(hidden_in), split(cotangent)
    vector = lambda v: fill(v.astype(F32).reshape(parts, 1, columns))
    gain_one, gain_two, route = vector(gain_attn), vector(gain_ffn), vector(router)
    chosen = selected.reshape(tokens, 1).astype(F32)

    small_gather = Gather(net, small)
    medium_all = lax.all_gather(medium, AXES, axis=0, tiled=False)
    small_gather.step()
    small_gather.step()
    small_gather.step()
    xn4, s1, fg4, mix, slope = first_norm(hid4, cot4, gain_one, route, chosen)
    xn4 = at(xn4)
    small_gather.step()
    small_all = small_gather.finish()
    keys = heads_of(small_all[:, :, :kv_rows], KV_HEADS)
    values = heads_of(small_all[:, :, kv_rows:], KV_HEADS)
    wkv = jnp.concatenate([keys, values], axis=2).reshape(parts, KV_HEADS * TILE, width)
    spread = ring.spread(kv_project(groups, xn4, wkv, kv_tables, tags))
    next(spread)
    large_all = lax.all_gather(clock.after(large), AXES, axis=0, tiled=False)
    next(spread)
    queries = heads_of(medium_all[:, :q_rows], QUERY_HEADS)
    wq_pad = jnp.concatenate([queries, queries[:, :, half:], queries[:, :, :half]], axis=2)
    wq_pad = wq_pad.reshape(parts, QUERY_HEADS * TILE, width)
    q = at(q_project(xn4, wq_pad, q_tables[0], q_tables[1] + q_tables[2], groups))
    next(spread)
    next(spread)
    slot_ids = ring.slot_ids()
    kvs = next(spread)
    o, lse = at(*attention_forward(slot_ids, q, seg_rows, kvs, ring.pairs))
    outputs = heads_of(medium_all[:, q_rows:], QUERY_HEADS)
    wo_pad = jnp.concatenate([jnp.zeros_like(outputs), outputs], axis=2)
    wo_pad = wo_pad.reshape(parts, QUERY_HEADS * TILE, width)
    mid4, x24, s2 = out_project(o, wo_pad, hid4, gain_two)
    x24 = at(x24)

    ffn_all = large_all.reshape((parts, shard_count // 2, 2) + large.shape)
    bits = net.order[:-1][::-1]
    parts_bits = [bit for bit in bits if bit > net.core]
    shards_bits = [bit for bit in bits if bit < net.core]
    out_a, xg_a, keep_a, send_a = ffn(my_part, my_shard, 0, 3 * chunk_rows, x24, fg4, ffn_all, False)
    scatter_a = Scatter(net, keep_a, send_a, 1, 3 * chunk_rows, parts_bits + shards_bits)
    out_b, xg_b, keep_b, send_b = ffn(my_part, my_shard, 1, 3 * chunk_rows, x24, fg4, ffn_all, True)
    scatter_b = Scatter(net, keep_b, send_b, 1, 3 * chunk_rows, shards_bits[:1] + parts_bits + shards_bits[1:])
    scatter_a.step()
    out_b = at(out_b)
    hidden_out, part4, ag4, router_sum, gain_two_sum = middle_step(
        mid4, hid4, cot4, (out_a, out_b), (xg_a, xg_b), mix, slope, s2, gain_two, route
    )
    ag4 = at(ag4)
    scatter_b.step()
    do = at(out_back(ag4, wo_pad))
    dq, dkvs = attention_backward(slot_ids, q, do, o, lse, seg_rows, q_tables, kvs, ring.pairs)
    dq = at(dq)
    scatter_b.land()
    scatter_a.land()
    collect = ring.collect(dkvs)
    next(collect)
    scatter_b.send()
    keep_qo, send_qo, xg_q = qo_back(my_part, dq, xn4, wq_pad, o, ag4)
    xg_q = at(xg_q)
    next(collect)
    scatter_qo = Scatter(net, keep_qo, send_qo, 2, q_rows)
    next(collect)
    scatter_a.send()
    scatter_qo.step()
    next(collect)
    scatter_b.step()
    scatter_qo.step()
    dkv = next(collect).reshape(tokens, KV_HEADS * TILE)
    kvb, keep_kv, send_kv = kv_back(my_part, dkv, kv_tables, xn4)

    def by_kind(array):
        tiles = array.reshape(array.shape[0], KV_HEADS, 2, HEAD_DIM, width)
        return jnp.transpose(tiles, (0, 2, 1, 3, 4))

    scatter_kv = Scatter(net, by_kind(keep_kv), by_kind(send_kv), 2, kv_rows)
    kvb = at(kvb)
    grad_in, gain_one_sum = final_step(xg_q, kvb, wkv, hid4, part4, s1, gain_one)
    scatter_kv.step()
    scatter_b.step()
    scatter_a.step()
    scatter_qo.step()
    sums = SumAll(net, jnp.stack([gain_one_sum, gain_two_sum, router_sum]))
    sums.step()
    scatter_kv.step()
    sums.step()
    scatter_a.step()
    scatter_qo.step()
    scatter_kv.step()
    sums.step()
    scatter_b.land()
    scatter_kv.step()
    sums.step()
    scatter_a.land()
    scatter_qo.land()
    for _ in range(net.bits):
        scatter_kv.step()
        sums.step()
    kv_grad = scatter_kv.result()
    sums = sums.result()[..., :columns].reshape(3, model)
    kv_grad = kv_grad[..., :columns]
    q_grad, o_grad = scatter_qo.result()[..., :columns]
    grads = [s.result().reshape(3, chunk_rows, width)[..., :columns] for s in (scatter_a, scatter_b)]
    gate_grad, up_grad, down_grad = jnp.concatenate(grads, axis=1)
    sums = sums + clock.token[0, 0]
    return (
        hidden_out.reshape(groups, rows, model),
        grad_in.reshape(groups, rows, model),
        sums[0],
        sums[1],
        sums[2],
        q_grad.T,
        kv_grad[0].T,
        kv_grad[1].T,
        o_grad,
        gate_grad.T,
        up_grad.T,
        down_grad,
    )


def solution(mesh):
    tokens = P("dp", "fsdp")
    inner_first = P("fsdp", "dp")
    return jax.shard_map(
        shards,
        mesh=mesh,
        in_specs=(P("dp", "fsdp", None),) + (tokens,) * 3 + (P(),) * 3
        + (tokens,) * 3 + (inner_first,) + (tokens,) * 2 + (inner_first, P("dp", "fsdp", None)),
        out_specs=(P("dp", "fsdp", None),) * 2 + (P(),) * 3
        + (tokens,) * 3 + (inner_first,) + (tokens,) * 2 + (inner_first,),
        check_vma=False,
    )
```

```python
import functools

import jax
import jax.numpy as jnp
from jax import lax
from jax.experimental import pallas as pl
from jax.experimental.pallas import tpu as pltpu
from jax.sharding import PartitionSpec as P

MODEL_DIM = 960
QUERY_HEADS = 15
KV_HEADS = 5
SHARE = QUERY_HEADS // KV_HEADS
HEAD_DIM = 64
TILE = 128
PROMPT = 1024
LONGEST = 192
EPSILON = 1e-05
THETA = 10000.0
MINUS_LARGE = -1e30
AXES = ("dp", "fsdp")
F32 = jnp.float32
BF16 = jnp.bfloat16
VMEM_BYTES = 60 * 1024 * 1024

NT = (((1,), (1,)), ((), ()))
NN = (((1,), (0,)), ((), ()))
TN = (((0,), (0,)), ((), ()))


def dot(a, b, dims=NN):
    return lax.dot_general(a, b, dims, preferred_element_type=F32)


def params(steps=0):
    return pltpu.CompilerParams(
        vmem_limit_bytes=VMEM_BYTES,
        dimension_semantics=("arbitrary",) * steps if steps else None,
    )


def cost(flops, moved, exps=0):
    return pl.CostEstimate(flops=int(flops), bytes_accessed=int(moved), transcendentals=int(exps))


def whole(shape):
    zeros = (0,) * len(shape)
    return pl.BlockSpec(shape, lambda *_: zeros)


def side_by_side(ref):
    return jnp.concatenate([ref[d] for d in range(ref.shape[0])], axis=1)


def by_distance(ref, my_part):
    parts = ref.shape[0]
    return jnp.concatenate([ref[pl.ds(my_part ^ e, 1)].reshape(ref.shape[1:]) for e in range(parts)], axis=1)


def whole_rows(pieces):
    return jnp.concatenate([piece[:, : MODEL_DIM // len(pieces)] for piece in pieces], axis=1)


def norm_kernel(hid_ref, cot_ref, gain_ref, router_ref, sel_ref, xn_ref, s1_ref, fg_ref, mix_ref, slope_ref):
    parts, _, width = hid_ref.shape
    square = 0.0
    logit = 0.0
    for d in range(parts):
        x = hid_ref[d].astype(F32)
        square = square + jnp.sum(x * x, axis=-1, keepdims=True)
        logit = logit + jnp.sum(x * router_ref[d], axis=-1, keepdims=True)
    scale = lax.rsqrt(square / MODEL_DIM + EPSILON)
    chance = 1.0 / (1.0 + jnp.exp(-logit))
    mix = sel_ref[...] * chance
    s1_ref[...] = scale
    mix_ref[...] = mix
    slope_ref[...] = mix * (1.0 - chance)
    for d in range(parts):
        x = hid_ref[d].astype(F32)
        xn_ref[d] = (x * scale * gain_ref[d]).astype(BF16)
        fg_ref[d] = (cot_ref[d].astype(F32) * mix).astype(BF16)


def first_norm(hid4, cot4, gain, router, chosen):
    parts, tokens, width = hid4.shape
    rows = 128
    block = pl.BlockSpec((parts, rows, width), lambda i: (0, i, 0))
    column = pl.BlockSpec((rows, 1), lambda i: (i, 0))
    vector = whole((parts, 1, width))
    return pl.pallas_call(
        norm_kernel,
        grid=(tokens // rows,),
        in_specs=[block, block, vector, vector, column],
        out_specs=[block, column, block, column, column],
        out_shape=[
            jax.ShapeDtypeStruct(hid4.shape, BF16),
            jax.ShapeDtypeStruct((tokens, 1), F32),
            jax.ShapeDtypeStruct(hid4.shape, BF16),
            jax.ShapeDtypeStruct((tokens, 1), F32),
            jax.ShapeDtypeStruct((tokens, 1), F32),
        ],
        compiler_params=params(1),
        cost_estimate=cost(tokens * 960 * 10, tokens * 960 * 8),
        name="first_norm",
    )(hid4, cot4, gain, router, chosen)


def kv_kernel(xn_ref, w_ref, cos_ref, sin1_ref, sin2_ref, tag_ref, out_ref):
    rows = xn_ref.shape[1]
    total = dot(side_by_side(xn_ref), side_by_side(w_ref), NT)
    for h in range(KV_HEADS):
        u = total[:, h * TILE : (h + 1) * TILE]
        turned = (
            u * cos_ref[...]
            + pltpu.roll(u, TILE - HEAD_DIM // 2, 1) * sin1_ref[...]
            + pltpu.roll(u, HEAD_DIM // 2, 1) * sin2_ref[...]
        )
        out_ref[:rows, h * TILE : (h + 1) * TILE] = turned.astype(BF16)
        out_ref[rows:, h * TILE : (h + 1) * TILE] = tag_ref[0]


def kv_project(groups, xn4, wkv, tables, tags):
    parts, tokens, width = xn4.shape
    rows = tokens // groups
    table = pl.BlockSpec((rows, TILE), lambda g: (g, 0))
    return pl.pallas_call(
        kv_kernel,
        grid=(groups,),
        in_specs=[
            pl.BlockSpec((parts, rows, width), lambda g: (0, g, 0)),
            whole(wkv.shape),
            table,
            table,
            table,
            pl.BlockSpec((1, 16, TILE), lambda g: (g, 0, 0)),
        ],
        out_specs=pl.BlockSpec((None, rows + 16, KV_HEADS * TILE), lambda g: (g, 0, 0)),
        out_shape=jax.ShapeDtypeStruct((groups, rows + 16, KV_HEADS * TILE), BF16),
        compiler_params=params(1),
        cost_estimate=cost(2 * tokens * 960 * 640, 3 * tokens * 960 * 2),
        name="kv_project",
    )(xn4, wkv, *tables, tags)


def q_kernel(xn_ref, w_ref, cos_ref, sin_ref, out_ref):
    total = dot(side_by_side(xn_ref), side_by_side(w_ref), NT)
    for h in range(QUERY_HEADS):
        u = total[:, h * TILE : (h + 1) * TILE]
        turned = u * cos_ref[...] + pltpu.roll(u, HEAD_DIM, 1) * sin_ref[...]
        out_ref[:, h * TILE : (h + 1) * TILE] = turned.astype(BF16)


def q_project(xn4, wq_pad, cos_q, sin_q, groups):
    parts, tokens, width = xn4.shape
    rows = tokens // groups
    table = pl.BlockSpec((rows, TILE), lambda g: (g, 0))
    return pl.pallas_call(
        q_kernel,
        grid=(groups,),
        in_specs=[
            pl.BlockSpec((parts, rows, width), lambda g: (0, g, 0)),
            whole(wq_pad.shape),
            table,
            table,
        ],
        out_specs=pl.BlockSpec((rows, QUERY_HEADS * TILE), lambda g: (g, 0)),
        out_shape=jax.ShapeDtypeStruct((tokens, QUERY_HEADS * TILE), BF16),
        compiler_params=params(1),
        cost_estimate=cost(2 * tokens * 960 * 1920, 6 * tokens * 960 * 2),
        name="q_project",
    )(xn4, wq_pad, cos_q, sin_q)


def slot_needed(slot_ref, s, rows):
    own = slot_ref[0]
    block = slot_ref[s]
    prompt_blocks = PROMPT // rows
    reach = -(-(LONGEST - 1) // rows)
    near = (block < prompt_blocks) | (block >= own - reach)
    return (block >= 0) & (block <= own) & near


def fill_bias(slot_ref, seg_ref, kv_refs, pair_ref, key_ref, turned):
    pairs, rows, _ = pair_ref.shape
    for s, kv_ref in enumerate(kv_refs):
        needed = slot_needed(slot_ref, s, rows)
        for i in range(rows // TILE):
            here = slice(i * TILE, (i + 1) * TILE)
            tag_row = kv_ref[rows : rows + 16, 0:TILE].astype(F32)[i : i + 1]
            tag = jnp.where(needed, jnp.broadcast_to(tag_row, (TILE, TILE)).T, -1.0)
            if s >= pairs:
                lane = lax.broadcasted_iota(jnp.int32, (TILE, TILE), 1)
                hidden = (tag != 0.0) & (lane == HEAD_DIM)
                key_ref[s - pairs, here, :] = jnp.where(hidden, MINUS_LARGE, 0.0).astype(BF16)
                continue
            for j in range(rows // TILE):
                there = slice(j * TILE, (j + 1) * TILE)
                allowed = (tag == 0.0) | (tag == seg_ref[0, :, there])
                if s == 0:
                    key_row = i * TILE + lax.broadcasted_iota(jnp.int32, (TILE, TILE), 0)
                    query_row = j * TILE + lax.broadcasted_iota(jnp.int32, (TILE, TILE), 1)
                    allowed = (allowed & (key_row <= query_row)) | (key_row == query_row)
                bias = jnp.where(allowed, 0.0, MINUS_LARGE)
                if turned:
                    pair_ref[s, there, here] = bias.T
                else:
                    pair_ref[s, here, there] = bias


def lanes_of(dtype, shape, test):
    return jnp.where(test(lax.broadcasted_iota(jnp.int32, shape, 1)), 1.0, 0.0).astype(dtype)


def load_keys(kv_refs, pair_ref, key_ref):
    pairs, rows, _ = pair_ref.shape
    kvs = [ref[:rows, :] for ref in kv_refs]
    other = lanes_of(BF16, (1, TILE), lambda lane: lane != HEAD_DIM)
    marked = [kv * other + (key_ref[s - pairs] if s >= pairs else 0.0) for s, kv in enumerate(kvs)]
    return jnp.concatenate(kvs, axis=0), jnp.concatenate([m.astype(BF16) for m in marked], axis=0)


def mark(q):
    return q + lanes_of(BF16, (1, TILE), lambda lane: lane == HEAD_DIM)


def forward_kernel(slots, slot_ref, q_ref, seg_ref, *refs):
    kv_refs = refs[:slots]
    o_ref, lse_ref, pair_ref, key_ref = refs[slots:]
    rows = q_ref.shape[0]
    pairs = pair_ref.shape[0]

    @pl.when(pl.program_id(1) == 0)
    def _():
        fill_bias(slot_ref, seg_ref, kv_refs, pair_ref, key_ref, True)

    kvs, marked = load_keys(kv_refs, pair_ref, key_ref)
    low = lanes_of(BF16, (1, TILE), lambda lane: lane < HEAD_DIM)
    counted = kvs * (1.0 - low) + low
    lane = lax.broadcasted_iota(jnp.int32, (rows, TILE), 1)
    weights, peaks = [], []
    for j in range(SHARE):
        here = slice(j * TILE, (j + 1) * TILE)
        raw = dot(mark(q_ref[:, here]), marked, NT)
        parts = [raw[:, s * rows : (s + 1) * rows] + pair_ref[s] for s in range(pairs)]
        if slots > pairs:
            parts.append(raw[:, pairs * rows :])
        score = jnp.concatenate(parts, axis=1)
        peak = score[:, :TILE]
        for t in range(1, score.shape[1] // TILE):
            peak = jnp.maximum(peak, score[:, t * TILE : (t + 1) * TILE])
        peak = jnp.max(peak, axis=1, keepdims=True)
        peaks.append(peak)
        weights.append(jnp.exp(score - peak).astype(BF16))
    accs = dot(jnp.concatenate(weights, axis=0), counted)
    for j, peak in enumerate(peaks):
        here = slice(j * TILE, (j + 1) * TILE)
        acc = accs[j * rows : (j + 1) * rows]
        total = jnp.where(lane < HEAD_DIM, acc, 1.0)
        mixed = acc * pltpu.roll(1.0 / total, HEAD_DIM, 1)
        o_ref[:, here] = jnp.where(lane >= HEAD_DIM, mixed, 0.0).astype(BF16)
        lse_ref[0, 0, :, j * rows : (j + 1) * rows] = (peak + jnp.log(total)).T[0:1]


def attention_forward(slot_ids, q, seg, kvs, pairs):
    groups, _, rows = seg.shape
    slots = len(kvs)
    tokens = groups * rows
    wide = SHARE * rows
    heads = pl.BlockSpec((rows, SHARE * TILE), lambda g, h, _: (g, h))
    return pl.pallas_call(
        functools.partial(forward_kernel, slots),
        grid_spec=pltpu.PrefetchScalarGridSpec(
            num_scalar_prefetch=1,
            grid=(groups, KV_HEADS),
            in_specs=[heads, pl.BlockSpec((1, 1, rows), lambda g, h, _: (g, 0, 0))]
            + [pl.BlockSpec((None, rows + 16, TILE), lambda g, h, _: (g, 0, h))] * slots,
            out_specs=[heads, pl.BlockSpec((1, 1, 1, wide), lambda g, h, _: (g, h, 0, 0))],
            scratch_shapes=[
                pltpu.VMEM((pairs, rows, rows), F32),
                pltpu.VMEM((max(slots - pairs, 1), rows, TILE), BF16),
            ],
        ),
        out_shape=[
            jax.ShapeDtypeStruct(q.shape, BF16),
            jax.ShapeDtypeStruct((groups, KV_HEADS, 1, wide), F32),
        ],
        compiler_params=params(2),
        cost_estimate=cost(2 * 15 * tokens * 1536 * 256, 8 * tokens * 960 * 2, 15 * tokens * 1536),
        name="attention_forward",
    )(slot_ids, q, seg, *kvs)


def backward_kernel(slots, slot_ref, q_ref, do_ref, o_ref, lse_ref, seg_ref, cos_ref, sin1_ref, sin2_ref, *refs):
    kv_refs = refs[:slots]
    dq_ref = refs[slots]
    dkv_refs = refs[slots + 1 : -2]
    pair_ref, key_ref = refs[-2:]
    rows = q_ref.shape[0]

    @pl.when(pl.program_id(1) == 0)
    def _():
        fill_bias(slot_ref, seg_ref, kv_refs, pair_ref, key_ref, False)

    kvs, marked = load_keys(kv_refs, pair_ref, key_ref)
    pairs = pair_ref.shape[0]
    left, right = [], []
    for j in range(SHARE):
        here = slice(j * TILE, (j + 1) * TILE)
        q, do = q_ref[:, here], do_ref[:, here]
        delta = jnp.sum((do.astype(F32) * o_ref[:, here].astype(F32)).T, axis=0, keepdims=True)
        raw = dot(marked, mark(q), NT)
        parts = [raw[s * rows : (s + 1) * rows] + pair_ref[s] for s in range(pairs)]
        if slots > pairs:
            parts.append(raw[pairs * rows :])
        prob = jnp.exp(jnp.concatenate(parts, axis=0) - lse_ref[0, 0, :, j * rows : (j + 1) * rows])
        slope = (prob * (dot(kvs, do, NT) - delta)).astype(BF16)
        left += [slope, prob.astype(BF16)]
        right += [q, do]
        part = dot(slope, kvs, TN)
        back = (
            part * cos_ref[...]
            - pltpu.roll(part, TILE - HEAD_DIM // 2, 1) * sin1_ref[...]
            - pltpu.roll(part, HEAD_DIM // 2, 1) * sin2_ref[...]
        )
        dq_ref[:, here] = back.astype(BF16)
    right = jnp.concatenate(right, axis=0)
    for s in range(slots):
        band = jnp.concatenate([part[s * rows : (s + 1) * rows] for part in left], axis=1)
        dkv_refs[s][...] = dot(band, right).astype(BF16)


def attention_backward(slot_ids, q, do, o, lse, seg, tables, kvs, pairs):
    groups, _, rows = seg.shape
    slots = len(kvs)
    heads = pl.BlockSpec((rows, SHARE * TILE), lambda g, h, _: (g, h))
    seg_spec = pl.BlockSpec((1, 1, rows), lambda g, h, _: (g, 0, 0))
    kv_spec = pl.BlockSpec((None, rows + 16, TILE), lambda g, h, _: (g, 0, h))
    lse_spec = pl.BlockSpec((1, 1, 1, SHARE * rows), lambda g, h, _: (g, h, 0, 0))
    table = pl.BlockSpec((rows, TILE), lambda g, h, _: (g, 0))
    grad = pl.BlockSpec((None, rows, TILE), lambda g, h, _: (g, 0, h))
    tokens = groups * rows
    out = pl.pallas_call(
        functools.partial(backward_kernel, slots),
        grid_spec=pltpu.PrefetchScalarGridSpec(
            num_scalar_prefetch=1,
            grid=(groups, KV_HEADS),
            in_specs=[heads, heads, heads, lse_spec, seg_spec, table, table, table] + [kv_spec] * slots,
            out_specs=[heads] + [grad] * slots,
            scratch_shapes=[
                pltpu.VMEM((pairs, rows, rows), F32),
                pltpu.VMEM((max(slots - pairs, 1), rows, TILE), BF16),
            ],
        ),
        out_shape=[jax.ShapeDtypeStruct(q.shape, BF16)]
        + [jax.ShapeDtypeStruct((groups, rows, KV_HEADS * TILE), BF16)] * slots,
        compiler_params=params(2),
        cost_estimate=cost(5 * 15 * tokens * 1536 * 256, 16 * tokens * 960 * 2, 15 * tokens * 1536),
        name="attention_backward",
    )(slot_ids, q, do, o, lse, seg, *tables, *kvs)
    return out[0], out[1:]


def out_kernel(o_ref, w_ref, hid_ref, gain_ref, mid_ref, x2_ref, s2_ref):
    parts, _, width = hid_ref.shape
    out = dot(o_ref[...], side_by_side(w_ref))
    square = 0.0
    for d in range(parts):
        middle = hid_ref[d].astype(F32) + out[:, d * width : (d + 1) * width]
        mid_ref[d] = middle
        square = square + jnp.sum(middle * middle, axis=-1, keepdims=True)
    scale = lax.rsqrt(square / MODEL_DIM + EPSILON)
    s2_ref[...] = scale
    for d in range(parts):
        x2_ref[d] = (mid_ref[d] * scale * gain_ref[d]).astype(BF16)


def out_project(o, wo_pad, hid4, gain):
    parts, tokens, width = hid4.shape
    rows = 256
    block = pl.BlockSpec((parts, rows, width), lambda i: (0, i, 0))
    column = pl.BlockSpec((rows, 1), lambda i: (i, 0))
    return pl.pallas_call(
        out_kernel,
        grid=(tokens // rows,),
        in_specs=[
            pl.BlockSpec((rows, o.shape[1]), lambda i: (i, 0)),
            whole(wo_pad.shape),
            block,
            whole((parts, 1, width)),
        ],
        out_specs=[block, block, column],
        out_shape=[
            jax.ShapeDtypeStruct(hid4.shape, F32),
            jax.ShapeDtypeStruct(hid4.shape, BF16),
            jax.ShapeDtypeStruct((tokens, 1), F32),
        ],
        compiler_params=params(1),
        cost_estimate=cost(2 * tokens * 960 * 1920, 8 * tokens * 960 * 2),
        name="out_project",
    )(o, wo_pad, hid4, gain)


def ffn_kernel(meta_ref, x_ref, fg_ref, w_ref, out_ref, xg_ref, keep_ref, send_ref):
    parts, count, rows3, width = w_ref.shape
    rows = rows3 // 3
    my_part, my_place = meta_ref[0], meta_ref[2]
    bits = count.bit_length() - 1
    turn_bits = [sum((i >> b & 1) << (bits - 1 - b) for b in range(bits)) for i in range(count)]

    def weight(which):
        band = slice(which * rows, (which + 1) * rows)
        block = lambda d, i: w_ref[d, pl.ds(my_place ^ i, 1), band, :].reshape(rows, width)
        lines = [jnp.concatenate([block(d, i) for d in range(parts)], axis=1) for i in turn_bits]
        return jnp.concatenate(lines, axis=0)

    w_gate, w_up, w_down = (weight(which) for which in range(3))
    x, fg = side_by_side(x_ref), side_by_side(fg_ref)
    gate = dot(x, w_gate, NT)
    up = dot(x, w_up, NT)
    hidden_grad = dot(fg, w_down, NT)
    chance = 1.0 / (1.0 + jnp.exp(-gate))
    silu = gate * chance
    hidden = (silu * up).astype(BF16)
    up_grad = (hidden_grad * silu).astype(BF16)
    gate_grad = (hidden_grad * up * chance * (1.0 + gate * (1.0 - chance))).astype(BF16)

    first = pl.program_id(0) == 0
    out = dot(hidden, w_down)
    back = dot(jnp.concatenate([gate_grad, up_grad], axis=1), jnp.concatenate([w_gate, w_up], axis=0))
    for d in range(parts):
        here = slice(d * width, (d + 1) * width)

        @pl.when(first)
        def _(d=d, here=here):
            out_ref[d] = out[:, here]
            xg_ref[d] = back[:, here]

        @pl.when(jnp.logical_not(first))
        def _(d=d, here=here):
            out_ref[d] += out[:, here]
            xg_ref[d] += back[:, here]

    x, fg = by_distance(x_ref, my_part), by_distance(fg_ref, my_part)
    for which, left in enumerate((gate_grad, up_grad, hidden)):
        left, right = left.T, fg if which == 2 else x
        for i in range(count):
            grad = dot(left[i * rows : (i + 1) * rows], right).astype(BF16)
            for e in range(parts):
                target = send_ref if e % 2 else keep_ref
                target[e // 2, i, which * rows : (which + 1) * rows, :] = grad[:, e * width : (e + 1) * width]


def ffn(my_part, my_shard, chunk, rows3, x4, fg4, weights, shard_first):
    parts, tokens, width = x4.shape
    half = weights.shape[1]
    block = pl.BlockSpec((parts, half, None, rows3, width), lambda j, m: (0, 0, m[1] ^ j, chunk, 0))
    if shard_first:
        grad_block = pl.BlockSpec((None, parts // 2, half, rows3, width), lambda j, m: (j, 0, 0, 0, 0))
        grad = jax.ShapeDtypeStruct((2, parts // 2, half, rows3, width), BF16)
    else:
        grad_block = pl.BlockSpec((parts // 2, None, half, rows3, width), lambda j, m: (0, j, 0, 0, 0))
        grad = jax.ShapeDtypeStruct((parts // 2, 2, half, rows3, width), BF16)
    meta = jnp.stack([my_part, my_shard % 2, my_shard // 2]).astype(jnp.int32)
    return pl.pallas_call(
        ffn_kernel,
        grid_spec=pltpu.PrefetchScalarGridSpec(
            num_scalar_prefetch=1,
            grid=(2,),
            in_specs=[whole(x4.shape), whole(x4.shape), block],
            out_specs=[whole(x4.shape), whole(x4.shape), grad_block, grad_block],
        ),
        out_shape=[jax.ShapeDtypeStruct(x4.shape, F32)] * 2 + [grad, grad],
        compiler_params=params(1),
        cost_estimate=cost(12 * tokens * 960 * rows3 * half, 8 * tokens * 960 * 2 + 8 * 960 * rows3 * half),
        name="ffn",
    )(meta, x4, fg4, weights)


def middle_kernel(
    mid_ref, hid_ref, cot_ref, out_a_ref, out_b_ref, xg_a_ref, xg_b_ref, mix_ref, slope_ref, s2_ref, gain_ref, router_ref,
    hidden_ref, part_ref, ag_ref, router_grad_ref, gain_grad_ref,
):
    parts, rows, width = mid_ref.shape
    mix = mix_ref[...]
    scale = s2_ref[...]
    inner = 0.0
    mean = 0.0
    rows_out = []
    for d in range(parts):
        middle = mid_ref[d]
        inputs = hid_ref[d].astype(F32)
        branch = (middle - inputs) + (out_a_ref[d] + out_b_ref[d])
        upstream = cot_ref[d].astype(F32)
        inner = inner + jnp.sum(upstream * branch, axis=-1, keepdims=True)
        rows_out.append(inputs + mix * branch)
        mean = mean + jnp.sum((xg_a_ref[d] + xg_b_ref[d]) * gain_ref[d] * middle, axis=-1, keepdims=True)
    hidden_ref[...] = whole_rows(rows_out).astype(BF16)
    logit_grad = slope_ref[...] * inner
    mean = mean / MODEL_DIM * (scale * scale * scale)
    first = pl.program_id(0) == 0
    for d in range(parts):
        middle = mid_ref[d]
        inputs = hid_ref[d].astype(F32)
        upstream = cot_ref[d].astype(F32)
        grad = xg_a_ref[d] + xg_b_ref[d]
        middle_grad = scale * (grad * gain_ref[d]) - middle * mean
        ag_ref[d] = (upstream * mix + middle_grad).astype(BF16)
        part_ref[d] = upstream + logit_grad * router_ref[d] + middle_grad
        router_grad = jnp.sum(logit_grad * inputs, axis=0, keepdims=True)
        gain_grad = jnp.sum(grad * middle * scale, axis=0, keepdims=True)

        @pl.when(first)
        def _(d=d, router_grad=router_grad, gain_grad=gain_grad):
            router_grad_ref[d] = router_grad
            gain_grad_ref[d] = gain_grad

        @pl.when(jnp.logical_not(first))
        def _(d=d, router_grad=router_grad, gain_grad=gain_grad):
            router_grad_ref[d] += router_grad
            gain_grad_ref[d] += gain_grad


def middle_step(mid4, hid4, cot4, outs, grads, mix, slope, s2, gain, router):
    parts, tokens, width = mid4.shape
    rows = 256
    block = pl.BlockSpec((parts, rows, width), lambda i: (0, i, 0))
    column = pl.BlockSpec((rows, 1), lambda i: (i, 0))
    vector = whole((parts, 1, width))
    return pl.pallas_call(
        middle_kernel,
        grid=(tokens // rows,),
        in_specs=[block] * 7 + [column] * 3 + [vector] * 2,
        out_specs=[pl.BlockSpec((rows, MODEL_DIM), lambda i: (i, 0)), block, block, vector, vector],
        out_shape=[
            jax.ShapeDtypeStruct((tokens, MODEL_DIM), BF16),
            jax.ShapeDtypeStruct(mid4.shape, F32),
            jax.ShapeDtypeStruct(mid4.shape, BF16),
            jax.ShapeDtypeStruct((parts, 1, width), F32),
            jax.ShapeDtypeStruct((parts, 1, width), F32),
        ],
        compiler_params=params(1),
        cost_estimate=cost(tokens * 960 * 30, tokens * 960 * 36),
        name="middle_step",
    )(mid4, hid4, cot4, *outs, *grads, mix, slope, s2, gain, router)


def compact(tile_major, upper):
    count = tile_major.shape[0] // TILE
    start = HEAD_DIM if upper else 0
    return jnp.concatenate(
        [tile_major[h * TILE + start : h * TILE + start + HEAD_DIM] for h in range(count)], axis=0
    )


def out_back_kernel(ag_ref, w_ref, do_ref):
    do_ref[...] = dot(side_by_side(ag_ref), side_by_side(w_ref), NT).astype(BF16)


def out_back(ag4, wo_pad):
    parts, tokens, width = ag4.shape
    rows = 256
    return pl.pallas_call(
        out_back_kernel,
        grid=(tokens // rows,),
        in_specs=[pl.BlockSpec((parts, rows, width), lambda i: (0, i, 0)), whole(wo_pad.shape)],
        out_specs=pl.BlockSpec((rows, wo_pad.shape[1]), lambda i: (i, 0)),
        out_shape=jax.ShapeDtypeStruct((tokens, wo_pad.shape[1]), BF16),
        compiler_params=params(1),
        cost_estimate=cost(2 * tokens * 960 * 1920, 6 * tokens * 960 * 2),
        name="out_back",
    )(ag4, wo_pad)


def part_grads(left, ref, my_part, targets):
    parts, _, width = ref.shape
    right = by_distance(ref, my_part)
    rows = left.shape[0]
    step = rows // 4
    for r in range(0, rows, step):
        grad = dot(left[r : r + step], right).astype(BF16)
        for e in range(parts):
            targets[e % 2][e // 2, r : r + step] = grad[:, e * width : (e + 1) * width]


def qo_back_kernel(meta_ref, dq_ref, xn_ref, w_ref, o_ref, ag_ref, keep_ref, send_ref, xg_ref):
    parts, _, width = xn_ref.shape
    sides = ((compact(dq_ref[...].T, False), xn_ref), (compact(o_ref[...].T, True), ag_ref))
    for i, (left, ref) in enumerate(sides):
        part_grads(left, ref, meta_ref[0], (keep_ref.at[:, i], send_ref.at[:, i]))
    back = dot(dq_ref[...], side_by_side(w_ref))
    for d in range(parts):
        xg_ref[d] = back[:, d * width : (d + 1) * width]


def qo_back(my_part, dq, xn4, wq_pad, o, ag4):
    parts, tokens, width = xn4.shape
    grad = jax.ShapeDtypeStruct((parts // 2, 2, QUERY_HEADS * HEAD_DIM, width), BF16)
    return pl.pallas_call(
        qo_back_kernel,
        grid_spec=pltpu.PrefetchScalarGridSpec(
            num_scalar_prefetch=1,
            grid=(1,),
            in_specs=[whole(a.shape) for a in (dq, xn4, wq_pad, o, ag4)],
            out_specs=[whole(grad.shape), whole(grad.shape), whole(xn4.shape)],
        ),
        out_shape=[grad, grad, jax.ShapeDtypeStruct(xn4.shape, F32)],
        compiler_params=params(1),
        cost_estimate=cost(2 * tokens * 960 * 3840, 14 * tokens * 960 * 2),
        name="qo_back",
    )(my_part.reshape(1), dq, xn4, wq_pad, o, ag4)


def kv_back_kernel(meta_ref, dkv_ref, cos_ref, sin1_ref, sin2_ref, xn_ref, back_ref, keep_ref, send_ref):
    for h in range(KV_HEADS):
        u = dkv_ref[:, h * TILE : (h + 1) * TILE].astype(F32)
        back = (
            u * cos_ref[...]
            - pltpu.roll(u, TILE - HEAD_DIM // 2, 1) * sin1_ref[...]
            - pltpu.roll(u, HEAD_DIM // 2, 1) * sin2_ref[...]
        )
        back_ref[:, h * TILE : (h + 1) * TILE] = back.astype(BF16)
    part_grads(back_ref[...].T, xn_ref, meta_ref[0], (keep_ref, send_ref))


def kv_back(my_part, dkv, tables, xn4):
    parts, tokens, width = xn4.shape
    grad = jax.ShapeDtypeStruct((parts // 2, KV_HEADS * TILE, width), BF16)
    table = whole((tokens, TILE))
    return pl.pallas_call(
        kv_back_kernel,
        grid_spec=pltpu.PrefetchScalarGridSpec(
            num_scalar_prefetch=1,
            grid=(1,),
            in_specs=[whole(dkv.shape), table, table, table, whole(xn4.shape)],
            out_specs=[whole((tokens, KV_HEADS * TILE)), whole(grad.shape), whole(grad.shape)],
        ),
        out_shape=[jax.ShapeDtypeStruct((tokens, KV_HEADS * TILE), BF16), grad, grad],
        compiler_params=params(1),
        cost_estimate=cost(2 * tokens * 960 * 640, 6 * tokens * 960 * 2),
        name="kv_back",
    )(my_part.reshape(1), dkv, *tables, xn4)


def final_kernel(xg_ref, kvb_ref, wkv_ref, hid_ref, part_ref, s1_ref, gain_ref, out_ref, gain_grad_ref):
    parts, rows, width = hid_ref.shape
    scale = s1_ref[...]
    back = dot(kvb_ref[...], side_by_side(wkv_ref))
    scaled_rows = []
    mean = 0.0
    first = pl.program_id(0) == 0
    for d in range(parts):
        grad = xg_ref[d] + back[:, d * width : (d + 1) * width]
        inputs = hid_ref[d].astype(F32)
        gain_grad = jnp.sum(grad * inputs * scale, axis=0, keepdims=True)
        scaled = grad * gain_ref[d]
        scaled_rows.append(scaled)
        mean = mean + jnp.sum(scaled * inputs, axis=-1, keepdims=True)

        @pl.when(first)
        def _(d=d, gain_grad=gain_grad):
            gain_grad_ref[d] = gain_grad

        @pl.when(jnp.logical_not(first))
        def _(d=d, gain_grad=gain_grad):
            gain_grad_ref[d] += gain_grad

    mean = mean / MODEL_DIM * (scale * scale * scale)
    out_ref[...] = whole_rows(
        [part_ref[d] + scale * scaled_rows[d] - hid_ref[d].astype(F32) * mean for d in range(parts)]
    )


def final_step(xg4, kvb, wkv, hid4, part4, s1, gain):
    parts, tokens, width = hid4.shape
    rows = 256
    block = pl.BlockSpec((parts, rows, width), lambda i: (0, i, 0))
    column = pl.BlockSpec((rows, 1), lambda i: (i, 0))
    vector = whole((parts, 1, width))
    return pl.pallas_call(
        final_kernel,
        grid=(tokens // rows,),
        in_specs=[
            block,
            pl.BlockSpec((rows, kvb.shape[1]), lambda i: (i, 0)),
            whole(wkv.shape),
            block,
            block,
            column,
            vector,
        ],
        out_specs=[pl.BlockSpec((rows, MODEL_DIM), lambda i: (i, 0)), vector],
        out_shape=[
            jax.ShapeDtypeStruct((tokens, MODEL_DIM), F32),
            jax.ShapeDtypeStruct((parts, 1, width), F32),
        ],
        compiler_params=params(1),
        cost_estimate=cost(2 * tokens * 960 * 640, 10 * tokens * 960 * 2),
        name="final_step",
    )(xg4, kvb, wkv, hid4, part4, s1, gain)


class Clock:
    def __init__(self):
        self.token = jnp.zeros((8, TILE), F32)

    def at(self, *values):
        out = lax.optimization_barrier(values + (self.token,))
        self.token = out[-1]
        return out[0] if len(values) == 1 else out[:-1]

    def after(self, value):
        return lax.optimization_barrier((value, self.token))[0]


def add(mine, other, dtype=BF16):
    return (mine.astype(F32) + other.astype(F32)).astype(dtype)


class Net:
    def __init__(self, clock, parts, shards):
        self.clock = clock
        self.parts, self.shards = parts, shards
        self.size = parts * shards
        self.index = lax.axis_index("dp") * shards + lax.axis_index("fsdp")
        self.bits = self.size.bit_length() - 1
        self.core = shards.bit_length() - 1
        self.order = list(range(self.core - 1, -1, -1)) + list(range(self.core + 1, self.bits)) + [self.core]

    def swap(self, array, bit):
        flip = 1 << bit
        return lax.ppermute(self.clock.at(array), AXES, [(i, i ^ flip) for i in range(self.size)])

    def on(self, bit):
        return (self.index >> bit) & 1 == 1


class Gather:
    def __init__(self, net, array):
        self.net = net
        self.shape = array.shape
        self.array = array
        self.left = list(net.order)
        self.other = None

    def step(self):
        net = self.net
        if self.other is not None:
            bit = self.left.pop(0)
            other = net.clock.at(self.other)
            here = net.on(bit)
            self.array = jnp.stack([jnp.where(here, other, self.array), jnp.where(here, self.array, other)])
        if self.left:
            self.other = net.swap(self.array, self.left[0])

    def finish(self):
        while self.left:
            self.step()
        net = self.net
        place = {bit: net.bits - 1 - i for i, bit in enumerate(net.order)}
        high_first = [place[bit] for bit in range(net.bits - 1, -1, -1)]
        array = jnp.transpose(self.array, high_first + list(range(net.bits, self.array.ndim)))
        return array.reshape((net.parts, net.shards) + self.shape)


class Scatter:
    def __init__(self, net, keep, send, sections, rows, by_distance=None):
        self.net, self.relative = net, by_distance is not None
        self.left = [net.core] + (by_distance or list(reversed(net.order[:-1])))
        width = keep.shape[-1]
        if self.relative:
            shape = (-1, rows, width)
        else:
            shape = (net.parts // 2, sections, net.shards, rows, width)
        self.keep, self.other = keep.reshape(shape), net.swap(send, self.left.pop(0)).reshape(shape)

    def halves(self, array, bit):
        if self.relative or bit > self.net.core:
            half = array.shape[0] // 2
            return array[:half], array[half:]
        if array.ndim == 5:
            array = array[0]
        pairs = array.reshape((array.shape[0], -1, 2) + array.shape[2:])
        on = (self.net.index >> bit) & 1
        pick = lambda i: lax.dynamic_index_in_dim(pairs, i, 2, keepdims=False)
        return pick(on), pick(1 - on)

    def land(self):
        self.other = self.net.clock.at(self.other)

    def send(self):
        bit = self.left.pop(0)
        keep, send = self.halves(self.keep, bit)
        other_keep, other_send = self.halves(self.other, bit)
        self.keep = add(keep, other_keep)
        self.other = self.net.swap(add(send, other_send), bit)

    def step(self):
        if self.left:
            self.land()
            self.send()

    def result(self):
        while self.left:
            self.step()
        grad = add(self.keep, self.net.clock.at(self.other), F32)
        return grad[0] if self.relative else grad.reshape((grad.shape[-4],) + grad.shape[-2:])


class SumAll:
    def __init__(self, net, array):
        self.net, self.array = net, array
        self.left = list(reversed(net.order))
        self.other = None

    def step(self):
        if self.other is not None:
            self.array = self.array + self.net.clock.at(self.other)
            self.other = None
        if self.left:
            self.other = self.net.swap(self.array, self.left.pop(0))

    def result(self):
        while self.left or self.other is not None:
            self.step()
        return self.array


class EightShards:
    a_moves = [(2 * z, 2 * z + 1) for z in range(4)] + [(7, 6)]
    b_moves = [(2, 3), (3, 2), (4, 5), (5, 4), (6, 7), (7, 6)]
    c_moves = [(4, 5), (5, 4), (6, 7), (7, 6)]

    def __init__(self, clock, parts, shards):
        self.clock, self.parts, self.shards = clock, parts, shards
        self.shard = lax.axis_index("fsdp")
        self.z, self.y = self.shard // 2, self.shard % 2
        self.top, self.odd = self.z == 3, self.y == 1

    def move(self, array, moves):
        pairs = [(d * self.shards + a, d * self.shards + b) for d in range(self.parts) for a, b in moves]
        return lax.ppermute(self.clock.at(array), AXES, pairs)

    def up(self, array, lowest):
        return self.move(array, [(2 * z + y, 2 * z + y + 2) for z in range(lowest, 3) for y in range(2)])

    def down(self, array, lowest):
        return self.move(array, [(2 * z + y + 2, 2 * z + y) for z in range(lowest, 3) for y in range(2)])

    def slot_ids(self):
        shard, z, y = self.shard, self.z, self.y
        none = jnp.int32(-1)
        return jnp.stack(
            [
                shard,
                jnp.where(y == 1, shard - 1, jnp.where(z == 3, 5, none)),
                jnp.where(z == 3, 3 - y, jnp.where(z >= 1, 2 * (z - 1) + 1 - y, none)),
                jnp.where(z >= 2, shard - 4, none),
                jnp.where(z >= 2, 1 - y, none),
                jnp.where(z == 3, y, jnp.where(z >= 1, shard - 2, none)),
            ]
        ).astype(jnp.int32)

    def spread(self, own):
        at = self.clock.at
        up1 = self.up(own, 0)
        yield
        up1 = at(up1)
        up2 = self.up(up1, 1)
        a = self.move(jnp.where(self.top & self.odd, up1, own), self.a_moves)
        yield
        up2, a = at(up2, a)
        up3 = self.up(up2, 2)
        b = self.move(jnp.where(self.top, up2, up1), self.b_moves)
        yield
        up3, b = at(up3, b)
        c = self.move(jnp.where(self.top, up3, up2), self.c_moves)
        yield
        last = jnp.where(self.top, up3, up1)
        c = at(c)
        yield [own, a, b, up2, c, last]

    pairs = 2

    def collect(self, grads):
        at = self.clock.at
        own, a, b, up2, c, last = grads
        back = lambda moves: [(t, s) for s, t in moves]
        wide = lambda array: array.astype(F32)
        from_c, from_b = self.move(c, back(self.c_moves)), self.move(b, back(self.b_moves))
        yield
        from_c = wide(at(from_c))
        first = self.down((wide(last) + from_c).astype(BF16), 2)
        from_a = self.move(a, back(self.a_moves))
        yield
        from_b, first = at(from_b, first)
        from_b, first = wide(from_b), wide(first)
        second = self.down((wide(up2) + jnp.where(self.top, from_b, from_c + first)).astype(BF16), 1)
        yield
        from_a, second = at(from_a, second)
        from_a, second = wide(from_a), wide(second)
        late = self.top & self.odd
        level = jnp.where(self.top, jnp.where(self.odd, from_a, 0.0), wide(last) + from_b + second)
        third = self.down(level.astype(BF16), 0)
        yield
        third = wide(at(third))
        yield (wide(own) + jnp.where(late, 0.0, from_a) + third).astype(BF16)


class AnyShards:
    def __init__(self, clock, parts, shards):
        self.shards = shards
        self.pairs = shards
        self.shard = lax.axis_index("fsdp")

    def slot_ids(self):
        return (self.shard - jnp.arange(self.shards)).astype(jnp.int32)

    def pick(self, array, s):
        return lax.dynamic_index_in_dim(array, (self.shard - s) % self.shards, 0, keepdims=False)

    def spread(self, own):
        every = lax.all_gather(own, "fsdp", axis=0, tiled=False)
        yield from (None,) * 4
        yield [own] + [self.pick(every, s) for s in range(1, self.shards)]

    def collect(self, grads):
        every = jnp.stack(grads)
        order = jnp.stack([self.pick(every, s) for s in range(self.shards)])
        yield from (None,) * 4
        yield lax.psum_scatter(order, "fsdp", scatter_dimension=0, tiled=False)


def shards(
    hidden_in, segment, position, selected, gain_attn, gain_ffn, router,
    w_query, key_weight, value_weight, w_output, w_gate, w_up, w_down, cotangent,
):
    groups, rows, model = hidden_in.shape
    tokens = groups * rows
    parts, shard_count = lax.axis_size("dp"), lax.axis_size("fsdp")
    columns = model // parts
    width = -(-columns // TILE) * TILE
    fill = lambda array: jnp.pad(array, ((0, 0),) * (array.ndim - 1) + ((0, width - columns),))
    clock = Clock()
    at = clock.at
    net = Net(clock, parts, shard_count)
    my_part, my_shard = lax.axis_index("dp"), lax.axis_index("fsdp")
    ring = (EightShards if shard_count == 8 else AnyShards)(clock, parts, shard_count)

    small = fill(jnp.concatenate([key_weight.T, value_weight.T], axis=0))
    medium = fill(jnp.concatenate([w_query.T, w_output], axis=0))
    kv_rows, q_rows = key_weight.shape[1], w_query.shape[1]
    gate_rows, up_rows = w_gate.T, w_up.T
    chunk_rows = w_down.shape[0] // 2
    large = [w[c * chunk_rows : (c + 1) * chunk_rows] for c in range(2) for w in (gate_rows, up_rows, w_down)]
    large = fill(jnp.concatenate(large, axis=0))

    def heads_of(array, count):
        return array.reshape(parts, count, HEAD_DIM, width)

    def split(array):
        return fill(jnp.transpose(array.reshape(tokens, parts, columns), (1, 0, 2)))

    half = HEAD_DIM // 2
    frequency = THETA ** (-(jnp.arange(half).astype(F32) * 2.0) / HEAD_DIM)
    angles = position.reshape(tokens).astype(F32)[:, None] * frequency[None, :]
    cos, sin = jnp.cos(angles), jnp.sin(angles)
    zero, one = jnp.zeros_like(cos), jnp.ones_like(cos)
    table = lambda *four: jnp.concatenate(four, axis=1)
    kv_tables = (table(cos, cos, one, one), table(-sin, zero, zero, zero), table(zero, sin, zero, zero))
    shrink = HEAD_DIM**-0.5
    q_tables = tuple(
        shrink * t
        for t in (table(cos, cos, zero, zero), table(-sin, zero, zero, zero), table(zero, sin, zero, zero))
    )
    seg_rows = segment.astype(F32).reshape(groups, 1, rows)
    tags = jnp.where(selected == 1, segment, -1).astype(BF16).reshape(groups, rows // TILE, TILE)
    tags = jnp.pad(tags, ((0, 0), (0, 16 - rows // TILE), (0, 0)))
    hid4, cot4 = split(hidden_in), split(cotangent)
    vector = lambda v: fill(v.astype(F32).reshape(parts, 1, columns))
    gain_one, gain_two, route = vector(gain_attn), vector(gain_ffn), vector(router)
    chosen = selected.reshape(tokens, 1).astype(F32)

    small_gather = Gather(net, small)
    medium_all = lax.all_gather(medium, AXES, axis=0, tiled=False)
    small_gather.step()
    small_gather.step()
    small_gather.step()
    xn4, s1, fg4, mix, slope = first_norm(hid4, cot4, gain_one, route, chosen)
    xn4 = at(xn4)
    small_gather.step()
    small_all = small_gather.finish()
    keys = heads_of(small_all[:, :, :kv_rows], KV_HEADS)
    values = heads_of(small_all[:, :, kv_rows:], KV_HEADS)
    wkv = jnp.concatenate([keys, values], axis=2).reshape(parts, KV_HEADS * TILE, width)
    spread = ring.spread(kv_project(groups, xn4, wkv, kv_tables, tags))
    next(spread)
    large_all = lax.all_gather(clock.after(large), AXES, axis=0, tiled=False)
    next(spread)
    queries = heads_of(medium_all[:, :q_rows], QUERY_HEADS)
    wq_pad = jnp.concatenate([queries, queries[:, :, half:], queries[:, :, :half]], axis=2)
    wq_pad = wq_pad.reshape(parts, QUERY_HEADS * TILE, width)
    q = at(q_project(xn4, wq_pad, q_tables[0], q_tables[1] + q_tables[2], groups))
    next(spread)
    next(spread)
    slot_ids = ring.slot_ids()
    kvs = next(spread)
    o, lse = at(*attention_forward(slot_ids, q, seg_rows, kvs, ring.pairs))
    outputs = heads_of(medium_all[:, q_rows:], QUERY_HEADS)
    wo_pad = jnp.concatenate([jnp.zeros_like(outputs), outputs], axis=2)
    wo_pad = wo_pad.reshape(parts, QUERY_HEADS * TILE, width)
    mid4, x24, s2 = out_project(o, wo_pad, hid4, gain_two)
    x24 = at(x24)

    ffn_all = large_all.reshape((parts, shard_count // 2, 2) + large.shape)
    bits = net.order[:-1][::-1]
    parts_bits = [bit for bit in bits if bit > net.core]
    shards_bits = [bit for bit in bits if bit < net.core]
    out_a, xg_a, keep_a, send_a = ffn(my_part, my_shard, 0, 3 * chunk_rows, x24, fg4, ffn_all, False)
    scatter_a = Scatter(net, keep_a, send_a, 1, 3 * chunk_rows, parts_bits + shards_bits)
    out_b, xg_b, keep_b, send_b = ffn(my_part, my_shard, 1, 3 * chunk_rows, x24, fg4, ffn_all, True)
    scatter_b = Scatter(net, keep_b, send_b, 1, 3 * chunk_rows, shards_bits[:1] + parts_bits + shards_bits[1:])
    scatter_a.step()
    out_b = at(out_b)
    hidden_out, part4, ag4, router_sum, gain_two_sum = middle_step(
        mid4, hid4, cot4, (out_a, out_b), (xg_a, xg_b), mix, slope, s2, gain_two, route
    )
    ag4 = at(ag4)
    scatter_b.step()
    do = at(out_back(ag4, wo_pad))
    dq, dkvs = attention_backward(slot_ids, q, do, o, lse, seg_rows, q_tables, kvs, ring.pairs)
    dq = at(dq)
    scatter_b.land()
    scatter_a.land()
    collect = ring.collect(dkvs)
    next(collect)
    scatter_b.send()
    keep_qo, send_qo, xg_q = qo_back(my_part, dq, xn4, wq_pad, o, ag4)
    xg_q = at(xg_q)
    next(collect)
    scatter_qo = Scatter(net, keep_qo, send_qo, 2, q_rows)
    next(collect)
    scatter_a.send()
    scatter_qo.step()
    next(collect)
    scatter_b.step()
    scatter_qo.step()
    dkv = next(collect).reshape(tokens, KV_HEADS * TILE)
    kvb, keep_kv, send_kv = kv_back(my_part, dkv, kv_tables, xn4)

    def by_kind(array):
        tiles = array.reshape(array.shape[0], KV_HEADS, 2, HEAD_DIM, width)
        return jnp.transpose(tiles, (0, 2, 1, 3, 4))

    scatter_kv = Scatter(net, by_kind(keep_kv), by_kind(send_kv), 2, kv_rows)
    kvb = at(kvb)
    grad_in, gain_one_sum = final_step(xg_q, kvb, wkv, hid4, part4, s1, gain_one)
    scatter_kv.step()
    scatter_b.step()
    scatter_a.step()
    scatter_qo.step()
    sums = SumAll(net, jnp.stack([gain_one_sum, gain_two_sum, router_sum]))
    sums.step()
    scatter_kv.step()
    sums.step()
    scatter_a.step()
    scatter_qo.step()
    scatter_kv.step()
    sums.step()
    scatter_b.land()
    scatter_kv.step()
    sums.step()
    scatter_a.land()
    scatter_qo.land()
    for _ in range(net.bits):
        scatter_kv.step()
        sums.step()
    kv_grad = scatter_kv.result()
    sums = sums.result()[..., :columns].reshape(3, model)
    kv_grad = kv_grad[..., :columns]
    q_grad, o_grad = scatter_qo.result()[..., :columns]
    grads = [s.result().reshape(3, chunk_rows, width)[..., :columns] for s in (scatter_a, scatter_b)]
    gate_grad, up_grad, down_grad = jnp.concatenate(grads, axis=1)
    sums = sums + clock.token[0, 0]
    return (
        hidden_out.reshape(groups, rows, model),
        grad_in.reshape(groups, rows, model),
        sums[0],
        sums[1],
        sums[2],
        q_grad.T,
        kv_grad[0].T,
        kv_grad[1].T,
        o_grad,
        gate_grad.T,
        up_grad.T,
        down_grad,
    )


def solution(mesh):
    tokens = P("dp", "fsdp")
    inner_first = P("fsdp", "dp")
    return jax.shard_map(
        shards,
        mesh=mesh,
        in_specs=(P("dp", "fsdp", None),) + (tokens,) * 3 + (P(),) * 3
        + (tokens,) * 3 + (inner_first,) + (tokens,) * 2 + (inner_first, P("dp", "fsdp", None)),
        out_specs=(P("dp", "fsdp", None),) * 2 + (P(),) * 3
        + (tokens,) * 3 + (inner_first,) + (tokens,) * 2 + (inner_first,),
        check_vma=False,
    )
```
